256 devices in a mesh: sta: 32 (over x, y, core), tpl: 8 (over z).
Axes of the slice: x: 4, y: 4, z: 8, core: 2. Of those that a mesh axis runs over, the one named last changes fastest.
Arguments:
- waveforms: bfloat16 [512, 3, 5376], P('sta'), may hold values from -6 to 6
- station_home: int32 [512], replicated, may hold values from 0 to 511, as said below
- templates: bfloat16 [2048, 20, 768], P(('sta', 'tpl')), may hold values from -6 to 6
- template_stations: int32 [2048, 20], P(('sta', 'tpl')), may hold values from 0 to 511, as said below
- station_counts: int32 [2048], P(('sta', 'tpl')), may hold values from 4 to 20
- moveouts: int32 [2048, 20], P(('sta', 'tpl')), may hold values from 0 to 4
Outputs:
- stack: float32 [2048, 4608], P(('sta', 'tpl'))
- network: float32 [4608], replicated
The draws below stay inside these ranges and needn't reach their ends.
Inputs may be any that keep to these rules, and one draw needn't show every extreme that they name: `station_home`: a permutation of the rows. `template_stations`: the live slots k < station_counts[t] of a template name distinct stations; later slots are ignored; among the live slots of the 8 templates of one device, at most 6 name stations whose rows station_home puts on one index of sta.
All inputs are finite; a program needn't handle non-finite values.
Results may differ from the reference program's by a relative error of at most 0.0003.
Values may be sent and summed in bfloat16 or wider, within the bound.
No kernel may reach another device: no remote copies, remote signals or barrier semaphores. Data moves between devices by JAX's collectives and lax.ppermute only.
A program may use at most 128 MiB of HBM per device.

```python
import jax
import jax.numpy as jnp
from jax import lax

STA_DEV = 16
TPL_DEV = 8
SLOTS = 20
L = 256
BLOCK = 128
LAG_BLOCKS = 40
MOVE_BLOCKS = 4
STATIONS = 512
TEMPLATES = 2048
SAMPLES = 5376
N_STA = 32


def station_layout(key):
    return jax.random.permutation(key, STA_DEV * N_STA).astype(jnp.int32)


def draw_station_home(key, part):
    return station_layout(key)


def draw_template_stations(key, part):
    home = station_layout(key)
    key = jax.random.fold_in(key, 7)
    key_base, key_local = jax.random.split(key)
    groups = TEMPLATES // TPL_DEV
    pick = jax.random.randint(key_base, (groups,), 0, N_STA)
    base = pick * pick // N_STA
    tpl_index = jnp.arange(TPL_DEV)
    slot_index = jnp.arange(SLOTS)
    position = 10 * tpl_index[:, None] + (slot_index // 2)[None, :]
    owner = (base[:, None, None] + position[None, :, :]) % N_STA
    rank = 2 * (slot_index // 2 // N_STA) + slot_index % 2
    scores = jax.random.randint(key_local, (groups, TPL_DEV, N_STA, STA_DEV), 0, 1 << 20) * STA_DEV + jnp.arange(STA_DEV)
    order = jnp.argsort(scores, axis=-1).astype(jnp.int32)
    chosen = jnp.take_along_axis(order, owner[..., None].astype(jnp.int32), axis=2)
    rank_full = jnp.broadcast_to(rank[None, None, :, None], (groups, TPL_DEV, SLOTS, 1)).astype(jnp.int32)
    local = jnp.take_along_axis(chosen, rank_full, axis=3)[..., 0]
    rows = owner * STA_DEV + local
    station_of_row = jnp.argsort(home)
    return station_of_row[rows].reshape(TEMPLATES, SLOTS).astype(jnp.int32)


def draw_station_counts(key, part):
    key = jax.random.fold_in(key, 13)
    counts = jax.random.randint(key, (TEMPLATES,), 4, SLOTS + 1)
    place = jnp.arange(TEMPLATES) % TPL_DEV
    group = jnp.arange(TEMPLATES) // TPL_DEV
    counts = jnp.where(place < 2, SLOTS, jnp.where(place == 2, 4, counts))
    counts = jnp.where(group == 0, SLOTS, counts)
    return counts.astype(jnp.int32)


def touch_ends(values, key, least, high):
    spot = [jax.random.randint(jax.random.fold_in(key, axis), (), 0, length) for axis, length in enumerate(values.shape)]
    longest = values.shape.index(max(values.shape))
    neighbour = spot[:longest] + [(spot[longest] + 1) % values.shape[longest]] + spot[longest + 1:]
    return values.at[tuple(spot)].set(least).at[tuple(neighbour)].set(high)


def levels(own_key, dims, shards, smallest, high):
    factor_of, own = 1.0, jax.random.fold_in(own_key, 6)
    for dim, shards_of in shards:
        heights = jnp.exp(jax.random.uniform(jax.random.fold_in(own, dim), (shards_of,), jnp.float32, smallest / len(shards), high / len(shards)))
        factor_of = factor_of * jnp.repeat(heights, dims[dim] // shards_of).reshape([-1 if axis == dim else 1 for axis in range(len(dims))])
    return factor_of


def normal_values(rng, shape, spread, limit, cuts=(), held_as=jnp.bfloat16):
    array = jax.random.normal(rng, shape, jnp.float32) * spread
    if len(cuts) > 0:
        array = levels(rng, shape, cuts, -0.22, 0.18) * array
    return jnp.clip(array, min=-limit, max=limit).astype(held_as)


def setup_inputs(seed: int = 0) -> dict:
    arg_keys = jax.random.split(jax.random.key(seed), 7)
    return {
        "waveforms": normal_values(arg_keys[0], (STATIONS, 3, SAMPLES), 1.0, 6.0, ((0, 32),)),
        "station_home": draw_station_home(jax.random.fold_in(arg_keys[6], 71), 0),
        "templates": normal_values(arg_keys[2], (TEMPLATES, SLOTS, 3 * L), 1.0, 6.0, ((0, 256),)),
        "template_stations": draw_template_stations(jax.random.fold_in(arg_keys[6], 71), 0),
        "station_counts": draw_station_counts(jax.random.fold_in(arg_keys[6], 71), 0),
        "moveouts": touch_ends(jax.random.randint(arg_keys[5], (TEMPLATES, SLOTS), 0, MOVE_BLOCKS + 1), jax.random.fold_in(arg_keys[5], 1), 0, MOVE_BLOCKS).astype(jnp.int32),
    }


EPS = 1e-06

def windows(x):
    count = x.shape[0]
    reach = L // BLOCK
    blocks = x.reshape(count, 3, LAG_BLOCKS + reach, BLOCK)
    parts = [blocks[:, :, start:start + LAG_BLOCKS, :] for start in range(reach + 1)]
    joined = jnp.concatenate(parts, axis=-1)
    return jnp.transpose(joined, (0, 2, 1, 3))

def energy(window):
    squares = lax.optimization_barrier(jnp.sum(window.astype(jnp.float32) ** 2, axis=2))
    upper = jnp.arange(BLOCK + L)[:, None]
    lower = jnp.arange(BLOCK)[None, :]
    boxes = ((upper >= lower) & (upper - lower < L)).astype(jnp.float32)
    return jnp.einsum('nbu,uj->nbj', squares, boxes, precision=lax.Precision.HIGHEST) / (3.0 * L)

def toeplitz(pieces):
    count, comps, length = pieces.shape
    padded = jnp.concatenate([pieces, jnp.zeros((count, comps, BLOCK + 1), pieces.dtype)], axis=-1)
    flat = jnp.tile(padded, (1, 1, BLOCK))
    return flat[..., :BLOCK * (length + BLOCK)].reshape(count, comps, BLOCK, length + BLOCK)

def shift(traces, offsets):
    kept = LAG_BLOCKS - MOVE_BLOCKS
    moved = jax.vmap(lambda trace, offset: lax.dynamic_slice_in_dim(trace, offset, kept, 0))(traces, offsets)
    return moved.reshape(traces.shape[0], kept * BLOCK)

def one_template(waveforms, station_home, items):
    template, stations, count, offsets = items
    rows = station_home[stations]
    window = windows(waveforms[rows])
    power = energy(window)
    pieces = template.reshape(SLOTS, 3, L)
    corr = jnp.einsum('pbcu,pcju->pbj', window.astype(jnp.float32), toeplitz(pieces).astype(jnp.float32), precision=lax.Precision.HIGHEST)
    flat = pieces.astype(jnp.float32)
    tmean = lax.optimization_barrier(jnp.mean(flat * flat, axis=(1, 2)))
    scaled = corr / (3.0 * L * jnp.sqrt(power + EPS) * jnp.sqrt(tmean + EPS)[:, None, None])
    moved = shift(scaled, offsets)
    live = (jnp.arange(SLOTS) < count).astype(jnp.float32)
    total = lax.optimization_barrier(jnp.sum(moved * live[:, None], axis=0))
    return total * jnp.sqrt(3.0 * L / count.astype(jnp.float32))

def reference(waveforms, station_home, templates, template_stations, station_counts, moveouts):
    stack = lax.map(lambda items: one_template(waveforms, station_home, items), (templates, template_stations, station_counts, moveouts))
    network = lax.optimization_barrier(jnp.max(stack, axis=0))
    return (stack, network)
```

```python
import functools

import jax
import jax.numpy as jnp
from jax import lax
from jax.experimental import pallas as pl
from jax.experimental.pallas import tpu as pltpu
from jax.sharding import PartitionSpec as P

SLOTS = 20
L = 256
BLOCK = 128
LAG_BLOCKS = 40
MOVE_BLOCKS = 4
EPS = 1e-06

PHASES = 16
COLS = LAG_BLOCKS * BLOCK // PHASES
KEPT = (LAG_BLOCKS - MOVE_BLOCKS) * BLOCK // PHASES
WIDE = 384
REACH = L // PHASES
DEPTH = 3 * L + BLOCK
CHUNK = 8
CAP = 6
ROWS = 8
BLOCKS = 14

HIGHEST = lax.Precision.HIGHEST
NT = (((1,), (1,)), ((), ()))


def iota(shape, dim):
    return lax.broadcasted_iota(jnp.int32, shape, dim)


def dot(a, b, dims=None):
    if dims is None:
        dims = (((1,), (0,)), ((), ()))
    return lax.dot_general(a, b, dims, preferred_element_type=jnp.float32)


def pack_kernel(slots_ref, home_ref, templates_ref, send_ref, dest_ref):
    total = templates_ref.shape[0]
    width = send_ref.shape[0]
    sta_dev = home_ref.shape[1] // width
    stations = slots_ref[0:1, :]
    moves = slots_ref[1:2, :]
    counts = slots_ref[2:3, :]
    n_sta = home_ref.shape[1]
    home = home_ref[...]
    high = home // sta_dev
    low = home - high * sta_dev
    rows = iota((8, n_sta), 0)
    table = jnp.where(rows == 0, high, jnp.where(rows == 1, low, 0)).astype(jnp.bfloat16)
    hit = (iota((n_sta, total), 0) == stations).astype(jnp.bfloat16)
    found = dot(table, hit)
    owner = found[0:1, :].astype(jnp.int32)
    local = found[1:2, :]
    live = iota((1, total), 1) // 8 < counts
    at_owner = jnp.where((iota((width, total), 0) == owner) & live, 1.0, 0.0)
    before = (iota((total, total), 0) < iota((total, total), 1)).astype(jnp.bfloat16)
    rank = jnp.sum(at_owner * dot(at_owner.astype(jnp.bfloat16), before), axis=0, keepdims=True)
    dest = jnp.where(live, owner * ROWS + rank.astype(jnp.int32), -1)
    dest_ref[...] = dest
    pick = (iota((width * ROWS, total), 0) == dest).astype(jnp.bfloat16)
    send = dot(pick, templates_ref[...]).astype(jnp.bfloat16)
    kind = iota((BLOCK, total), 0)
    fields = jnp.where(
        kind == 0, local, jnp.where(kind == 1, moves.astype(jnp.float32), jnp.where(kind == 2, 1.0, 0.0))
    ).astype(jnp.bfloat16)
    tail = dot(pick, fields, NT).astype(jnp.bfloat16)
    send_ref[:, :, : 3 * L] = send.reshape(width, ROWS, 3 * L)
    send_ref[:, :, 3 * L :] = tail.reshape(width, ROWS, BLOCK)


def prep_kernel(wave_ref, xs_ref, inv_ref, wide_ref):
    stations = wave_ref.shape[1]
    tiles = wave_ref.shape[2] // BLOCK
    wide_ref[...] = wave_ref[...].astype(jnp.float32)
    lane = iota((8, BLOCK), 1)
    own = (lane // PHASES == iota((8, BLOCK), 0)).astype(jnp.float32)
    spread = (
        (iota((3 * PHASES, 3 * BLOCK), 1) // BLOCK == iota((3 * PHASES, 3 * BLOCK), 0) // PHASES)
        & (iota((3 * PHASES, 3 * BLOCK), 1) % PHASES == iota((3 * PHASES, 3 * BLOCK), 0) % PHASES)
    ).astype(jnp.bfloat16)
    sub = iota((PHASES, WIDE), 0)

    @pl.loop(0, stations)
    def _(s):
        comps = []
        for c in range(3):
            parts = []
            group = wide_ref[c, pl.ds(pl.multiple_of(s // 8 * 8, 8), 8), :]
            line = pltpu.roll(group, (8 - s % 8) % 8, 0)[0:1, :]
            for r in range(tiles):
                row = line[:, r * BLOCK : (r + 1) * BLOCK]
                parts.append(jnp.broadcast_to(row, (8, BLOCK)) * own)
            parts.append(jnp.zeros((WIDE - 8 * tiles, BLOCK), jnp.float32))
            comps.append(jnp.concatenate(parts, axis=0).astype(jnp.bfloat16))
        grid = jnp.concatenate(comps, axis=1)
        phases = dot(spread, grid, NT)
        squares = jnp.zeros((PHASES, WIDE), jnp.float32)
        for c in range(3):
            x = phases[c * PHASES : (c + 1) * PHASES]
            squares = squares + x * x
            for r in range(REACH + 1):
                moved = x if r == 0 else pltpu.roll(x, WIDE - r, 1)
                at = c * L + r * PHASES if r < REACH else 3 * L + c * PHASES
                xs_ref[s, at : at + PHASES, :] = moved.astype(jnp.bfloat16)
        xs_ref[s, 3 * L + 3 * PHASES :, :] = jnp.zeros((DEPTH - 3 * L - 3 * PHASES, WIDE), jnp.bfloat16)
        up = squares
        down = jnp.where(sub >= 1, pltpu.roll(squares, 1, 0), 0.0)
        for step in (1, 2, 4, 8):
            up = up + jnp.where(sub < PHASES - step, pltpu.roll(up, PHASES - step, 0), 0.0)
            down = down + jnp.where(sub >= step, pltpu.roll(down, step, 0), 0.0)
        whole = jnp.broadcast_to(up[0:1, :], (PHASES, WIDE))
        two = whole + pltpu.roll(whole, WIDE - 1, 1)
        four = two + pltpu.roll(two, WIDE - 2, 1)
        eight = four + pltpu.roll(four, WIDE - 4, 1)
        fifteen = (
            pltpu.roll(eight, WIDE - 1, 1)
            + pltpu.roll(four, WIDE - 9, 1)
            + pltpu.roll(two, WIDE - 13, 1)
            + pltpu.roll(whole, WIDE - 15, 1)
        )
        power = (up + fifteen + pltpu.roll(down, WIDE - REACH, 1)) / (3.0 * L)
        inv_ref[s] = 1.0 / (3.0 * L * jnp.sqrt(power + EPS))


def correlate_kernel(got_ref, xs_ref, inv_ref, out_ref, sorted_ref, order_ref, held_ref, tails_ref, table_ref, sem):
    width = got_ref.shape[0]
    stations = xs_ref.shape[0]
    total = width * ROWS
    room = sorted_ref.shape[0]
    got = got_ref[...].reshape(total, DEPTH)
    pieces = got[:, : 3 * L]
    eye = (iota((8, BLOCK), 0) == iota((8, BLOCK), 1)).astype(jnp.bfloat16)
    fields = dot(eye, got[:, 3 * L :], NT)
    live = fields[2:3, :] > 0.5
    at_station = jnp.where(
        (iota((stations, total), 0) == fields[0:1, :].astype(jnp.int32)) & live, 1.0, 0.0
    )
    before = (iota((total, total), 0) < iota((total, total), 1)).astype(jnp.bfloat16)
    rank = dot(at_station.astype(jnp.bfloat16), before)
    chunks = jnp.floor((jnp.sum(at_station, axis=1, keepdims=True) + (CHUNK - 1)) / CHUNK)
    earlier = (iota((stations, stations), 1) < iota((stations, stations), 0)).astype(jnp.bfloat16)
    start = dot(earlier, jnp.broadcast_to(chunks, (stations, BLOCK)).astype(jnp.bfloat16))[:, 0:1]
    place = jnp.sum(at_station * (start * CHUNK + rank), axis=0, keepdims=True).astype(jnp.int32)
    place = jnp.where(live, place, -1)
    pick = (iota((room, total), 0) == place).astype(jnp.bfloat16)
    sorted_ref[...] = dot(pick, pieces)
    kind = iota((8, total), 0)
    rows = jnp.where(
        kind == 3,
        iota((8, total), 1).astype(jnp.float32),
        jnp.where(kind < 3, fields, 0.0),
    ).astype(jnp.bfloat16)
    table = dot(rows, pick, NT)
    table = jnp.where(iota((8, room), 0) == 4, jnp.sum(chunks), table)
    order_ref[...] = table.astype(jnp.int32)
    copy = pltpu.make_async_copy(order_ref, table_ref, sem)
    copy.start()
    copy.wait()

    u = iota((PHASES, L), 1)
    j = iota((PHASES, L), 0)
    late = u >= j
    early = (u < j)[:, :BLOCK]
    lane = iota((PHASES, BLOCK), 1)
    column = iota((PHASES, WIDE), 1)

    @pl.loop(0, table_ref[4, 0])
    def _(i):
        first = pl.multiple_of(i * CHUNK, CHUNK)
        s = table_ref[0, first]
        slot = sorted_ref[pl.ds(first, CHUNK), :]
        mean = jnp.sum(slot * slot, axis=1, keepdims=True) / (3.0 * L)
        unit = 1.0 / jnp.sqrt(mean + EPS)
        bands = []
        for k in range(CHUNK):
            tail = jnp.zeros((PHASES, BLOCK), jnp.float32)
            band = []
            for c in range(3):
                row = jnp.broadcast_to(slot[k : k + 1, c * L : (c + 1) * L], (PHASES, L))
                turned = pltpu.roll(row, 0, 1, stride=1, stride_axis=0)
                band.append(jnp.where(late, turned, 0.0).astype(jnp.bfloat16))
                rest = jnp.where(early, turned[:, :BLOCK], 0.0)
                tail = tail + (rest if c == 0 else pltpu.roll(rest, c * PHASES, 1))
            band.append(tail.astype(jnp.bfloat16))
            bands.append(jnp.concatenate(band, axis=1))
        corr = dot(jnp.concatenate(bands, axis=0), xs_ref[s])
        inv = inv_ref[s]
        for k in range(CHUNK):
            held_ref[k] = corr[k * PHASES : (k + 1) * PHASES] * inv * unit[k : k + 1, :]
        for k in range(CHUNK):

            @pl.when(table_ref[2, first + k] > 0)
            def _(k=k):
                move = table_ref[1, first + k]
                target = table_ref[3, first + k]
                o = target // ROWS
                rk = target % ROWS
                y = pltpu.roll(held_ref[k], (WIDE - move * (BLOCK // PHASES)) % WIDE, 1)
                y = jnp.where(column < KEPT, y, 0.0)
                top = jnp.max(jnp.abs(y), axis=1, keepdims=True)
                power = jnp.zeros_like(top)
                for step in (64, 32, 16, 8, 4, 2, 1):
                    small = top < 2.0**-step
                    top = jnp.where(small, top * 2.0**step, top)
                    power = power + jnp.where(small, float(step), 0.0)
                scale = jnp.full_like(top, 32767.0)
                for step in (64, 32, 16, 8, 4, 2, 1):
                    on = jnp.floor(power / step) - 2.0 * jnp.floor(power / (2 * step)) > 0.5
                    scale = jnp.where(on, scale * 2.0**step, scale)
                q = jnp.clip(jnp.round(y * scale), -32767.0, 32767.0).astype(jnp.int32)
                out_ref[o, 2 * rk] = q[:, :BLOCK].astype(jnp.int16)
                out_ref[o, 2 * rk + 1] = q[:, BLOCK : 2 * BLOCK].astype(jnp.int16)
                left = 32 * (rk % 4)
                end = pltpu.roll(q[:, 2 * BLOCK :], left, 1)
                b = rk // 4
                tails_ref[o, b] = jnp.where((lane >= left) & (lane < left + 32), end, tails_ref[o, b])
                tails_ref[o, 1] = jnp.where(lane == 64 + rk, power.astype(jnp.int32), tails_ref[o, 1])

    @pl.loop(0, width)
    def _(o):
        out_ref[o, 12] = tails_ref[o, 0].astype(jnp.int16)
        out_ref[o, 13] = tails_ref[o, 1].astype(jnp.int16)


def add_kernel(dest_ref, count_ref, back_ref, stack_ref, best_ref):
    lane = iota((PHASES, BLOCK), 1)

    def one_template(t, best):
        count = count_ref[t]

        def one_slot(k, total):
            dest = dest_ref[0, k * 8 + t]
            o = dest // ROWS
            rk = dest % ROWS
            power = pltpu.roll(
                back_ref[o, 13].astype(jnp.int32).astype(jnp.float32), (64 - rk) % BLOCK, 1
            )[:, 0:1]
            scale = jnp.full_like(power, 1.0 / 32767.0)
            for step in (64, 32, 16, 8, 4, 2, 1):
                on = jnp.floor(power / step) - 2.0 * jnp.floor(power / (2 * step)) > 0.5
                scale = jnp.where(on, scale * 2.0**-step, scale)
            tail = back_ref[o, 12 + rk // 4].astype(jnp.int32)
            tail = pltpu.roll(tail, (BLOCK - 32 * (rk % 4)) % BLOCK, 1)
            parts = (
                back_ref[o, 2 * rk].astype(jnp.int32),
                back_ref[o, 2 * rk + 1].astype(jnp.int32),
                tail,
            )
            return tuple(a + p.astype(jnp.float32) * scale for a, p in zip(total, parts))

        zero = jnp.zeros((PHASES, BLOCK), jnp.float32)
        total = lax.fori_loop(0, count, one_slot, (zero, zero, zero))
        factor = jnp.sqrt(3.0 * L / jnp.full((1, 1), count, jnp.int32).astype(jnp.float32))
        whole = jnp.concatenate(total, axis=1) * factor
        stack_ref[t] = whole[:, :KEPT]
        return jnp.maximum(best, whole)

    start = jnp.full((PHASES, WIDE), -jnp.inf, jnp.float32)
    best = lax.fori_loop(0, stack_ref.shape[0], one_template, start)
    best_ref[...] = best[:, :KEPT]


VMEM = pl.BlockSpec(memory_space=pltpu.VMEM)
SMEM = pl.BlockSpec(memory_space=pltpu.SMEM)


def params(mib):
    return pltpu.CompilerParams(vmem_limit_bytes=mib * 2**20)


def body(waveforms, station_home, templates, template_stations, station_counts, moveouts):
    stations, _, samples = waveforms.shape
    tpl_dev = templates.shape[0]
    width = lax.axis_size("sta")
    total = tpl_dev * SLOTS
    slots = jnp.stack(
        [template_stations.T.reshape(total), moveouts.T.reshape(total), jnp.tile(station_counts, SLOTS)]
    )
    send, dest = pl.pallas_call(
        pack_kernel,
        out_shape=(
            jax.ShapeDtypeStruct((width, ROWS, DEPTH), jnp.bfloat16),
            jax.ShapeDtypeStruct((1, total), jnp.int32),
        ),
        in_specs=[VMEM] * 3,
        out_specs=(VMEM, VMEM),
        compiler_params=params(32),
    )(slots, station_home.reshape(1, -1), templates.transpose(1, 0, 2).reshape(total, 3 * L))
    got = lax.all_to_all(send, "sta", split_axis=0, concat_axis=0, tiled=True)
    xs, inv = pl.pallas_call(
        prep_kernel,
        out_shape=(
            jax.ShapeDtypeStruct((stations, DEPTH, WIDE), jnp.bfloat16),
            jax.ShapeDtypeStruct((stations, PHASES, WIDE), jnp.float32),
        ),
        in_specs=[VMEM],
        out_specs=(VMEM, VMEM),
        scratch_shapes=[pltpu.VMEM((3, stations, samples), jnp.float32)],
        compiler_params=params(32),
        cost_estimate=pl.CostEstimate(flops=2 * 10**9, bytes_accessed=12 * 2**20, transcendentals=0),
    )(waveforms.transpose(1, 0, 2))
    room = 8 * (width * CAP // CHUNK + stations)
    traces = pl.pallas_call(
        correlate_kernel,
        out_shape=jax.ShapeDtypeStruct((width, BLOCKS, PHASES, BLOCK), jnp.int16),
        in_specs=[VMEM] * 3,
        out_specs=VMEM,
        scratch_shapes=[
            pltpu.VMEM((room, 3 * L), jnp.float32),
            pltpu.VMEM((8, room), jnp.int32),
            pltpu.VMEM((CHUNK, PHASES, WIDE), jnp.float32),
            pltpu.VMEM((width, 2, PHASES, BLOCK), jnp.int32),
            pltpu.SMEM((8, room), jnp.int32),
            pltpu.SemaphoreType.DMA,
        ],
        compiler_params=params(40),
    )(got, xs, inv)
    back = lax.all_to_all(traces, "sta", split_axis=0, concat_axis=0, tiled=True)
    stack, best = pl.pallas_call(
        add_kernel,
        out_shape=(
            jax.ShapeDtypeStruct((tpl_dev, PHASES, KEPT), jnp.float32),
            jax.ShapeDtypeStruct((PHASES, KEPT), jnp.float32),
        ),
        in_specs=[SMEM, SMEM, VMEM],
        out_specs=(VMEM, VMEM),
        compiler_params=params(32),
    )(dest, station_counts, back)
    stack = stack.transpose(0, 2, 1).reshape(tpl_dev, PHASES * KEPT)
    best = best.T.reshape(PHASES * KEPT)
    network = best_of_all(best.reshape(-1, BLOCK)).reshape(PHASES * KEPT)
    return (stack, network)


def best_of_all(best):
    for axis in ("tpl", "sta"):
        size = lax.axis_size(axis)
        step = 1
        while step < size:
            other = lax.ppermute(best, axis, [(i, i ^ step) for i in range(size)])
            best = jnp.maximum(best, other)
            step *= 2
    return best


def solution(mesh):
    in_specs = (
        P("sta", None, None),
        P(),
        P(("sta", "tpl"), None, None),
        P(("sta", "tpl"), None),
        P(("sta", "tpl")),
        P(("sta", "tpl"), None),
    )
    out_specs = (P(("sta", "tpl"), None), P())
    return jax.shard_map(body, mesh=mesh, in_specs=in_specs, out_specs=out_specs, check_vma=False)
```

```python
import functools

import jax
import jax.numpy as jnp
from jax import lax
from jax.experimental import pallas as pl
from jax.experimental.pallas import tpu as pltpu
from jax.sharding import PartitionSpec as P

SLOTS = 20
L = 256
BLOCK = 128
LAG_BLOCKS = 40
MOVE_BLOCKS = 4
EPS = 1e-06

PHASES = 16
COLS = LAG_BLOCKS * BLOCK // PHASES
KEPT = (LAG_BLOCKS - MOVE_BLOCKS) * BLOCK // PHASES
WIDE = 384
REACH = L // PHASES
DEPTH = 3 * L + BLOCK
CHUNK = 8
CAP = 6
ROWS = 8
BLOCKS = 14

FINE = 8.0
FULL = 32700.0
NT = (((1,), (1,)), ((), ()))


def iota(shape, dim):
    return lax.broadcasted_iota(jnp.int32, shape, dim)


def dot(a, b, dims=None):
    if dims is None:
        dims = (((1,), (0,)), ((), ()))
    return lax.dot_general(a, b, dims, preferred_element_type=jnp.float32)


def pack_kernel(
    stations_hbm, moves_hbm, counts_hbm, home_hbm, templates_hbm, send_ref, dest_ref,
    stations_ref, moves_ref, counts_ref, home_ref, templates_ref, sems,
):
    copies = [
        pltpu.make_async_copy(src, dst, sems.at[i])
        for i, (src, dst) in enumerate(
            (
                (stations_hbm, stations_ref),
                (moves_hbm, moves_ref),
                (counts_hbm, counts_ref),
                (home_hbm, home_ref),
                (templates_hbm, templates_ref),
            )
        )
    ]
    for copy in copies:
        copy.start()
    tpl_dev, slots = stations_ref.shape
    total = tpl_dev * slots
    width = send_ref.shape[0]
    parts = home_ref.shape[0]
    sta_dev = parts * BLOCK // width
    place = iota((1, total), 1)
    of_template = place % tpl_dev
    for copy in copies[:4]:
        copy.wait()
    stations = stations_ref[...]
    high = stations // 16
    fields = jnp.concatenate([high, stations - 16 * high, moves_ref[...]], axis=0)
    expand = (iota((slots, total), 1) // tpl_dev == iota((slots, total), 0)).astype(jnp.bfloat16)
    spread = dot(fields.astype(jnp.float32).astype(jnp.bfloat16), expand)
    mine = iota((tpl_dev, total), 0) == of_template
    rows = [
        jnp.sum(jnp.where(mine, spread[i * tpl_dev : (i + 1) * tpl_dev], 0.0), axis=0, keepdims=True)
        for i in range(3)
    ]
    station = (rows[0] * 16.0 + rows[1]).astype(jnp.int32)
    moves = rows[2]
    counts = jnp.zeros((1, total), jnp.int32)
    for t in range(tpl_dev):
        counts = jnp.where(of_template == t, counts_ref[t], counts)
    home = home_ref[...]
    owners = home // sta_dev
    table = jnp.concatenate([owners, home - owners * sta_dev], axis=0)
    hit = (iota((BLOCK, total), 0) == station % BLOCK).astype(jnp.bfloat16)
    found = dot(table.astype(jnp.float32).astype(jnp.bfloat16), hit)
    part = iota((parts, total), 0) == station // BLOCK
    owner = jnp.sum(jnp.where(part, found[:parts], 0.0), axis=0, keepdims=True).astype(jnp.int32)
    local = jnp.sum(jnp.where(part, found[parts:], 0.0), axis=0, keepdims=True)
    live = place // tpl_dev < counts
    at_owner = jnp.where((iota((width, total), 0) == owner) & live, 1.0, 0.0)
    before = (iota((total, total), 0) < iota((total, total), 1)).astype(jnp.bfloat16)
    rank = jnp.sum(at_owner * dot(at_owner.astype(jnp.bfloat16), before), axis=0, keepdims=True)
    dest = jnp.where(live, owner * ROWS + rank.astype(jnp.int32), -1)
    dest_ref[...] = dest
    pick = (iota((width * ROWS, total), 0) == dest).astype(jnp.bfloat16)
    kind = iota((BLOCK, total), 0)
    fields = jnp.where(
        kind == 0, local, jnp.where(kind == 1, moves, jnp.where(kind == 2, 1.0, 0.0))
    ).astype(jnp.bfloat16)
    tail = dot(pick, fields, NT).astype(jnp.bfloat16)
    copies[4].wait()
    send = dot(pick, templates_ref[...].reshape(total, 3 * L)).astype(jnp.bfloat16)
    send_ref[:, :, : 3 * L] = send.reshape(width, ROWS, 3 * L)
    send_ref[:, :, 3 * L :] = tail.reshape(width, ROWS, BLOCK)


def prep_kernel(wave_ref, xs_ref, inv_ref, wide_ref):
    tiles = wave_ref.shape[2] // BLOCK

    @pl.when(pl.program_id(0) == 0)
    def _():
        wide_ref[...] = wave_ref[...].astype(jnp.float32)

    lane = iota((8, BLOCK), 1)
    own = (lane // PHASES == iota((8, BLOCK), 0)).astype(jnp.float32)
    spread = (
        (iota((3 * PHASES, 3 * BLOCK), 1) // BLOCK == iota((3 * PHASES, 3 * BLOCK), 0) // PHASES)
        & (iota((3 * PHASES, 3 * BLOCK), 1) % PHASES == iota((3 * PHASES, 3 * BLOCK), 0) % PHASES)
    ).astype(jnp.bfloat16)
    sub = iota((PHASES, WIDE), 0)
    s = pl.program_id(0)

    def one_station():
        comps = []
        for c in range(3):
            parts = []
            group = wide_ref[c, pl.ds(pl.multiple_of(s // 8 * 8, 8), 8), :]
            line = pltpu.roll(group, (8 - s % 8) % 8, 0)[0:1, :]
            for r in range(tiles):
                row = line[:, r * BLOCK : (r + 1) * BLOCK]
                parts.append(jnp.broadcast_to(row, (8, BLOCK)) * own)
            parts.append(jnp.zeros((WIDE - 8 * tiles, BLOCK), jnp.float32))
            comps.append(jnp.concatenate(parts, axis=0).astype(jnp.bfloat16))
        grid = jnp.concatenate(comps, axis=1)
        phases = dot(spread, grid, NT)
        squares = jnp.zeros((PHASES, WIDE), jnp.float32)
        for c in range(3):
            x = phases[c * PHASES : (c + 1) * PHASES]
            squares = squares + x * x
            for r in range(REACH + 1):
                moved = x if r == 0 else pltpu.roll(x, WIDE - r, 1)
                at = c * L + r * PHASES if r < REACH else 3 * L + c * PHASES
                xs_ref[0, at : at + PHASES, :] = moved.astype(jnp.bfloat16)
        xs_ref[0, 3 * L + 3 * PHASES :, :] = jnp.zeros((DEPTH - 3 * L - 3 * PHASES, WIDE), jnp.bfloat16)
        up = squares
        down = jnp.where(sub >= 1, pltpu.roll(squares, 1, 0), 0.0)
        for step in (1, 2, 4, 8):
            up = up + jnp.where(sub < PHASES - step, pltpu.roll(up, PHASES - step, 0), 0.0)
            down = down + jnp.where(sub >= step, pltpu.roll(down, step, 0), 0.0)
        whole = jnp.broadcast_to(up[0:1, :], (PHASES, WIDE))
        two = whole + pltpu.roll(whole, WIDE - 1, 1)
        four = two + pltpu.roll(two, WIDE - 2, 1)
        eight = four + pltpu.roll(four, WIDE - 4, 1)
        fifteen = (
            pltpu.roll(eight, WIDE - 1, 1)
            + pltpu.roll(four, WIDE - 9, 1)
            + pltpu.roll(two, WIDE - 13, 1)
            + pltpu.roll(whole, WIDE - 15, 1)
        )
        power = (up + fifteen + pltpu.roll(down, WIDE - REACH, 1)) / (3.0 * L)
        inv_ref[0] = 1.0 / (3.0 * L * jnp.sqrt(power + EPS))

    one_station()


def correlate_kernel(
    got_ref, xs_hbm, inv_ref, out_ref, xs_ref, sorted_ref, order_ref, held_ref, table_ref, sem, xs_sems
):
    width = got_ref.shape[0]
    stations = xs_ref.shape[0]
    total = width * ROWS
    room = sorted_ref.shape[0]
    loads = [pltpu.make_async_copy(xs_hbm.at[s], xs_ref.at[s], xs_sems.at[s]) for s in range(stations)]
    for load in loads:
        load.start()
    got = got_ref[...].reshape(total, DEPTH)
    pieces = got[:, : 3 * L]
    eye = (iota((8, BLOCK), 0) == iota((8, BLOCK), 1)).astype(jnp.bfloat16)
    fields = dot(eye, got[:, 3 * L :], NT)
    live = fields[2:3, :] > 0.5
    at_station = jnp.where(
        (iota((stations, total), 0) == fields[0:1, :].astype(jnp.int32)) & live, 1.0, 0.0
    )
    before = (iota((total, total), 0) < iota((total, total), 1)).astype(jnp.bfloat16)
    rank = dot(at_station.astype(jnp.bfloat16), before)
    chunks = jnp.floor((jnp.sum(at_station, axis=1, keepdims=True) + (CHUNK - 1)) / CHUNK)
    earlier = (iota((stations, stations), 1) < iota((stations, stations), 0)).astype(jnp.bfloat16)
    start = dot(earlier, jnp.broadcast_to(chunks, (stations, BLOCK)).astype(jnp.bfloat16))[:, 0:1]
    place = jnp.sum(at_station * (start * CHUNK + rank), axis=0, keepdims=True).astype(jnp.int32)
    place = jnp.where(live, place, -1)
    pick = (iota((room, total), 0) == place).astype(jnp.bfloat16)
    kind = iota((8, total), 0)
    rows = jnp.where(
        kind == 3, iota((8, total), 1).astype(jnp.float32), jnp.where(kind < 3, fields, 0.0)
    ).astype(jnp.bfloat16)
    table = dot(rows, pick, NT)
    kind = iota((8, room), 0)
    table = jnp.where((kind == 3) & (table[2:3, :] < 0.5), float(total), table)
    table = jnp.where(kind == 4, jnp.sum(chunks), table)
    order_ref[...] = table.astype(jnp.int32)
    copy = pltpu.make_async_copy(order_ref, table_ref, sem)
    copy.start()
    sorted_ref[...] = dot(pick, pieces)
    copy.wait()
    for load in loads:
        load.wait()

    sub = iota((PHASES, BLOCK), 0)
    lane = iota((PHASES, BLOCK), 1)
    late = lane >= sub

    def toeplitz(slot):
        bands = []
        for k in range(CHUNK):
            tail = jnp.zeros((PHASES, BLOCK), jnp.float32)
            band = []
            for c in range(3):
                turned = []
                for h in range(2):
                    at = c * L + h * BLOCK
                    row = jnp.broadcast_to(slot[k : k + 1, at : at + BLOCK], (PHASES, BLOCK))
                    turned.append(pltpu.roll(row, 0, 1, stride=1, stride_axis=0))
                band.append(jnp.where(late, turned[0], 0.0).astype(jnp.bfloat16))
                band.append(jnp.where(late, turned[1], turned[0]).astype(jnp.bfloat16))
                rest = jnp.where(late, 0.0, turned[1])
                tail = tail + (rest if c == 0 else pltpu.roll(rest, c * PHASES, 1))
            band.append(tail.astype(jnp.bfloat16))
            bands.append(jnp.concatenate(band, axis=1))
        return jnp.concatenate(bands, axis=0)

    def chunk(i):
        first = pl.multiple_of(i * CHUNK, CHUNK)
        s = table_ref[0, first]
        slot = sorted_ref[pl.ds(first, CHUNK), :]
        mean = jnp.sum(slot * slot, axis=1, keepdims=True) / (3.0 * L)
        unit = 1.0 / jnp.sqrt(mean + EPS)
        corr = dot(toeplitz(slot), xs_ref[s])
        inv = inv_ref[s]
        for k in range(CHUNK):
            y = corr[k * PHASES : (k + 1) * PHASES] * (inv * unit[k : k + 1, :])
            move = table_ref[1, first + k] * (BLOCK // PHASES)
            turned = [
                pltpu.roll(y[:, b * BLOCK : (b + 1) * BLOCK], (BLOCK - move) % BLOCK, 1) for b in range(3)
            ]
            stay = lane < BLOCK - move
            target = table_ref[3, first + k]
            held_ref[target, :, :BLOCK] = jnp.where(stay, turned[0], turned[1])
            held_ref[target, :, BLOCK : 2 * BLOCK] = jnp.where(stay, turned[1], turned[2])
            held_ref[target, :, 2 * BLOCK :] = turned[2]

    @pl.loop(0, (table_ref[4, 0] + 1) // 2)
    def _(i):
        chunk(2 * i)
        chunk(2 * i + 1)

    end = KEPT - 2 * BLOCK

    @pl.loop(0, width)
    def _(o):
        tails, powers = [], []
        for r in range(CAP):
            y = held_ref[o * ROWS + r]
            a, b = y[:, :BLOCK], y[:, BLOCK : 2 * BLOCK]
            c = jnp.where(lane < end, y[:, 2 * BLOCK :], 0.0)
            top = jnp.maximum(jnp.maximum(jnp.abs(a), jnp.abs(b)), jnp.abs(c))
            top = jnp.maximum(jnp.max(top, axis=1, keepdims=True), 2.0**-110)
            power = jnp.ceil(FINE * jnp.log2(jnp.broadcast_to(top, (PHASES, BLOCK))))
            scale = FULL * jnp.exp2(power * (-1.0 / FINE))
            out_ref[o, 2 * r] = jnp.round(a * scale).astype(jnp.int32).astype(jnp.int16)
            out_ref[o, 2 * r + 1] = jnp.round(b * scale).astype(jnp.int32).astype(jnp.int16)
            c = jnp.round(c * scale)
            tails.append(c if r % 4 == 0 else pltpu.roll(c, end * (r % 4), 1))
            powers.append(power)
        first = jnp.where(
            lane < end, tails[0], jnp.where(lane < 2 * end, tails[1], jnp.where(lane < 3 * end, tails[2], tails[3]))
        )
        second = jnp.where(lane < end, tails[4], jnp.where(lane < 2 * end, tails[5], 0.0))
        for r in range(CAP):
            second = jnp.where(lane == 2 * end + r, powers[r], second)
        out_ref[o, 12] = first.astype(jnp.int32).astype(jnp.int16)
        out_ref[o, 13] = second.astype(jnp.int32).astype(jnp.int16)


def add_kernel(dest_ref, count_ref, back_ref, stack_ref, best_ref, scale_ref, tail_ref):
    width = back_ref.shape[0]
    end = KEPT - 2 * BLOCK

    def wide(x):
        return x.astype(jnp.int32).astype(jnp.float32)

    @pl.loop(0, width)
    def _(o):
        first, second = wide(back_ref[o, 12]), wide(back_ref[o, 13])
        scales = jnp.exp2(second * (1.0 / FINE)) * (1.0 / FULL)
        for r in range(CAP):
            scale = jnp.broadcast_to(scales[:, 2 * end + r : 2 * end + r + 1], (PHASES, BLOCK))
            tail = first if r < 4 else second
            tail = tail if r % 4 == 0 else pltpu.roll(tail, BLOCK - end * (r % 4), 1)
            scale_ref[o * ROWS + r] = scale
            tail_ref[o * ROWS + r] = tail

    def one_template(t, best):
        count = count_ref[t]

        def four_slots(g, total):
            for i in range(4):
                k = 4 * g + i
                dest = jnp.maximum(dest_ref[0, k * 8 + t], 0)
                o = dest // ROWS
                r = dest % ROWS
                scale = jnp.where(k < count, scale_ref[dest], 0.0)
                parts = (wide(back_ref[o, 2 * r]), wide(back_ref[o, 2 * r + 1]), tail_ref[dest])
                total = tuple(a + p * scale for a, p in zip(total, parts))
            return total

        zero = jnp.zeros((PHASES, BLOCK), jnp.float32)
        total = lax.fori_loop(0, (count + 3) // 4, four_slots, (zero, zero, zero))
        factor = jnp.sqrt(3.0 * L / jnp.full((1, 1), count, jnp.int32).astype(jnp.float32))
        whole = jnp.concatenate(total, axis=1) * factor
        stack_ref[t] = whole[:, :KEPT]
        return jnp.maximum(best, whole)

    start = jnp.full((PHASES, WIDE), -jnp.inf, jnp.float32)
    best = lax.fori_loop(0, stack_ref.shape[0], one_template, start)
    best_ref[...] = best[:, :KEPT]


VMEM = pl.BlockSpec(memory_space=pltpu.VMEM)
ANY = pl.BlockSpec(memory_space=pl.ANY)
SMEM = pl.BlockSpec(memory_space=pltpu.SMEM)


def params(mib):
    return pltpu.CompilerParams(vmem_limit_bytes=mib * 2**20)


def body(waveforms, station_home, templates, template_stations, station_counts, moveouts):
    stations, _, samples = waveforms.shape
    tpl_dev = templates.shape[0]
    width = lax.axis_size("sta")
    total = tpl_dev * SLOTS
    parts = station_home.shape[0] // BLOCK
    send, dest = pl.pallas_call(
        pack_kernel,
        out_shape=(
            jax.ShapeDtypeStruct((width, ROWS, DEPTH), jnp.bfloat16),
            jax.ShapeDtypeStruct((1, total), jnp.int32),
        ),
        in_specs=[ANY] * 5,
        out_specs=(VMEM, VMEM),
        scratch_shapes=[
            pltpu.VMEM((tpl_dev, SLOTS), jnp.int32),
            pltpu.VMEM((tpl_dev, SLOTS), jnp.int32),
            pltpu.SMEM((tpl_dev,), jnp.int32),
            pltpu.VMEM((parts, BLOCK), jnp.int32),
            pltpu.VMEM((SLOTS, tpl_dev, 3 * L), jnp.bfloat16),
            pltpu.SemaphoreType.DMA((5,)),
        ],
        compiler_params=params(60),
    )(
        template_stations,
        moveouts,
        station_counts,
        station_home.reshape(parts, BLOCK),
        templates.transpose(1, 0, 2),
    )
    got = lax.all_to_all(send, "sta", split_axis=0, concat_axis=0, tiled=True)
    xs, inv = pl.pallas_call(
        prep_kernel,
        grid=(stations,),
        out_shape=(
            jax.ShapeDtypeStruct((stations, DEPTH, WIDE), jnp.bfloat16),
            jax.ShapeDtypeStruct((stations, PHASES, WIDE), jnp.float32),
        ),
        in_specs=[pl.BlockSpec((3, stations, samples), lambda s: (0, 0, 0))],
        out_specs=(
            pl.BlockSpec((1, DEPTH, WIDE), lambda s: (s, 0, 0)),
            pl.BlockSpec((1, PHASES, WIDE), lambda s: (s, 0, 0)),
        ),
        scratch_shapes=[pltpu.VMEM((3, stations, samples), jnp.float32)],
        compiler_params=params(50),
        cost_estimate=pl.CostEstimate(flops=2 * 10**9, bytes_accessed=12 * 2**20, transcendentals=0),
    )(waveforms.transpose(1, 0, 2))
    room = 8 * (width * CAP // CHUNK + stations)
    traces = pl.pallas_call(
        correlate_kernel,
        out_shape=jax.ShapeDtypeStruct((width, BLOCKS, PHASES, BLOCK), jnp.int16),
        in_specs=[VMEM, ANY, VMEM],
        out_specs=VMEM,
        scratch_shapes=[
            pltpu.VMEM((stations, DEPTH, WIDE), jnp.bfloat16),
            pltpu.VMEM((room, 3 * L), jnp.float32),
            pltpu.VMEM((8, room), jnp.int32),
            pltpu.VMEM((width * ROWS + 1, PHASES, WIDE), jnp.float32),
            pltpu.SMEM((8, room), jnp.int32),
            pltpu.SemaphoreType.DMA,
            pltpu.SemaphoreType.DMA((stations,)),
        ],
        compiler_params=params(54),
    )(got, xs, inv)
    back = lax.all_to_all(traces, "sta", split_axis=0, concat_axis=0, tiled=True)
    stack, best = pl.pallas_call(
        add_kernel,
        out_shape=(
            jax.ShapeDtypeStruct((tpl_dev, PHASES, KEPT), jnp.float32),
            jax.ShapeDtypeStruct((PHASES, KEPT), jnp.float32),
        ),
        in_specs=[SMEM, SMEM, VMEM],
        out_specs=(VMEM, VMEM),
        scratch_shapes=[
            pltpu.VMEM((width * ROWS, PHASES, BLOCK), jnp.float32),
            pltpu.VMEM((width * ROWS, PHASES, BLOCK), jnp.float32),
        ],
        compiler_params=params(32),
    )(dest, station_counts, back)
    stack = stack.transpose(0, 2, 1).reshape(tpl_dev, PHASES * KEPT)
    best = best.T.reshape(PHASES * KEPT)
    network = best_of_all(best.reshape(-1, BLOCK)).reshape(PHASES * KEPT)
    return (stack, network)


def best_of_all(best):
    for axis in ("tpl", "sta"):
        size = lax.axis_size(axis)
        step = 1
        while step < size:
            other = lax.ppermute(best, axis, [(i, i ^ step) for i in range(size)])
            best = jnp.maximum(best, other)
            step *= 2
    return best


def solution(mesh):
    in_specs = (
        P("sta", None, None),
        P(),
        P(("sta", "tpl"), None, None),
        P(("sta", "tpl"), None),
        P(("sta", "tpl")),
        P(("sta", "tpl"), None),
    )
    out_specs = (P(("sta", "tpl"), None), P())
    return jax.shard_map(body, mesh=mesh, in_specs=in_specs, out_specs=out_specs, check_vma=False)
```

```python
import functools

import jax
import jax.numpy as jnp
from jax import lax
from jax.experimental import pallas as pl
from jax.experimental.pallas import tpu as pltpu
from jax.sharding import PartitionSpec as P

SLOTS = 20
L = 256
BLOCK = 128
LAG_BLOCKS = 40
MOVE_BLOCKS = 4
EPS = 1e-06

PHASES = 16
COLS = LAG_BLOCKS * BLOCK // PHASES
KEPT = (LAG_BLOCKS - MOVE_BLOCKS) * BLOCK // PHASES
WIDE = 384
REACH = L // PHASES
DEPTH = 3 * L + BLOCK
CHUNK = 8
CAP = 6
ROWS = 8
HALF = 3
BLOCKS = 7

FINE = 8.0
FULL = 32700.0
NT = (((1,), (1,)), ((), ()))


def iota(shape, dim):
    return lax.broadcasted_iota(jnp.int32, shape, dim)


def dot(a, b, dims=None):
    if dims is None:
        dims = (((1,), (0,)), ((), ()))
    return lax.dot_general(a, b, dims, preferred_element_type=jnp.float32)


def pack_kernel(
    stations_hbm, moves_hbm, counts_hbm, home_hbm, templates_hbm, send_ref, list_ref,
    stations_ref, moves_ref, counts_ref, home_ref, templates_ref, sems,
):
    copies = [
        pltpu.make_async_copy(src, dst, sems.at[i])
        for i, (src, dst) in enumerate(
            (
                (stations_hbm, stations_ref),
                (moves_hbm, moves_ref),
                (counts_hbm, counts_ref),
                (home_hbm, home_ref),
                (templates_hbm, templates_ref),
            )
        )
    ]
    for copy in copies:
        copy.start()
    tpl_dev, slots = stations_ref.shape
    total = tpl_dev * slots
    width = send_ref.shape[0]
    parts = home_ref.shape[0]
    sta_dev = parts * BLOCK // width
    place = iota((1, total), 1)
    of_template = place % tpl_dev
    for copy in copies[:4]:
        copy.wait()
    stations = stations_ref[...]
    high = stations // 16
    fields = jnp.concatenate([high, stations - 16 * high, moves_ref[...]], axis=0)
    expand = (iota((slots, total), 1) // tpl_dev == iota((slots, total), 0)).astype(jnp.bfloat16)
    spread = dot(fields.astype(jnp.float32).astype(jnp.bfloat16), expand)
    mine = iota((tpl_dev, total), 0) == of_template
    rows = [
        jnp.sum(jnp.where(mine, spread[i * tpl_dev : (i + 1) * tpl_dev], 0.0), axis=0, keepdims=True)
        for i in range(3)
    ]
    station = (rows[0] * 16.0 + rows[1]).astype(jnp.int32)
    moves = rows[2]
    counts = jnp.zeros((1, total), jnp.int32)
    for t in range(tpl_dev):
        counts = jnp.where(of_template == t, counts_ref[t], counts)
    home = home_ref[...]
    owners = home // sta_dev
    table = jnp.concatenate([owners, home - owners * sta_dev], axis=0)
    hit = (iota((BLOCK, total), 0) == station % BLOCK).astype(jnp.bfloat16)
    found = dot(table.astype(jnp.float32).astype(jnp.bfloat16), hit)
    part = iota((parts, total), 0) == station // BLOCK
    owner = jnp.sum(jnp.where(part, found[:parts], 0.0), axis=0, keepdims=True).astype(jnp.int32)
    local = jnp.sum(jnp.where(part, found[parts:], 0.0), axis=0, keepdims=True)
    live = place // tpl_dev < counts
    before = (iota((total, total), 0) < iota((total, total), 1)).astype(jnp.bfloat16)
    pairs = width * tpl_dev
    of_pair = jnp.where((iota((pairs, total), 0) == owner * tpl_dev + of_template) & live, 1.0, 0.0)
    earlier = jnp.sum(of_pair * dot(of_pair.astype(jnp.bfloat16), before), axis=0, keepdims=True)
    first = live & (earlier < 0.5)
    present = jnp.minimum(jnp.sum(of_pair, axis=1, keepdims=True), 1.0)
    row, col = iota((pairs, pairs), 0), iota((pairs, pairs), 1)
    lower = ((row // tpl_dev == col // tpl_dev) & (col < row)).astype(jnp.bfloat16)
    order = dot(lower, jnp.broadcast_to(present, (pairs, BLOCK)).astype(jnp.bfloat16))[:, 0:1]
    turn = jnp.sum(of_pair * order, axis=0, keepdims=True)
    over = jnp.max(jnp.where(live & (turn > HALF - 0.5), 1.0, 0.0))
    late = turn > HALF - 0.5
    home_of = (jnp.where(late, width, 0) + owner) * 4 + jnp.where(late, turn - HALF, turn).astype(jnp.int32)
    own_first = jnp.where((iota((tpl_dev, total), 0) == of_template) & first, 1.0, 0.0)
    nth = dot(own_first.astype(jnp.bfloat16), before)
    nth = jnp.sum(own_first * nth, axis=0, keepdims=True).astype(jnp.int32)
    entry = (iota((BLOCK, total), 0) == nth).astype(jnp.bfloat16)
    listed = dot((own_first * home_of.astype(jnp.float32)).astype(jnp.bfloat16), entry, NT)
    number = jnp.sum(own_first, axis=1, keepdims=True)
    list_ref[...] = jnp.where(iota((tpl_dev, BLOCK), 1) == BLOCK - 1, number, listed).astype(jnp.int32)
    at_owner = jnp.where((iota((width, total), 0) == owner) & live, 1.0, 0.0)
    rank = jnp.sum(at_owner * dot(at_owner.astype(jnp.bfloat16), before), axis=0, keepdims=True)
    dest = jnp.where(live, owner * ROWS + rank.astype(jnp.int32), -1)
    pick = (iota((width * ROWS, total), 0) == dest).astype(jnp.bfloat16)
    kind = iota((BLOCK, total), 0)
    fields = jnp.where(kind == 0, local, jnp.where(kind == 1, moves, jnp.where(kind == 2, 1.0, 0.0)))
    fields = jnp.where(kind == 3, turn, fields).astype(jnp.bfloat16)
    tail = dot(pick, fields, NT)
    tail = jnp.where(iota(tail.shape, 1) == 4, over, tail).astype(jnp.bfloat16)
    copies[4].wait()
    send = dot(pick, templates_ref[...].reshape(total, 3 * L)).astype(jnp.bfloat16)
    send_ref[:, :, : 3 * L] = send.reshape(width, ROWS, 3 * L)
    send_ref[:, :, 3 * L :] = tail.reshape(width, ROWS, BLOCK)


def prep_kernel(wave_ref, xs_ref, inv_ref, wide_ref):
    tiles = wave_ref.shape[2] // BLOCK

    @pl.when(pl.program_id(0) == 0)
    def _():
        wide_ref[...] = wave_ref[...].astype(jnp.float32)

    lane = iota((8, BLOCK), 1)
    own = (lane // PHASES == iota((8, BLOCK), 0)).astype(jnp.float32)
    spread = (
        (iota((3 * PHASES, 3 * BLOCK), 1) // BLOCK == iota((3 * PHASES, 3 * BLOCK), 0) // PHASES)
        & (iota((3 * PHASES, 3 * BLOCK), 1) % PHASES == iota((3 * PHASES, 3 * BLOCK), 0) % PHASES)
    ).astype(jnp.bfloat16)
    sub = iota((PHASES, WIDE), 0)
    s = pl.program_id(0)

    def one_station():
        comps = []
        for c in range(3):
            parts = []
            group = wide_ref[c, pl.ds(pl.multiple_of(s // 8 * 8, 8), 8), :]
            line = pltpu.roll(group, (8 - s % 8) % 8, 0)[0:1, :]
            for r in range(tiles):
                row = line[:, r * BLOCK : (r + 1) * BLOCK]
                parts.append(jnp.broadcast_to(row, (8, BLOCK)) * own)
            parts.append(jnp.zeros((WIDE - 8 * tiles, BLOCK), jnp.float32))
            comps.append(jnp.concatenate(parts, axis=0).astype(jnp.bfloat16))
        grid = jnp.concatenate(comps, axis=1)
        phases = dot(spread, grid, NT)
        squares = jnp.zeros((PHASES, WIDE), jnp.float32)
        for c in range(3):
            x = phases[c * PHASES : (c + 1) * PHASES]
            squares = squares + x * x
            for r in range(REACH + 1):
                moved = x if r == 0 else pltpu.roll(x, WIDE - r, 1)
                at = c * L + r * PHASES if r < REACH else 3 * L + c * PHASES
                xs_ref[0, at : at + PHASES, :] = moved.astype(jnp.bfloat16)
        xs_ref[0, 3 * L + 3 * PHASES :, :] = jnp.zeros((DEPTH - 3 * L - 3 * PHASES, WIDE), jnp.bfloat16)
        up = squares
        down = jnp.where(sub >= 1, pltpu.roll(squares, 1, 0), 0.0)
        for step in (1, 2, 4, 8):
            up = up + jnp.where(sub < PHASES - step, pltpu.roll(up, PHASES - step, 0), 0.0)
            down = down + jnp.where(sub >= step, pltpu.roll(down, step, 0), 0.0)
        whole = jnp.broadcast_to(up[0:1, :], (PHASES, WIDE))
        two = whole + pltpu.roll(whole, WIDE - 1, 1)
        four = two + pltpu.roll(two, WIDE - 2, 1)
        eight = four + pltpu.roll(four, WIDE - 4, 1)
        fifteen = (
            pltpu.roll(eight, WIDE - 1, 1)
            + pltpu.roll(four, WIDE - 9, 1)
            + pltpu.roll(two, WIDE - 13, 1)
            + pltpu.roll(whole, WIDE - 15, 1)
        )
        power = (up + fifteen + pltpu.roll(down, WIDE - REACH, 1)) / (3.0 * L)
        inv_ref[0] = 1.0 / (3.0 * L * jnp.sqrt(power + EPS))

    one_station()


def correlate_kernel(
    got_ref, xs_hbm, inv_ref, out_ref, more_ref, flag_ref, xs_ref, sorted_ref, order_ref, held_ref, table_ref, sem, xs_sems
):
    width = got_ref.shape[0]
    stations = xs_ref.shape[0]
    total = width * ROWS
    room = sorted_ref.shape[0]
    loads = [pltpu.make_async_copy(xs_hbm.at[s], xs_ref.at[s], xs_sems.at[s]) for s in range(stations)]
    for load in loads:
        load.start()
    got = got_ref[...].reshape(total, DEPTH)
    pieces = got[:, : 3 * L]
    eye = (iota((8, BLOCK), 0) == iota((8, BLOCK), 1)).astype(jnp.bfloat16)
    fields = dot(eye, got[:, 3 * L :], NT)
    live = fields[2:3, :] > 0.5
    at_station = jnp.where(
        (iota((stations, total), 0) == fields[0:1, :].astype(jnp.int32)) & live, 1.0, 0.0
    )
    before = (iota((total, total), 0) < iota((total, total), 1)).astype(jnp.bfloat16)
    rank = dot(at_station.astype(jnp.bfloat16), before)
    chunks = jnp.floor((jnp.sum(at_station, axis=1, keepdims=True) + (CHUNK - 1)) / CHUNK)
    earlier = (iota((stations, stations), 1) < iota((stations, stations), 0)).astype(jnp.bfloat16)
    start = dot(earlier, jnp.broadcast_to(chunks, (stations, BLOCK)).astype(jnp.bfloat16))[:, 0:1]
    place = jnp.sum(at_station * (start * CHUNK + rank), axis=0, keepdims=True).astype(jnp.int32)
    place = jnp.where(live, place, -1)
    pick = (iota((room, total), 0) == place).astype(jnp.bfloat16)
    kind = iota((8, total), 0)
    late = fields[3:4, :] > HALF - 0.5
    source = iota((1, total), 1) // ROWS
    turn = jnp.where(late, fields[3:4, :] - HALF, fields[3:4, :]).astype(jnp.int32)
    target = ((jnp.where(late, width, 0) + source) * 4 + turn).astype(jnp.float32)
    rows = jnp.where(kind == 3, target, jnp.where(kind < 3, fields, 0.0)).astype(jnp.bfloat16)
    table = dot(rows, pick, NT)
    over = jnp.max(fields[4:5, :])
    kind = iota((8, room), 0)
    table = jnp.where((kind == 3) & (table[2:3, :] < 0.5), float(held_ref.shape[0] - 1), table)
    table = jnp.where(kind == 4, jnp.sum(chunks), jnp.where(kind == 5, over, table))
    order_ref[...] = table.astype(jnp.int32)
    copy = pltpu.make_async_copy(order_ref, table_ref, sem)
    copy.start()
    flag_ref[...] = jnp.full(flag_ref.shape, over, jnp.float32).astype(jnp.int32)
    sorted_ref[...] = dot(pick, pieces)
    blank = jnp.zeros((PHASES, WIDE), jnp.float32)

    @pl.loop(0, held_ref.shape[0] // 8)
    def _(i):
        for r in range(8):
            held_ref[8 * i + r] = blank

    copy.wait()

    def arrive(s, carry):
        pltpu.make_async_copy(xs_hbm.at[s], xs_ref.at[s], xs_sems.at[s]).wait()
        return carry

    sub = iota((PHASES, BLOCK), 0)
    lane = iota((PHASES, BLOCK), 1)
    late = lane >= sub

    def toeplitz(slot):
        bands = []
        for k in range(CHUNK):
            tail = jnp.zeros((PHASES, BLOCK), jnp.float32)
            band = []
            for c in range(3):
                turned = []
                for h in range(2):
                    at = c * L + h * BLOCK
                    row = jnp.broadcast_to(slot[k : k + 1, at : at + BLOCK], (PHASES, BLOCK))
                    turned.append(pltpu.roll(row, 0, 1, stride=1, stride_axis=0))
                band.append(jnp.where(late, turned[0], 0.0).astype(jnp.bfloat16))
                band.append(jnp.where(late, turned[1], turned[0]).astype(jnp.bfloat16))
                rest = jnp.where(late, 0.0, turned[1])
                tail = tail + (rest if c == 0 else pltpu.roll(rest, c * PHASES, 1))
            band.append(tail.astype(jnp.bfloat16))
            bands.append(jnp.concatenate(band, axis=1))
        return jnp.concatenate(bands, axis=0)

    def chunk(i):
        first = pl.multiple_of(i * CHUNK, CHUNK)
        s = table_ref[0, first]
        slot = sorted_ref[pl.ds(first, CHUNK), :]
        mean = jnp.sum(slot * slot, axis=1, keepdims=True) / (3.0 * L)
        unit = 1.0 / jnp.sqrt(mean + EPS)
        corr = dot(toeplitz(slot), xs_ref[s])
        inv = inv_ref[s]
        for k in range(CHUNK):
            y = corr[k * PHASES : (k + 1) * PHASES] * (inv * unit[k : k + 1, :])
            move = table_ref[1, first + k] * (BLOCK // PHASES)
            turned = [
                pltpu.roll(y[:, b * BLOCK : (b + 1) * BLOCK], (BLOCK - move) % BLOCK, 1) for b in range(3)
            ]
            stay = lane < BLOCK - move
            target = table_ref[3, first + k]
            held_ref[target, :, :BLOCK] += jnp.where(stay, turned[0], turned[1])
            held_ref[target, :, BLOCK : 2 * BLOCK] += jnp.where(stay, turned[1], turned[2])
            held_ref[target, :, 2 * BLOCK :] += turned[2]

    def two_chunks(i, ready):
        last = jnp.maximum(table_ref[0, 16 * i], table_ref[0, 16 * i + 8]) + 1
        lax.fori_loop(ready, last, arrive, 0)
        chunk(2 * i)
        chunk(2 * i + 1)
        return jnp.maximum(ready, last)

    ready = lax.fori_loop(0, (table_ref[4, 0] + 1) // 2, two_chunks, 0)
    lax.fori_loop(ready, stations, arrive, 0)
    end = KEPT - 2 * BLOCK

    def finish(ref, o, at):
        last = jnp.zeros((PHASES, BLOCK), jnp.float32)
        for r in range(HALF):
            y = held_ref[at * 4 + r]
            a, b = y[:, :BLOCK], y[:, BLOCK : 2 * BLOCK]
            c = jnp.where(lane < end, y[:, 2 * BLOCK :], 0.0)
            top = jnp.maximum(jnp.maximum(jnp.abs(a), jnp.abs(b)), jnp.abs(c))
            top = jnp.maximum(jnp.max(top, axis=1, keepdims=True), 2.0**-110)
            power = jnp.ceil(FINE * jnp.log2(jnp.broadcast_to(top, (PHASES, BLOCK))))
            scale = FULL * jnp.exp2(power * (-1.0 / FINE))
            ref[o, 2 * r] = jnp.round(a * scale).astype(jnp.int32).astype(jnp.int16)
            ref[o, 2 * r + 1] = jnp.round(b * scale).astype(jnp.int32).astype(jnp.int16)
            c = jnp.round(c * scale)
            last = last + (c if r == 0 else pltpu.roll(c, end * r, 1))
            last = jnp.where(lane == HALF * end + r, power, last)
        ref[o, 2 * HALF] = last.astype(jnp.int32).astype(jnp.int16)

    @pl.loop(0, width // 2)
    def _(i):
        finish(out_ref, 2 * i, 2 * i)
        finish(out_ref, 2 * i + 1, 2 * i + 1)

    @pl.when(table_ref[5, 0] > 0)
    def _():
        @pl.loop(0, width)
        def _(o):
            finish(more_ref, o, width + o)


def add_kernel(list_ref, count_ref, back_ref, stack_ref, best_ref, scale_ref, tail_ref):
    end = KEPT - 2 * BLOCK

    def wide(x):
        return x.astype(jnp.int32).astype(jnp.float32)

    @pl.loop(0, back_ref.shape[0] // 2)
    def _(i):
        for o in (2 * i, 2 * i + 1):
            last = wide(back_ref[o, 2 * HALF])
            scales = jnp.exp2(last * (1.0 / FINE)) * (1.0 / FULL)
            for r in range(HALF):
                at = HALF * end + r
                scale_ref[o * 4 + r] = jnp.broadcast_to(scales[:, at : at + 1], (PHASES, BLOCK))
                tail_ref[o * 4 + r] = last if r == 0 else pltpu.roll(last, BLOCK - end * r, 1)

    def one_template(t, best):
        count = count_ref[t]
        number = list_ref[t, BLOCK - 1]

        def four_traces(g, total):
            for i in range(4):
                entry = list_ref[t, 4 * g + i]
                o = entry // 4
                r = entry % 4
                scale = jnp.where(4 * g + i < number, scale_ref[entry], 0.0)
                parts = (wide(back_ref[o, 2 * r]), wide(back_ref[o, 2 * r + 1]), tail_ref[entry])
                total = tuple(a + p * scale for a, p in zip(total, parts))
            return total

        zero = jnp.zeros((PHASES, BLOCK), jnp.float32)
        total = lax.fori_loop(0, (number + 3) // 4, four_traces, (zero, zero, zero))
        factor = jnp.sqrt(3.0 * L / jnp.full((1, 1), count, jnp.int32).astype(jnp.float32))
        whole = jnp.concatenate(total, axis=1) * factor
        stack_ref[t] = whole[:, :KEPT]
        return jnp.maximum(best, whole)

    start = jnp.full((PHASES, WIDE), -jnp.inf, jnp.float32)
    best = lax.fori_loop(0, stack_ref.shape[0], one_template, start)
    best_ref[...] = best[:, :KEPT]


VMEM = pl.BlockSpec(memory_space=pltpu.VMEM)
ANY = pl.BlockSpec(memory_space=pl.ANY)
SMEM = pl.BlockSpec(memory_space=pltpu.SMEM)


def params(mib):
    return pltpu.CompilerParams(vmem_limit_bytes=mib * 2**20)


def correlate_call(got, xs, inv):
    width = got.shape[0]
    stations = xs.shape[0]
    room = 8 * (width * CAP // CHUNK + stations)
    return pl.pallas_call(
        correlate_kernel,
        out_shape=(
            jax.ShapeDtypeStruct((width, BLOCKS, PHASES, BLOCK), jnp.int16),
            jax.ShapeDtypeStruct((width, BLOCKS, PHASES, BLOCK), jnp.int16),
            jax.ShapeDtypeStruct((1, BLOCK), jnp.int32),
        ),
        in_specs=[VMEM, ANY, VMEM],
        out_specs=(VMEM, VMEM, VMEM),
        scratch_shapes=[
            pltpu.VMEM((stations, DEPTH, WIDE), jnp.bfloat16),
            pltpu.VMEM((room, 3 * L), jnp.float32),
            pltpu.VMEM((8, room), jnp.int32),
            pltpu.VMEM((8 * width + 8, PHASES, WIDE), jnp.float32),
            pltpu.SMEM((8, room), jnp.int32),
            pltpu.SemaphoreType.DMA,
            pltpu.SemaphoreType.DMA((stations,)),
        ],
        compiler_params=params(54),
    )(got, xs, inv)


def add_call(listed, counts, back):
    tpl_dev = counts.shape[0]
    return pl.pallas_call(
        add_kernel,
        out_shape=(
            jax.ShapeDtypeStruct((tpl_dev, PHASES, KEPT), jnp.float32),
            jax.ShapeDtypeStruct((PHASES, KEPT), jnp.float32),
        ),
        in_specs=[SMEM, SMEM, VMEM],
        out_specs=(VMEM, VMEM),
        scratch_shapes=[
            pltpu.VMEM((back.shape[0] * 4, PHASES, BLOCK), jnp.float32),
            pltpu.VMEM((back.shape[0] * 4, PHASES, BLOCK), jnp.float32),
        ],
        compiler_params=params(32),
    )(listed, counts, back)


def body(waveforms, station_home, templates, template_stations, station_counts, moveouts):
    stations, _, samples = waveforms.shape
    tpl_dev = templates.shape[0]
    width = lax.axis_size("sta")
    parts = station_home.shape[0] // BLOCK
    send, listed = pl.pallas_call(
        pack_kernel,
        out_shape=(
            jax.ShapeDtypeStruct((width, ROWS, DEPTH), jnp.bfloat16),
            jax.ShapeDtypeStruct((tpl_dev, BLOCK), jnp.int32),
        ),
        in_specs=[ANY] * 5,
        out_specs=(VMEM, VMEM),
        scratch_shapes=[
            pltpu.VMEM((tpl_dev, SLOTS), jnp.int32),
            pltpu.VMEM((tpl_dev, SLOTS), jnp.int32),
            pltpu.SMEM((tpl_dev,), jnp.int32),
            pltpu.VMEM((parts, BLOCK), jnp.int32),
            pltpu.VMEM((SLOTS, tpl_dev, 3 * L), jnp.bfloat16),
            pltpu.SemaphoreType.DMA((5,)),
        ],
        compiler_params=params(60),
    )(
        template_stations,
        moveouts,
        station_counts,
        station_home.reshape(parts, BLOCK),
        templates.transpose(1, 0, 2),
    )
    got = lax.all_to_all(send, "sta", split_axis=0, concat_axis=0, tiled=True)
    xs, inv = pl.pallas_call(
        prep_kernel,
        grid=(stations,),
        out_shape=(
            jax.ShapeDtypeStruct((stations, DEPTH, WIDE), jnp.bfloat16),
            jax.ShapeDtypeStruct((stations, PHASES, WIDE), jnp.float32),
        ),
        in_specs=[pl.BlockSpec((3, stations, samples), lambda s: (0, 0, 0))],
        out_specs=(
            pl.BlockSpec((1, DEPTH, WIDE), lambda s: (s, 0, 0)),
            pl.BlockSpec((1, PHASES, WIDE), lambda s: (s, 0, 0)),
        ),
        scratch_shapes=[pltpu.VMEM((3, stations, samples), jnp.float32)],
        compiler_params=params(50),
        cost_estimate=pl.CostEstimate(flops=2 * 10**9, bytes_accessed=12 * 2**20, transcendentals=0),
    )(waveforms.transpose(1, 0, 2))
    traces, more, flag = correlate_call(got, xs, inv)

    def home(x):
        return lax.all_to_all(x, "sta", split_axis=0, concat_axis=0, tiled=True)

    def one_exchange(traces, more):
        return add_call(listed, station_counts, home(traces))

    def two_exchanges(traces, more):
        return add_call(listed, station_counts, jnp.concatenate([home(traces), home(more)]))

    stack, best = lax.cond(flag[0, 0] > 0, two_exchanges, one_exchange, traces, more)
    stack = stack.transpose(0, 2, 1).reshape(tpl_dev, PHASES * KEPT)
    best = best.T.reshape(PHASES * KEPT)
    network = best_of_all(best.reshape(-1, BLOCK)).reshape(PHASES * KEPT)
    return (stack, network)


def best_of_all(best):
    for axis in ("tpl", "sta"):
        size = lax.axis_size(axis)
        step = 1
        while step < size:
            other = lax.ppermute(best, axis, [(i, i ^ step) for i in range(size)])
            best = jnp.maximum(best, other)
            step *= 2
    return best


def solution(mesh):
    in_specs = (
        P("sta", None, None),
        P(),
        P(("sta", "tpl"), None, None),
        P(("sta", "tpl"), None),
        P(("sta", "tpl")),
        P(("sta", "tpl"), None),
    )
    out_specs = (P(("sta", "tpl"), None), P())
    return jax.shard_map(body, mesh=mesh, in_specs=in_specs, out_specs=out_specs, check_vma=False)
```

```python
import functools

import jax
import jax.numpy as jnp
from jax import lax
from jax.experimental import pallas as pl
from jax.experimental.pallas import tpu as pltpu
from jax.sharding import PartitionSpec as P

SLOTS = 20
L = 256
BLOCK = 128
LAG_BLOCKS = 40
MOVE_BLOCKS = 4
EPS = 1e-06

PHASES = 16
COLS = LAG_BLOCKS * BLOCK // PHASES
KEPT = (LAG_BLOCKS - MOVE_BLOCKS) * BLOCK // PHASES
WIDE = 384
REACH = L // PHASES
DEPTH = 3 * L + BLOCK
INV = 3 * L + 3 * PHASES
CHUNK = 8
CAP = 6
ROWS = 8
HALF = 3
BLOCKS = 7

FINE = 8.0
FULL = 32700.0
NT = (((1,), (1,)), ((), ()))


def iota(shape, dim):
    return lax.broadcasted_iota(jnp.int32, shape, dim)


def dot(a, b, dims=None):
    if dims is None:
        dims = (((1,), (0,)), ((), ()))
    return lax.dot_general(a, b, dims, preferred_element_type=jnp.float32)


def pack_kernel(
    stations_hbm, moves_hbm, counts_hbm, home_hbm, templates_hbm, send_ref, list_ref,
    stations_ref, moves_ref, counts_ref, home_ref, templates_ref, sems,
):
    copies = [
        pltpu.make_async_copy(src, dst, sems.at[i])
        for i, (src, dst) in enumerate(
            (
                (stations_hbm, stations_ref),
                (moves_hbm, moves_ref),
                (counts_hbm, counts_ref),
                (home_hbm, home_ref),
                (templates_hbm, templates_ref),
            )
        )
    ]
    for copy in copies:
        copy.start()
    tpl_dev, slots = stations_ref.shape
    total = tpl_dev * slots
    width = send_ref.shape[0]
    parts = home_ref.shape[0]
    sta_dev = parts * BLOCK // width
    place = iota((1, total), 1)
    of_template = place % tpl_dev
    for copy in copies[:4]:
        copy.wait()
    stations = stations_ref[...]
    high = stations // 16
    fields = jnp.concatenate([high, stations - 16 * high, moves_ref[...]], axis=0)
    expand = (iota((slots, total), 1) // tpl_dev == iota((slots, total), 0)).astype(jnp.bfloat16)
    spread = dot(fields.astype(jnp.float32).astype(jnp.bfloat16), expand)
    mine = iota((tpl_dev, total), 0) == of_template
    rows = [
        jnp.sum(jnp.where(mine, spread[i * tpl_dev : (i + 1) * tpl_dev], 0.0), axis=0, keepdims=True)
        for i in range(3)
    ]
    station = (rows[0] * 16.0 + rows[1]).astype(jnp.int32)
    moves = rows[2]
    counts = jnp.zeros((1, total), jnp.int32)
    for t in range(tpl_dev):
        counts = jnp.where(of_template == t, counts_ref[t], counts)
    home = home_ref[...]
    owners = home // sta_dev
    table = jnp.concatenate([owners, home - owners * sta_dev], axis=0)
    hit = (iota((BLOCK, total), 0) == station % BLOCK).astype(jnp.bfloat16)
    found = dot(table.astype(jnp.float32).astype(jnp.bfloat16), hit)
    part = iota((parts, total), 0) == station // BLOCK
    owner = jnp.sum(jnp.where(part, found[:parts], 0.0), axis=0, keepdims=True).astype(jnp.int32)
    local = jnp.sum(jnp.where(part, found[parts:], 0.0), axis=0, keepdims=True)
    live = place // tpl_dev < counts
    before = (iota((total, total), 0) < iota((total, total), 1)).astype(jnp.bfloat16)
    pairs = width * tpl_dev
    of_pair = jnp.where((iota((pairs, total), 0) == owner * tpl_dev + of_template) & live, 1.0, 0.0)
    earlier = jnp.sum(of_pair * dot(of_pair.astype(jnp.bfloat16), before), axis=0, keepdims=True)
    first = live & (earlier < 0.5)
    present = jnp.minimum(jnp.sum(of_pair, axis=1, keepdims=True), 1.0)
    row, col = iota((pairs, pairs), 0), iota((pairs, pairs), 1)
    lower = ((row // tpl_dev == col // tpl_dev) & (col < row)).astype(jnp.bfloat16)
    order = dot(lower, jnp.broadcast_to(present, (pairs, BLOCK)).astype(jnp.bfloat16))[:, 0:1]
    turn = jnp.sum(of_pair * order, axis=0, keepdims=True)
    over = jnp.max(jnp.where(live & (turn > HALF - 0.5), 1.0, 0.0))
    late = turn > HALF - 0.5
    home_of = (jnp.where(late, width, 0) + owner) * 4 + jnp.where(late, turn - HALF, turn).astype(jnp.int32)
    own_first = jnp.where((iota((tpl_dev, total), 0) == of_template) & first, 1.0, 0.0)
    nth = dot(own_first.astype(jnp.bfloat16), before)
    nth = jnp.sum(own_first * nth, axis=0, keepdims=True).astype(jnp.int32)
    entry = (iota((BLOCK, total), 0) == nth).astype(jnp.bfloat16)
    listed = dot((own_first * home_of.astype(jnp.float32)).astype(jnp.bfloat16), entry, NT)
    number = jnp.sum(own_first, axis=1, keepdims=True)
    list_ref[...] = jnp.where(iota((tpl_dev, BLOCK), 1) == BLOCK - 1, number, listed).astype(jnp.int32)
    at_owner = jnp.where((iota((width, total), 0) == owner) & live, 1.0, 0.0)
    rank = jnp.sum(at_owner * dot(at_owner.astype(jnp.bfloat16), before), axis=0, keepdims=True)
    dest = jnp.where(live, owner * ROWS + rank.astype(jnp.int32), -1)
    pick = (iota((width * ROWS, total), 0) == dest).astype(jnp.bfloat16)
    kind = iota((BLOCK, total), 0)
    fields = jnp.where(kind == 0, local, jnp.where(kind == 1, moves, jnp.where(kind == 2, 1.0, 0.0)))
    fields = jnp.where(kind == 3, turn, fields).astype(jnp.bfloat16)
    tail = dot(pick, fields, NT)
    tail = jnp.where(iota(tail.shape, 1) == 4, over, tail).astype(jnp.bfloat16)
    copies[4].wait()
    send = dot(pick, templates_ref[...].reshape(total, 3 * L)).astype(jnp.bfloat16)
    send_ref[:, :, : 3 * L] = send.reshape(width, ROWS, 3 * L)
    send_ref[:, :, 3 * L :] = tail.reshape(width, ROWS, BLOCK)


def prep_kernel(wave_ref, xs_hbm, xs_ref, wide_ref, sems):
    tiles = wave_ref.shape[2] // BLOCK
    wide_ref[...] = wave_ref[...].astype(jnp.float32)
    lane = iota((8, BLOCK), 1)
    own = (lane // PHASES == iota((8, BLOCK), 0)).astype(jnp.float32)
    spread = (
        (iota((3 * PHASES, 3 * BLOCK), 1) // BLOCK == iota((3 * PHASES, 3 * BLOCK), 0) // PHASES)
        & (iota((3 * PHASES, 3 * BLOCK), 1) % PHASES == iota((3 * PHASES, 3 * BLOCK), 0) % PHASES)
    ).astype(jnp.bfloat16)
    sub = iota((PHASES, WIDE), 0)

    def one_station(s):
        comps = []
        for c in range(3):
            parts = []
            group = wide_ref[c, pl.ds(pl.multiple_of(s // 8 * 8, 8), 8), :]
            line = pltpu.roll(group, (8 - s % 8) % 8, 0)[0:1, :]
            for r in range(tiles):
                row = line[:, r * BLOCK : (r + 1) * BLOCK]
                parts.append(jnp.broadcast_to(row, (8, BLOCK)) * own)
            parts.append(jnp.zeros((WIDE - 8 * tiles, BLOCK), jnp.float32))
            comps.append(jnp.concatenate(parts, axis=0).astype(jnp.bfloat16))
        grid = jnp.concatenate(comps, axis=1)
        phases = dot(spread, grid, NT)
        squares = jnp.zeros((PHASES, WIDE), jnp.float32)
        for c in range(3):
            x = phases[c * PHASES : (c + 1) * PHASES]
            squares = squares + x * x
            for r in range(REACH + 1):
                moved = x if r == 0 else pltpu.roll(x, WIDE - r, 1)
                at = c * L + r * PHASES if r < REACH else 3 * L + c * PHASES
                xs_ref[s, at : at + PHASES, :] = moved.astype(jnp.bfloat16)
        up = squares
        down = jnp.where(sub >= 1, pltpu.roll(squares, 1, 0), 0.0)
        for step in (1, 2, 4, 8):
            up = up + jnp.where(sub < PHASES - step, pltpu.roll(up, PHASES - step, 0), 0.0)
            down = down + jnp.where(sub >= step, pltpu.roll(down, step, 0), 0.0)
        whole = jnp.broadcast_to(up[0:1, :], (PHASES, WIDE))
        two = whole + pltpu.roll(whole, WIDE - 1, 1)
        four = two + pltpu.roll(two, WIDE - 2, 1)
        eight = four + pltpu.roll(four, WIDE - 4, 1)
        fifteen = (
            pltpu.roll(eight, WIDE - 1, 1)
            + pltpu.roll(four, WIDE - 9, 1)
            + pltpu.roll(two, WIDE - 13, 1)
            + pltpu.roll(whole, WIDE - 15, 1)
        )
        power = (up + fifteen + pltpu.roll(down, WIDE - REACH, 1)) / (3.0 * L)
        inv = 1.0 / (3.0 * L * jnp.sqrt(power + EPS))
        for i in range(3):
            term = inv.astype(jnp.bfloat16)
            xs_ref[s, INV + i * PHASES : INV + (i + 1) * PHASES, :] = term
            inv = inv - term.astype(jnp.float32)
        xs_ref[s, INV + 3 * PHASES :, :] = jnp.zeros((DEPTH - INV - 3 * PHASES, WIDE), jnp.bfloat16)

    @pl.loop(0, wave_ref.shape[1] // 2)
    def _(i):
        one_station(2 * i)
        one_station(2 * i + 1)
        pair = pl.ds(2 * i, 2)
        pltpu.make_async_copy(xs_ref.at[pair], xs_hbm.at[pair], sems.at[i]).start()

    @pl.loop(0, wave_ref.shape[1] // 2)
    def _(i):
        pair = pl.ds(2 * i, 2)
        pltpu.make_async_copy(xs_ref.at[pair], xs_hbm.at[pair], sems.at[i]).wait()


def correlate_kernel(
    got_ref, xs_hbm, out_ref, more_ref, flag_ref, xs_ref, sorted_ref, order_ref, held_ref, table_ref, sem, xs_sems
):
    width = got_ref.shape[0]
    stations = xs_ref.shape[0]
    total = width * ROWS
    room = sorted_ref.shape[0]
    loads = [pltpu.make_async_copy(xs_hbm.at[s], xs_ref.at[s], xs_sems.at[s]) for s in range(stations)]
    for load in loads:
        load.start()
    got = got_ref[...].reshape(total, DEPTH)
    pieces = got[:, : 3 * L]
    eye = (iota((8, BLOCK), 0) == iota((8, BLOCK), 1)).astype(jnp.bfloat16)
    fields = dot(eye, got[:, 3 * L :], NT)
    live = fields[2:3, :] > 0.5
    at_station = jnp.where(
        (iota((stations, total), 0) == fields[0:1, :].astype(jnp.int32)) & live, 1.0, 0.0
    )
    before = (iota((total, total), 0) < iota((total, total), 1)).astype(jnp.bfloat16)
    rank = dot(at_station.astype(jnp.bfloat16), before)
    chunks = jnp.floor((jnp.sum(at_station, axis=1, keepdims=True) + (CHUNK - 1)) / CHUNK)
    earlier = (iota((stations, stations), 1) < iota((stations, stations), 0)).astype(jnp.bfloat16)
    start = dot(earlier, jnp.broadcast_to(chunks, (stations, BLOCK)).astype(jnp.bfloat16))[:, 0:1]
    place = jnp.sum(at_station * (start * CHUNK + rank), axis=0, keepdims=True).astype(jnp.int32)
    place = jnp.where(live, place, -1)
    pick = (iota((room, total), 0) == place).astype(jnp.bfloat16)
    kind = iota((8, total), 0)
    late = fields[3:4, :] > HALF - 0.5
    source = iota((1, total), 1) // ROWS
    turn = jnp.where(late, fields[3:4, :] - HALF, fields[3:4, :]).astype(jnp.int32)
    target = ((jnp.where(late, width, 0) + source) * 4 + turn).astype(jnp.float32)
    rows = jnp.where(kind == 3, target, jnp.where(kind < 3, fields, 0.0)).astype(jnp.bfloat16)
    table = dot(rows, pick, NT)
    over = jnp.max(fields[4:5, :])
    kind = iota((8, room), 0)
    table = jnp.where((kind == 3) & (table[2:3, :] < 0.5), float(held_ref.shape[0] - 1), table)
    table = jnp.where(kind == 4, jnp.sum(chunks), jnp.where(kind == 5, over, table))
    order_ref[...] = table.astype(jnp.int32)
    copy = pltpu.make_async_copy(order_ref, table_ref, sem)
    copy.start()
    flag_ref[...] = jnp.full(flag_ref.shape, over, jnp.float32).astype(jnp.int32)
    sorted_ref[...] = dot(pick, pieces)
    blank = jnp.zeros((PHASES, WIDE), jnp.float32)

    @pl.loop(0, held_ref.shape[0] // 8)
    def _(i):
        for r in range(8):
            held_ref[8 * i + r] = blank

    copy.wait()

    def arrive(s, carry):
        pltpu.make_async_copy(xs_hbm.at[s], xs_ref.at[s], xs_sems.at[s]).wait()
        return carry

    sub = iota((PHASES, BLOCK), 0)
    lane = iota((PHASES, BLOCK), 1)
    late = lane >= sub

    def toeplitz(slot):
        bands = []
        for k in range(CHUNK):
            tail = jnp.zeros((PHASES, BLOCK), jnp.float32)
            band = []
            for c in range(3):
                turned = []
                for h in range(2):
                    at = c * L + h * BLOCK
                    row = jnp.broadcast_to(slot[k : k + 1, at : at + BLOCK], (PHASES, BLOCK))
                    turned.append(pltpu.roll(row, 0, 1, stride=1, stride_axis=0))
                band.append(jnp.where(late, turned[0], 0.0).astype(jnp.bfloat16))
                band.append(jnp.where(late, turned[1], turned[0]).astype(jnp.bfloat16))
                rest = jnp.where(late, 0.0, turned[1])
                tail = tail + (rest if c == 0 else pltpu.roll(rest, c * PHASES, 1))
            band.append(tail.astype(jnp.bfloat16))
            bands.append(jnp.concatenate(band, axis=1))
        return jnp.concatenate(bands, axis=0)

    def chunk(i):
        first = pl.multiple_of(i * CHUNK, CHUNK)
        s = table_ref[0, first]
        slot = sorted_ref[pl.ds(first, CHUNK), :]
        mean = jnp.sum(slot * slot, axis=1, keepdims=True) / (3.0 * L)
        unit = 1.0 / jnp.sqrt(mean + EPS)
        corr = dot(toeplitz(slot), xs_ref[s])
        parts = [xs_ref[s, INV + i * PHASES : INV + (i + 1) * PHASES, :].astype(jnp.float32) for i in range(3)]
        inv = (parts[2] + parts[1]) + parts[0]
        for k in range(CHUNK):
            y = corr[k * PHASES : (k + 1) * PHASES] * (inv * unit[k : k + 1, :])
            move = table_ref[1, first + k] * (BLOCK // PHASES)
            turned = [
                pltpu.roll(y[:, b * BLOCK : (b + 1) * BLOCK], (BLOCK - move) % BLOCK, 1) for b in range(3)
            ]
            stay = lane < BLOCK - move
            target = table_ref[3, first + k]
            held_ref[target, :, :BLOCK] += jnp.where(stay, turned[0], turned[1])
            held_ref[target, :, BLOCK : 2 * BLOCK] += jnp.where(stay, turned[1], turned[2])
            held_ref[target, :, 2 * BLOCK :] += turned[2]

    def two_chunks(i, ready):
        last = jnp.maximum(table_ref[0, 16 * i], table_ref[0, 16 * i + 8]) + 1
        lax.fori_loop(ready, last, arrive, 0)
        chunk(2 * i)
        chunk(2 * i + 1)
        return jnp.maximum(ready, last)

    ready = lax.fori_loop(0, (table_ref[4, 0] + 1) // 2, two_chunks, 0)
    lax.fori_loop(ready, stations, arrive, 0)
    end = KEPT - 2 * BLOCK

    def finish(ref, o, at):
        last = jnp.zeros((PHASES, BLOCK), jnp.float32)
        for r in range(HALF):
            y = held_ref[at * 4 + r]
            a, b = y[:, :BLOCK], y[:, BLOCK : 2 * BLOCK]
            c = jnp.where(lane < end, y[:, 2 * BLOCK :], 0.0)
            top = jnp.maximum(jnp.maximum(jnp.abs(a), jnp.abs(b)), jnp.abs(c))
            top = jnp.maximum(jnp.max(top, axis=1, keepdims=True), 2.0**-110)
            power = jnp.ceil(FINE * jnp.log2(jnp.broadcast_to(top, (PHASES, BLOCK))))
            scale = FULL * jnp.exp2(power * (-1.0 / FINE))
            ref[o, 2 * r] = jnp.round(a * scale).astype(jnp.int32).astype(jnp.int16)
            ref[o, 2 * r + 1] = jnp.round(b * scale).astype(jnp.int32).astype(jnp.int16)
            c = jnp.round(c * scale)
            last = last + (c if r == 0 else pltpu.roll(c, end * r, 1))
            last = jnp.where(lane == HALF * end + r, power, last)
        ref[o, 2 * HALF] = last.astype(jnp.int32).astype(jnp.int16)

    @pl.loop(0, width // 2)
    def _(i):
        finish(out_ref, 2 * i, 2 * i)
        finish(out_ref, 2 * i + 1, 2 * i + 1)

    @pl.when(table_ref[5, 0] > 0)
    def _():
        @pl.loop(0, width)
        def _(o):
            finish(more_ref, o, width + o)


def add_kernel(list_ref, count_ref, back_ref, stack_ref, best_ref, scale_ref, tail_ref):
    end = KEPT - 2 * BLOCK

    def wide(x):
        return x.astype(jnp.int32).astype(jnp.float32)

    @pl.loop(0, back_ref.shape[0] // 2)
    def _(i):
        for o in (2 * i, 2 * i + 1):
            last = wide(back_ref[o, 2 * HALF])
            scales = jnp.exp2(last * (1.0 / FINE)) * (1.0 / FULL)
            for r in range(HALF):
                at = HALF * end + r
                scale_ref[o * 4 + r] = jnp.broadcast_to(scales[:, at : at + 1], (PHASES, BLOCK))
                tail_ref[o * 4 + r] = last if r == 0 else pltpu.roll(last, BLOCK - end * r, 1)

    def one_template(t, best):
        count = count_ref[t]
        number = list_ref[t, BLOCK - 1]

        def four_traces(g, total):
            for i in range(4):
                entry = list_ref[t, 4 * g + i]
                o = entry // 4
                r = entry % 4
                scale = jnp.where(4 * g + i < number, scale_ref[entry], 0.0)
                parts = (wide(back_ref[o, 2 * r]), wide(back_ref[o, 2 * r + 1]), tail_ref[entry])
                total = tuple(a + p * scale for a, p in zip(total, parts))
            return total

        zero = jnp.zeros((PHASES, BLOCK), jnp.float32)
        total = lax.fori_loop(0, (number + 3) // 4, four_traces, (zero, zero, zero))
        factor = jnp.sqrt(3.0 * L / jnp.full((1, 1), count, jnp.int32).astype(jnp.float32))
        whole = jnp.concatenate(total, axis=1) * factor
        stack_ref[t] = whole[:, :KEPT]
        return jnp.maximum(best, whole)

    start = jnp.full((PHASES, WIDE), -jnp.inf, jnp.float32)
    best = lax.fori_loop(0, stack_ref.shape[0], one_template, start)
    best_ref[...] = best[:, :KEPT]


VMEM = pl.BlockSpec(memory_space=pltpu.VMEM)
ANY = pl.BlockSpec(memory_space=pl.ANY)
SMEM = pl.BlockSpec(memory_space=pltpu.SMEM)


def params(mib):
    return pltpu.CompilerParams(vmem_limit_bytes=mib * 2**20)


def correlate_call(got, xs, stations):
    width = got.shape[0]
    room = 8 * (width * CAP // CHUNK + stations)
    return pl.pallas_call(
        correlate_kernel,
        out_shape=(
            jax.ShapeDtypeStruct((width, BLOCKS, PHASES, BLOCK), jnp.int16),
            jax.ShapeDtypeStruct((width, BLOCKS, PHASES, BLOCK), jnp.int16),
            jax.ShapeDtypeStruct((1, BLOCK), jnp.int32),
        ),
        in_specs=[VMEM, ANY],
        out_specs=(VMEM, VMEM, VMEM),
        scratch_shapes=[
            pltpu.VMEM((stations, DEPTH, WIDE), jnp.bfloat16),
            pltpu.VMEM((room, 3 * L), jnp.float32),
            pltpu.VMEM((8, room), jnp.int32),
            pltpu.VMEM((8 * width + 8, PHASES, WIDE), jnp.float32),
            pltpu.SMEM((8, room), jnp.int32),
            pltpu.SemaphoreType.DMA,
            pltpu.SemaphoreType.DMA((stations,)),
        ],
        compiler_params=params(40),
    )(got, xs)


def add_call(listed, counts, back):
    tpl_dev = counts.shape[0]
    return pl.pallas_call(
        add_kernel,
        out_shape=(
            jax.ShapeDtypeStruct((tpl_dev, PHASES, KEPT), jnp.float32),
            jax.ShapeDtypeStruct((PHASES, KEPT), jnp.float32),
        ),
        in_specs=[SMEM, SMEM, VMEM],
        out_specs=(VMEM, VMEM),
        scratch_shapes=[
            pltpu.VMEM((back.shape[0] * 4, PHASES, BLOCK), jnp.float32),
            pltpu.VMEM((back.shape[0] * 4, PHASES, BLOCK), jnp.float32),
        ],
        compiler_params=params(40),
    )(listed, counts, back)


def body(waveforms, station_home, templates, template_stations, station_counts, moveouts):
    stations, _, samples = waveforms.shape
    tpl_dev = templates.shape[0]
    width = lax.axis_size("sta")
    parts = station_home.shape[0] // BLOCK
    send, listed = pl.pallas_call(
        pack_kernel,
        out_shape=(
            jax.ShapeDtypeStruct((width, ROWS, DEPTH), jnp.bfloat16),
            jax.ShapeDtypeStruct((tpl_dev, BLOCK), jnp.int32),
        ),
        in_specs=[ANY] * 5,
        out_specs=(VMEM, VMEM),
        scratch_shapes=[
            pltpu.VMEM((tpl_dev, SLOTS), jnp.int32),
            pltpu.VMEM((tpl_dev, SLOTS), jnp.int32),
            pltpu.SMEM((tpl_dev,), jnp.int32),
            pltpu.VMEM((parts, BLOCK), jnp.int32),
            pltpu.VMEM((SLOTS, tpl_dev, 3 * L), jnp.bfloat16),
            pltpu.SemaphoreType.DMA((5,)),
        ],
        compiler_params=params(60),
    )(
        template_stations,
        moveouts,
        station_counts,
        station_home.reshape(parts, BLOCK),
        templates.transpose(1, 0, 2),
    )
    got = lax.all_to_all(send, "sta", split_axis=0, concat_axis=0, tiled=True)
    xs = pl.pallas_call(
        prep_kernel,
        out_shape=jax.ShapeDtypeStruct((2 * stations + 4, DEPTH, WIDE), jnp.bfloat16),
        in_specs=[VMEM],
        out_specs=ANY,
        scratch_shapes=[
            pltpu.VMEM((stations, DEPTH, WIDE), jnp.bfloat16),
            pltpu.VMEM((3, stations, samples), jnp.float32),
            pltpu.SemaphoreType.DMA((stations // 2,)),
        ],
        compiler_params=params(40),
        cost_estimate=pl.CostEstimate(flops=2 * 10**9, bytes_accessed=12 * 2**20, transcendentals=0),
    )(waveforms.transpose(1, 0, 2))
    traces, more, flag = correlate_call(got, xs, stations)

    def home(x):
        return lax.all_to_all(x, "sta", split_axis=0, concat_axis=0, tiled=True)

    def one_exchange(traces, more):
        return add_call(listed, station_counts, home(traces))

    def two_exchanges(traces, more):
        return add_call(listed, station_counts, jnp.concatenate([home(traces), home(more)]))

    stack, best = lax.cond(flag[0, 0] > 0, two_exchanges, one_exchange, traces, more)
    stack = stack.transpose(0, 2, 1).reshape(tpl_dev, PHASES * KEPT)
    best = best.T.reshape(PHASES * KEPT)
    network = best_of_all(best.reshape(-1, BLOCK)).reshape(PHASES * KEPT)
    return (stack, network)


def best_of_all(best):
    for axis, steps in (("tpl", (1, 2, 6)), ("sta", (1, 2, 6, 8, 24))):
        size = lax.axis_size(axis)
        for step in steps:
            other = lax.ppermute(best, axis, [(i, i ^ step) for i in range(size)])
            best = jnp.maximum(best, other)
    return best


def solution(mesh):
    in_specs = (
        P("sta", None, None),
        P(),
        P(("sta", "tpl"), None, None),
        P(("sta", "tpl"), None),
        P(("sta", "tpl")),
        P(("sta", "tpl"), None),
    )
    out_specs = (P(("sta", "tpl"), None), P())
    return jax.shard_map(body, mesh=mesh, in_specs=in_specs, out_specs=out_specs, check_vma=False)
```

```python
import functools

import jax
import jax.numpy as jnp
from jax import lax
from jax.experimental import pallas as pl
from jax.experimental.pallas import tpu as pltpu
from jax.sharding import PartitionSpec as P

SLOTS = 20
L = 256
BLOCK = 128
LAG_BLOCKS = 40
MOVE_BLOCKS = 4
EPS = 1e-06

PHASES = 16
COLS = LAG_BLOCKS * BLOCK // PHASES
KEPT = (LAG_BLOCKS - MOVE_BLOCKS) * BLOCK // PHASES
WIDE = 384
REACH = L // PHASES
DEPTH = 3 * L + BLOCK
INV = 3 * L + 3 * PHASES
CHUNK = 8
CAP = 6
ROWS = 8
HALF = 3
BLOCKS = 7

FINE = 8.0
FULL = 32700.0
NT = (((1,), (1,)), ((), ()))


def iota(shape, dim):
    return lax.broadcasted_iota(jnp.int32, shape, dim)


def dot(a, b, dims=None):
    if dims is None:
        dims = (((1,), (0,)), ((), ()))
    return lax.dot_general(a, b, dims, preferred_element_type=jnp.float32)


def pack_kernel(
    stations_hbm, moves_hbm, counts_hbm, home_hbm, templates_hbm, send_ref, list_ref,
    stations_ref, moves_ref, counts_ref, home_ref, templates_ref, sems,
):
    copies = [
        pltpu.make_async_copy(src, dst, sems.at[i])
        for i, (src, dst) in enumerate(
            (
                (stations_hbm, stations_ref),
                (moves_hbm, moves_ref),
                (counts_hbm, counts_ref),
                (home_hbm, home_ref),
                (templates_hbm, templates_ref),
            )
        )
    ]
    for copy in copies:
        copy.start()
    tpl_dev, slots = stations_ref.shape
    total = tpl_dev * slots
    width = send_ref.shape[0]
    parts = home_ref.shape[0]
    sta_dev = parts * BLOCK // width
    place = iota((1, total), 1)
    of_template = place % tpl_dev
    for copy in copies[:4]:
        copy.wait()
    stations = stations_ref[...]
    high = stations // 16
    fields = jnp.concatenate([high, stations - 16 * high, moves_ref[...]], axis=0)
    expand = (iota((slots, total), 1) // tpl_dev == iota((slots, total), 0)).astype(jnp.bfloat16)
    spread = dot(fields.astype(jnp.float32).astype(jnp.bfloat16), expand)
    mine = iota((tpl_dev, total), 0) == of_template
    rows = [
        jnp.sum(jnp.where(mine, spread[i * tpl_dev : (i + 1) * tpl_dev], 0.0), axis=0, keepdims=True)
        for i in range(3)
    ]
    station = (rows[0] * 16.0 + rows[1]).astype(jnp.int32)
    moves = rows[2]
    counts = jnp.zeros((1, total), jnp.int32)
    for t in range(tpl_dev):
        counts = jnp.where(of_template == t, counts_ref[t], counts)
    home = home_ref[...]
    owners = home // sta_dev
    table = jnp.concatenate([owners, home - owners * sta_dev], axis=0)
    hit = (iota((BLOCK, total), 0) == station % BLOCK).astype(jnp.bfloat16)
    found = dot(table.astype(jnp.float32).astype(jnp.bfloat16), hit)
    part = iota((parts, total), 0) == station // BLOCK
    owner = jnp.sum(jnp.where(part, found[:parts], 0.0), axis=0, keepdims=True).astype(jnp.int32)
    local = jnp.sum(jnp.where(part, found[parts:], 0.0), axis=0, keepdims=True)
    live = place // tpl_dev < counts
    before = (iota((total, total), 0) < iota((total, total), 1)).astype(jnp.bfloat16)
    pairs = width * tpl_dev
    of_pair = jnp.where((iota((pairs, total), 0) == owner * tpl_dev + of_template) & live, 1.0, 0.0)
    earlier = jnp.sum(of_pair * dot(of_pair.astype(jnp.bfloat16), before), axis=0, keepdims=True)
    first = live & (earlier < 0.5)
    present = jnp.minimum(jnp.sum(of_pair, axis=1, keepdims=True), 1.0)
    row, col = iota((pairs, pairs), 0), iota((pairs, pairs), 1)
    lower = ((row // tpl_dev == col // tpl_dev) & (col < row)).astype(jnp.bfloat16)
    order = dot(lower, jnp.broadcast_to(present, (pairs, BLOCK)).astype(jnp.bfloat16))[:, 0:1]
    turn = jnp.sum(of_pair * order, axis=0, keepdims=True)
    over = jnp.max(jnp.where(live & (turn > HALF - 0.5), 1.0, 0.0))
    late = turn > HALF - 0.5
    home_of = (jnp.where(late, width, 0) + owner) * 4 + jnp.where(late, turn - HALF, turn).astype(jnp.int32)
    own_first = jnp.where((iota((tpl_dev, total), 0) == of_template) & first, 1.0, 0.0)
    nth = dot(own_first.astype(jnp.bfloat16), before)
    nth = jnp.sum(own_first * nth, axis=0, keepdims=True).astype(jnp.int32)
    entry = (iota((BLOCK, total), 0) == nth).astype(jnp.bfloat16)
    listed = dot((own_first * home_of.astype(jnp.float32)).astype(jnp.bfloat16), entry, NT)
    number = jnp.sum(own_first, axis=1, keepdims=True)
    list_ref[...] = jnp.where(iota((tpl_dev, BLOCK), 1) == BLOCK - 1, number, listed).astype(jnp.int32)
    at_owner = jnp.where((iota((width, total), 0) == owner) & live, 1.0, 0.0)
    rank = jnp.sum(at_owner * dot(at_owner.astype(jnp.bfloat16), before), axis=0, keepdims=True)
    dest = jnp.where(live, owner * ROWS + rank.astype(jnp.int32), -1)
    pick = (iota((width * ROWS, total), 0) == dest).astype(jnp.bfloat16)
    kind = iota((BLOCK, total), 0)
    fields = jnp.where(kind == 0, local, jnp.where(kind == 1, moves, jnp.where(kind == 2, 1.0, 0.0)))
    fields = jnp.where(kind == 3, turn, fields).astype(jnp.bfloat16)
    tail = dot(pick, fields, NT)
    tail = jnp.where(iota(tail.shape, 1) == 4, over, tail).astype(jnp.bfloat16)
    copies[4].wait()
    send = dot(pick, templates_ref[...].reshape(total, 3 * L)).astype(jnp.bfloat16)
    send_ref[:, :, : 3 * L] = send.reshape(width, ROWS, 3 * L)
    send_ref[:, :, 3 * L :] = tail.reshape(width, ROWS, BLOCK)


def prep_kernel(wave_ref, xs_hbm, xs_ref, wide_ref, sems):
    tiles = wave_ref.shape[2] // BLOCK
    wide_ref[...] = wave_ref[...].astype(jnp.float32)
    lane = iota((8, BLOCK), 1)
    own = (lane // PHASES == iota((8, BLOCK), 0)).astype(jnp.float32)
    spread = (
        (iota((3 * PHASES, 3 * BLOCK), 1) // BLOCK == iota((3 * PHASES, 3 * BLOCK), 0) // PHASES)
        & (iota((3 * PHASES, 3 * BLOCK), 1) % PHASES == iota((3 * PHASES, 3 * BLOCK), 0) % PHASES)
    ).astype(jnp.bfloat16)
    sub = iota((PHASES, WIDE), 0)

    def one_station(s):
        comps = []
        for c in range(3):
            parts = []
            group = wide_ref[c, pl.ds(pl.multiple_of(s // 8 * 8, 8), 8), :]
            line = pltpu.roll(group, (8 - s % 8) % 8, 0)[0:1, :]
            for r in range(tiles):
                row = line[:, r * BLOCK : (r + 1) * BLOCK]
                parts.append(jnp.broadcast_to(row, (8, BLOCK)) * own)
            parts.append(jnp.zeros((WIDE - 8 * tiles, BLOCK), jnp.float32))
            comps.append(jnp.concatenate(parts, axis=0).astype(jnp.bfloat16))
        grid = jnp.concatenate(comps, axis=1)
        phases = dot(spread, grid, NT)
        squares = jnp.zeros((PHASES, WIDE), jnp.float32)
        for c in range(3):
            x = phases[c * PHASES : (c + 1) * PHASES]
            squares = squares + x * x
            for r in range(REACH + 1):
                moved = x if r == 0 else pltpu.roll(x, WIDE - r, 1)
                at = c * L + r * PHASES if r < REACH else 3 * L + c * PHASES
                xs_ref[s, at : at + PHASES, :] = moved.astype(jnp.bfloat16)
        up = squares
        down = jnp.where(sub >= 1, pltpu.roll(squares, 1, 0), 0.0)
        for step in (1, 2, 4, 8):
            up = up + jnp.where(sub < PHASES - step, pltpu.roll(up, PHASES - step, 0), 0.0)
            down = down + jnp.where(sub >= step, pltpu.roll(down, step, 0), 0.0)
        whole = jnp.broadcast_to(up[0:1, :], (PHASES, WIDE))
        two = whole + pltpu.roll(whole, WIDE - 1, 1)
        four = two + pltpu.roll(two, WIDE - 2, 1)
        eight = four + pltpu.roll(four, WIDE - 4, 1)
        fifteen = (
            pltpu.roll(eight, WIDE - 1, 1)
            + pltpu.roll(four, WIDE - 9, 1)
            + pltpu.roll(two, WIDE - 13, 1)
            + pltpu.roll(whole, WIDE - 15, 1)
        )
        power = (up + fifteen + pltpu.roll(down, WIDE - REACH, 1)) / (3.0 * L)
        inv = 1.0 / (3.0 * L * jnp.sqrt(power + EPS))
        for i in range(3):
            term = inv.astype(jnp.bfloat16)
            xs_ref[s, INV + i * PHASES : INV + (i + 1) * PHASES, :] = term
            inv = inv - term.astype(jnp.float32)
        xs_ref[s, INV + 3 * PHASES :, :] = jnp.zeros((DEPTH - INV - 3 * PHASES, WIDE), jnp.bfloat16)

    @pl.loop(0, wave_ref.shape[1] // 2)
    def _(i):
        one_station(2 * i)
        one_station(2 * i + 1)
        pair = pl.ds(2 * i, 2)
        pltpu.make_async_copy(xs_ref.at[pair], xs_hbm.at[pair], sems.at[i]).start()

    @pl.loop(0, wave_ref.shape[1] // 2)
    def _(i):
        pair = pl.ds(2 * i, 2)
        pltpu.make_async_copy(xs_ref.at[pair], xs_hbm.at[pair], sems.at[i]).wait()


def correlate_kernel(
    got_ref, xs_hbm, out_ref, more_ref, flag_ref, xs_ref, sorted_ref, order_ref, held_ref, table_ref, sem, xs_sems
):
    width = got_ref.shape[0]
    stations = xs_ref.shape[0]
    total = width * ROWS
    room = sorted_ref.shape[0]
    loads = [pltpu.make_async_copy(xs_hbm.at[s], xs_ref.at[s], xs_sems.at[s]) for s in range(stations)]
    for load in loads:
        load.start()
    got = got_ref[...].reshape(total, DEPTH)
    pieces = got[:, : 3 * L]
    eye = (iota((8, BLOCK), 0) == iota((8, BLOCK), 1)).astype(jnp.bfloat16)
    fields = dot(eye, got[:, 3 * L :], NT)
    live = fields[2:3, :] > 0.5
    at_station = jnp.where(
        (iota((stations, total), 0) == fields[0:1, :].astype(jnp.int32)) & live, 1.0, 0.0
    )
    before = (iota((total, total), 0) < iota((total, total), 1)).astype(jnp.bfloat16)
    rank = dot(at_station.astype(jnp.bfloat16), before)
    chunks = jnp.floor((jnp.sum(at_station, axis=1, keepdims=True) + (CHUNK - 1)) / CHUNK)
    earlier = (iota((stations, stations), 1) < iota((stations, stations), 0)).astype(jnp.bfloat16)
    start = dot(earlier, jnp.broadcast_to(chunks, (stations, BLOCK)).astype(jnp.bfloat16))[:, 0:1]
    place = jnp.sum(at_station * (start * CHUNK + rank), axis=0, keepdims=True).astype(jnp.int32)
    place = jnp.where(live, place, -1)
    pick = (iota((room, total), 0) == place).astype(jnp.bfloat16)
    kind = iota((8, total), 0)
    late = fields[3:4, :] > HALF - 0.5
    source = iota((1, total), 1) // ROWS
    turn = jnp.where(late, fields[3:4, :] - HALF, fields[3:4, :]).astype(jnp.int32)
    target = ((jnp.where(late, width, 0) + source) * 4 + turn).astype(jnp.float32)
    rows = jnp.where(kind == 3, target, jnp.where(kind < 3, fields, 0.0)).astype(jnp.bfloat16)
    table = dot(rows, pick, NT)
    over = jnp.max(fields[4:5, :])
    kind = iota((8, room), 0)
    table = jnp.where((kind == 3) & (table[2:3, :] < 0.5), float(held_ref.shape[0] - 1), table)
    table = jnp.where(kind == 4, jnp.sum(chunks), jnp.where(kind == 5, over, table))
    order_ref[...] = table.astype(jnp.int32)
    copy = pltpu.make_async_copy(order_ref, table_ref, sem)
    copy.start()
    flag_ref[...] = jnp.full(flag_ref.shape, over, jnp.float32).astype(jnp.int32)
    sorted_ref[...] = dot(pick, pieces)
    blank = jnp.zeros((PHASES, WIDE), jnp.float32)

    @pl.loop(0, jnp.where(over > 0.5, width, width // 2))
    def _(i):
        for r in (0, 1, 2, 4, 5, 6):
            held_ref[8 * i + r] = blank

    copy.wait()

    def arrive(s, carry):
        pltpu.make_async_copy(xs_hbm.at[s], xs_ref.at[s], xs_sems.at[s]).wait()
        return carry

    sub = iota((PHASES, BLOCK), 0)
    lane = iota((PHASES, BLOCK), 1)
    late = lane >= sub

    def toeplitz(slot):
        bands = []
        for k in range(CHUNK):
            tail = jnp.zeros((PHASES, BLOCK), jnp.float32)
            band = []
            for c in range(3):
                turned = []
                for h in range(2):
                    at = c * L + h * BLOCK
                    row = jnp.broadcast_to(slot[k : k + 1, at : at + BLOCK], (PHASES, BLOCK))
                    turned.append(pltpu.roll(row, 0, 1, stride=1, stride_axis=0))
                band.append(jnp.where(late, turned[0], 0.0).astype(jnp.bfloat16))
                band.append(jnp.where(late, turned[1], turned[0]).astype(jnp.bfloat16))
                rest = jnp.where(late, 0.0, turned[1])
                tail = tail + (rest if c == 0 else pltpu.roll(rest, c * PHASES, 1))
            band.append(tail.astype(jnp.bfloat16))
            bands.append(jnp.concatenate(band, axis=1))
        return jnp.concatenate(bands, axis=0)

    def chunk(i):
        first = pl.multiple_of(i * CHUNK, CHUNK)
        s = table_ref[0, first]
        slot = sorted_ref[pl.ds(first, CHUNK), :]
        mean = jnp.sum(slot * slot, axis=1, keepdims=True) / (3.0 * L)
        unit = 1.0 / jnp.sqrt(mean + EPS)
        corr = dot(toeplitz(slot), xs_ref[s])
        parts = [xs_ref[s, INV + i * PHASES : INV + (i + 1) * PHASES, :].astype(jnp.float32) for i in range(3)]
        inv = (parts[2] + parts[1]) + parts[0]
        for k in range(CHUNK):
            y = corr[k * PHASES : (k + 1) * PHASES] * (inv * unit[k : k + 1, :])
            move = table_ref[1, first + k] * (BLOCK // PHASES)
            turned = [
                pltpu.roll(y[:, b * BLOCK : (b + 1) * BLOCK], (BLOCK - move) % BLOCK, 1) for b in range(3)
            ]
            stay = lane < BLOCK - move
            target = table_ref[3, first + k]
            held_ref[target, :, :BLOCK] += jnp.where(stay, turned[0], turned[1])
            held_ref[target, :, BLOCK : 2 * BLOCK] += jnp.where(stay, turned[1], turned[2])
            held_ref[target, :, 2 * BLOCK :] += turned[2]

    def two_chunks(i, ready):
        last = jnp.maximum(table_ref[0, 16 * i], table_ref[0, 16 * i + 8]) + 1
        lax.fori_loop(ready, last, arrive, 0)
        chunk(2 * i)
        chunk(2 * i + 1)
        return jnp.maximum(ready, last)

    ready = lax.fori_loop(0, (table_ref[4, 0] + 1) // 2, two_chunks, 0)
    lax.fori_loop(ready, stations, arrive, 0)
    end = KEPT - 2 * BLOCK

    def finish(ref, o, at):
        last = jnp.zeros((PHASES, BLOCK), jnp.float32)
        for r in range(HALF):
            y = held_ref[at * 4 + r]
            a, b = y[:, :BLOCK], y[:, BLOCK : 2 * BLOCK]
            c = jnp.where(lane < end, y[:, 2 * BLOCK :], 0.0)
            top = jnp.maximum(jnp.maximum(jnp.abs(a), jnp.abs(b)), jnp.abs(c))
            top = jnp.maximum(jnp.max(top, axis=1, keepdims=True), 2.0**-110)
            power = jnp.ceil(FINE * jnp.log2(jnp.broadcast_to(top, (PHASES, BLOCK))))
            scale = FULL * jnp.exp2(power * (-1.0 / FINE))
            ref[o, 2 * r] = jnp.round(a * scale).astype(jnp.int32).astype(jnp.int16)
            ref[o, 2 * r + 1] = jnp.round(b * scale).astype(jnp.int32).astype(jnp.int16)
            c = jnp.round(c * scale)
            last = last + (c if r == 0 else pltpu.roll(c, end * r, 1))
            last = jnp.where(lane == HALF * end + r, power, last)
        ref[o, 2 * HALF] = last.astype(jnp.int32).astype(jnp.int16)

    @pl.loop(0, width // 4)
    def _(i):
        for r in range(4):
            finish(out_ref, 4 * i + r, 4 * i + r)

    @pl.when(table_ref[5, 0] > 0)
    def _():
        @pl.loop(0, width)
        def _(o):
            finish(more_ref, o, width + o)


def add_kernel(list_ref, count_ref, back_ref, stack_ref, best_ref, scale_ref, tail_ref):
    end = KEPT - 2 * BLOCK

    def wide(x):
        return x.astype(jnp.int32).astype(jnp.float32)

    @pl.loop(0, back_ref.shape[0] // 4)
    def _(i):
        for part in range(4):
            o = 4 * i + part
            last = wide(back_ref[o, 2 * HALF])
            scales = jnp.exp2(last * (1.0 / FINE)) * (1.0 / FULL)
            for r in range(HALF):
                at = HALF * end + r
                scale_ref[o * 4 + r] = jnp.broadcast_to(scales[:, at : at + 1], (PHASES, BLOCK))
                tail_ref[o * 4 + r] = last if r == 0 else pltpu.roll(last, BLOCK - end * r, 1)

    def one_template(t, best):
        count = count_ref[t]
        number = list_ref[t, BLOCK - 1]

        def four_traces(g, total):
            for i in range(4):
                entry = list_ref[t, 4 * g + i]
                o = entry // 4
                r = entry % 4
                scale = jnp.where(4 * g + i < number, scale_ref[entry], 0.0)
                parts = (wide(back_ref[o, 2 * r]), wide(back_ref[o, 2 * r + 1]), tail_ref[entry])
                total = tuple(a + p * scale for a, p in zip(total, parts))
            return total

        zero = jnp.zeros((PHASES, BLOCK), jnp.float32)
        total = lax.fori_loop(0, (number + 3) // 4, four_traces, (zero, zero, zero))
        factor = jnp.sqrt(3.0 * L / jnp.full((1, 1), count, jnp.int32).astype(jnp.float32))
        whole = jnp.concatenate(total, axis=1) * factor
        stack_ref[t] = whole[:, :KEPT]
        return jnp.maximum(best, whole)

    start = jnp.full((PHASES, WIDE), -jnp.inf, jnp.float32)
    best = lax.fori_loop(0, stack_ref.shape[0], one_template, start)
    best_ref[...] = best[:, :KEPT]


VMEM = pl.BlockSpec(memory_space=pltpu.VMEM)
ANY = pl.BlockSpec(memory_space=pl.ANY)
SMEM = pl.BlockSpec(memory_space=pltpu.SMEM)


def params(mib):
    return pltpu.CompilerParams(vmem_limit_bytes=mib * 2**20)


def correlate_call(got, xs, stations):
    width = got.shape[0]
    room = 8 * (width * CAP // CHUNK + stations)
    return pl.pallas_call(
        correlate_kernel,
        out_shape=(
            jax.ShapeDtypeStruct((width, BLOCKS, PHASES, BLOCK), jnp.int16),
            jax.ShapeDtypeStruct((width, BLOCKS, PHASES, BLOCK), jnp.int16),
            jax.ShapeDtypeStruct((1, BLOCK), jnp.int32),
        ),
        in_specs=[VMEM, ANY],
        out_specs=(VMEM, VMEM, VMEM),
        scratch_shapes=[
            pltpu.VMEM((stations, DEPTH, WIDE), jnp.bfloat16),
            pltpu.VMEM((room, 3 * L), jnp.float32),
            pltpu.VMEM((8, room), jnp.int32),
            pltpu.VMEM((8 * width + 8, PHASES, WIDE), jnp.float32),
            pltpu.SMEM((8, room), jnp.int32),
            pltpu.SemaphoreType.DMA,
            pltpu.SemaphoreType.DMA((stations,)),
        ],
        compiler_params=params(40),
    )(got, xs)


def add_call(listed, counts, back):
    tpl_dev = counts.shape[0]
    return pl.pallas_call(
        add_kernel,
        out_shape=(
            jax.ShapeDtypeStruct((tpl_dev, PHASES, KEPT), jnp.float32),
            jax.ShapeDtypeStruct((PHASES, KEPT), jnp.float32),
        ),
        in_specs=[SMEM, SMEM, VMEM],
        out_specs=(VMEM, VMEM),
        scratch_shapes=[
            pltpu.VMEM((back.shape[0] * 4, PHASES, BLOCK), jnp.float32),
            pltpu.VMEM((back.shape[0] * 4, PHASES, BLOCK), jnp.float32),
        ],
        compiler_params=params(40),
    )(listed, counts, back)


def body(waveforms, station_home, templates, template_stations, station_counts, moveouts):
    stations, _, samples = waveforms.shape
    tpl_dev = templates.shape[0]
    width = lax.axis_size("sta")
    parts = station_home.shape[0] // BLOCK
    send, listed = pl.pallas_call(
        pack_kernel,
        out_shape=(
            jax.ShapeDtypeStruct((width, ROWS, DEPTH), jnp.bfloat16),
            jax.ShapeDtypeStruct((tpl_dev, BLOCK), jnp.int32),
        ),
        in_specs=[ANY] * 5,
        out_specs=(VMEM, VMEM),
        scratch_shapes=[
            pltpu.VMEM((tpl_dev, SLOTS), jnp.int32),
            pltpu.VMEM((tpl_dev, SLOTS), jnp.int32),
            pltpu.SMEM((tpl_dev,), jnp.int32),
            pltpu.VMEM((parts, BLOCK), jnp.int32),
            pltpu.VMEM((SLOTS, tpl_dev, 3 * L), jnp.bfloat16),
            pltpu.SemaphoreType.DMA((5,)),
        ],
        compiler_params=params(60),
    )(
        template_stations,
        moveouts,
        station_counts,
        station_home.reshape(parts, BLOCK),
        templates.transpose(1, 0, 2),
    )
    got = lax.all_to_all(send, "sta", split_axis=0, concat_axis=0, tiled=True)
    xs = pl.pallas_call(
        prep_kernel,
        out_shape=jax.ShapeDtypeStruct((2 * stations + 4, DEPTH, WIDE), jnp.bfloat16),
        in_specs=[VMEM],
        out_specs=ANY,
        scratch_shapes=[
            pltpu.VMEM((stations, DEPTH, WIDE), jnp.bfloat16),
            pltpu.VMEM((3, stations, samples), jnp.float32),
            pltpu.SemaphoreType.DMA((stations // 2,)),
        ],
        compiler_params=params(40),
        cost_estimate=pl.CostEstimate(flops=2 * 10**9, bytes_accessed=12 * 2**20, transcendentals=0),
    )(waveforms.transpose(1, 0, 2))
    traces, more, flag = correlate_call(got, xs, stations)

    def home(x):
        return lax.all_to_all(x, "sta", split_axis=0, concat_axis=0, tiled=True)

    def one_exchange(traces, more):
        return add_call(listed, station_counts, home(traces))

    def two_exchanges(traces, more):
        return add_call(listed, station_counts, jnp.concatenate([home(traces), home(more)]))

    stack, best = lax.cond(flag[0, 0] > 0, two_exchanges, one_exchange, traces, more)
    stack = stack.transpose(0, 2, 1).reshape(tpl_dev, PHASES * KEPT)
    best = best.T.reshape(PHASES * KEPT)
    network = best_of_all(best.reshape(-1, BLOCK)).reshape(PHASES * KEPT)
    return (stack, network)


def best_of_all(best):
    rounds = (("tpl", (1, 2, 3)), ("tpl", (6,)), ("sta", (1,)), ("sta", (2, 6, 4)), ("sta", (8, 24, 16)))
    for axis, steps in rounds:
        size = lax.axis_size(axis)
        others = [lax.ppermute(best, axis, [(i, i ^ step) for i in range(size)]) for step in steps]
        for other in others:
            best = jnp.maximum(best, other)
    return best


def solution(mesh):
    in_specs = (
        P("sta", None, None),
        P(),
        P(("sta", "tpl"), None, None),
        P(("sta", "tpl"), None),
        P(("sta", "tpl")),
        P(("sta", "tpl"), None),
    )
    out_specs = (P(("sta", "tpl"), None), P())
    return jax.shard_map(body, mesh=mesh, in_specs=in_specs, out_specs=out_specs, check_vma=False)
```

```python
import functools

import jax
import jax.numpy as jnp
from jax import lax
from jax.experimental import pallas as pl
from jax.experimental.pallas import tpu as pltpu
from jax.sharding import PartitionSpec as P

SLOTS = 20
L = 256
BLOCK = 128
LAG_BLOCKS = 40
MOVE_BLOCKS = 4
EPS = 1e-06

PHASES = 16
COLS = LAG_BLOCKS * BLOCK // PHASES
KEPT = (LAG_BLOCKS - MOVE_BLOCKS) * BLOCK // PHASES
WIDE = 384
REACH = L // PHASES
DEPTH = 3 * L + BLOCK
INV = 3 * L + 3 * PHASES
CHUNK = 8
CAP = 6
ROWS = 8
HALF = 3
BLOCKS = 7

FINE = 8.0
FULL = 32700.0
NT = (((1,), (1,)), ((), ()))


def iota(shape, dim):
    return lax.broadcasted_iota(jnp.int32, shape, dim)


def dot(a, b, dims=None):
    if dims is None:
        dims = (((1,), (0,)), ((), ()))
    return lax.dot_general(a, b, dims, preferred_element_type=jnp.float32)


def pack_kernel(
    stations_hbm, moves_hbm, counts_hbm, home_hbm, templates_hbm, send_ref, list_ref,
    stations_ref, moves_ref, counts_ref, home_ref, templates_ref, sems,
):
    copies = [
        pltpu.make_async_copy(src, dst, sems.at[i])
        for i, (src, dst) in enumerate(
            (
                (stations_hbm, stations_ref),
                (moves_hbm, moves_ref),
                (counts_hbm, counts_ref),
                (home_hbm, home_ref),
                (templates_hbm, templates_ref),
            )
        )
    ]
    for copy in copies:
        copy.start()
    tpl_dev, slots = stations_ref.shape
    total = tpl_dev * slots
    width = send_ref.shape[0]
    parts = home_ref.shape[0]
    sta_dev = parts * BLOCK // width
    place = iota((1, total), 1)
    of_template = place % tpl_dev
    for copy in copies[:4]:
        copy.wait()
    stations = stations_ref[...]
    high = stations // 16
    fields = jnp.concatenate([high, stations - 16 * high, moves_ref[...]], axis=0)
    expand = (iota((slots, total), 1) // tpl_dev == iota((slots, total), 0)).astype(jnp.bfloat16)
    spread = dot(fields.astype(jnp.float32).astype(jnp.bfloat16), expand)
    mine = iota((tpl_dev, total), 0) == of_template
    rows = [
        jnp.sum(jnp.where(mine, spread[i * tpl_dev : (i + 1) * tpl_dev], 0.0), axis=0, keepdims=True)
        for i in range(3)
    ]
    station = (rows[0] * 16.0 + rows[1]).astype(jnp.int32)
    moves = rows[2]
    counts = jnp.zeros((1, total), jnp.int32)
    for t in range(tpl_dev):
        counts = jnp.where(of_template == t, counts_ref[t], counts)
    home = home_ref[...]
    owners = home // sta_dev
    table = jnp.concatenate([owners, home - owners * sta_dev], axis=0)
    hit = (iota((BLOCK, total), 0) == station % BLOCK).astype(jnp.bfloat16)
    found = dot(table.astype(jnp.float32).astype(jnp.bfloat16), hit)
    part = iota((parts, total), 0) == station // BLOCK
    owner = jnp.sum(jnp.where(part, found[:parts], 0.0), axis=0, keepdims=True).astype(jnp.int32)
    local = jnp.sum(jnp.where(part, found[parts:], 0.0), axis=0, keepdims=True)
    live = place // tpl_dev < counts
    before = (iota((total, total), 0) < iota((total, total), 1)).astype(jnp.bfloat16)
    pairs = width * tpl_dev
    of_pair = jnp.where((iota((pairs, total), 0) == owner * tpl_dev + of_template) & live, 1.0, 0.0)
    earlier = jnp.sum(of_pair * dot(of_pair.astype(jnp.bfloat16), before), axis=0, keepdims=True)
    first = live & (earlier < 0.5)
    present = jnp.minimum(jnp.sum(of_pair, axis=1, keepdims=True), 1.0)
    row, col = iota((pairs, pairs), 0), iota((pairs, pairs), 1)
    lower = ((row // tpl_dev == col // tpl_dev) & (col < row)).astype(jnp.bfloat16)
    order = dot(lower, jnp.broadcast_to(present, (pairs, BLOCK)).astype(jnp.bfloat16))[:, 0:1]
    turn = jnp.sum(of_pair * order, axis=0, keepdims=True)
    over = jnp.max(jnp.where(live & (turn > HALF - 0.5), 1.0, 0.0))
    late = turn > HALF - 0.5
    home_of = (jnp.where(late, width, 0) + owner) * 4 + jnp.where(late, turn - HALF, turn).astype(jnp.int32)
    own_first = jnp.where((iota((tpl_dev, total), 0) == of_template) & first, 1.0, 0.0)
    nth = dot(own_first.astype(jnp.bfloat16), before)
    nth = jnp.sum(own_first * nth, axis=0, keepdims=True).astype(jnp.int32)
    entry = (iota((BLOCK, total), 0) == nth).astype(jnp.bfloat16)
    listed = dot((own_first * home_of.astype(jnp.float32)).astype(jnp.bfloat16), entry, NT)
    number = jnp.sum(own_first, axis=1, keepdims=True)
    list_ref[...] = jnp.where(iota((tpl_dev, BLOCK), 1) == BLOCK - 1, number, listed).astype(jnp.int32)
    at_owner = jnp.where((iota((width, total), 0) == owner) & live, 1.0, 0.0)
    rank = jnp.sum(at_owner * dot(at_owner.astype(jnp.bfloat16), before), axis=0, keepdims=True)
    dest = jnp.where(live, owner * ROWS + rank.astype(jnp.int32), -1)
    pick = (iota((width * ROWS, total), 0) == dest).astype(jnp.bfloat16)
    kind = iota((BLOCK, total), 0)
    fields = jnp.where(kind == 0, local, jnp.where(kind == 1, moves, jnp.where(kind == 2, 1.0, 0.0)))
    fields = jnp.where(kind == 3, turn, fields).astype(jnp.bfloat16)
    tail = dot(pick, fields, NT)
    tail = jnp.where(iota(tail.shape, 1) == 4, over, tail).astype(jnp.bfloat16)
    copies[4].wait()
    send = dot(pick, templates_ref[...].reshape(total, 3 * L)).astype(jnp.bfloat16)
    send_ref[:, :, : 3 * L] = send.reshape(width, ROWS, 3 * L)
    send_ref[:, :, 3 * L :] = tail.reshape(width, ROWS, BLOCK)


def prep_kernel(wave_ref, xs_hbm, xs_ref, wide_ref, sems):
    tiles = wave_ref.shape[2] // BLOCK
    wide_ref[...] = wave_ref[...].astype(jnp.float32)
    lane = iota((8, BLOCK), 1)
    own = (lane // PHASES == iota((8, BLOCK), 0)).astype(jnp.float32)
    spread = (
        (iota((3 * PHASES, 3 * BLOCK), 1) // BLOCK == iota((3 * PHASES, 3 * BLOCK), 0) // PHASES)
        & (iota((3 * PHASES, 3 * BLOCK), 1) % PHASES == iota((3 * PHASES, 3 * BLOCK), 0) % PHASES)
    ).astype(jnp.bfloat16)
    sub = iota((PHASES, WIDE), 0)

    def one_station(s):
        comps = []
        for c in range(3):
            parts = []
            group = wide_ref[c, pl.ds(pl.multiple_of(s // 8 * 8, 8), 8), :]
            line = pltpu.roll(group, (8 - s % 8) % 8, 0)[0:1, :]
            for r in range(tiles):
                row = line[:, r * BLOCK : (r + 1) * BLOCK]
                parts.append(jnp.broadcast_to(row, (8, BLOCK)) * own)
            parts.append(jnp.zeros((WIDE - 8 * tiles, BLOCK), jnp.float32))
            comps.append(jnp.concatenate(parts, axis=0).astype(jnp.bfloat16))
        grid = jnp.concatenate(comps, axis=1)
        phases = dot(spread, grid, NT)
        squares = jnp.zeros((PHASES, WIDE), jnp.float32)
        for c in range(3):
            x = phases[c * PHASES : (c + 1) * PHASES]
            squares = squares + x * x
            for r in range(REACH + 1):
                moved = x if r == 0 else pltpu.roll(x, WIDE - r, 1)
                at = (c * (REACH + 1) + r) * PHASES
                xs_ref[s, at : at + PHASES, :] = moved.astype(jnp.bfloat16)
        up = squares
        down = jnp.where(sub >= 1, pltpu.roll(squares, 1, 0), 0.0)
        for step in (1, 2, 4, 8):
            up = up + jnp.where(sub < PHASES - step, pltpu.roll(up, PHASES - step, 0), 0.0)
            down = down + jnp.where(sub >= step, pltpu.roll(down, step, 0), 0.0)
        whole = jnp.broadcast_to(up[0:1, :], (PHASES, WIDE))
        two = whole + pltpu.roll(whole, WIDE - 1, 1)
        four = two + pltpu.roll(two, WIDE - 2, 1)
        eight = four + pltpu.roll(four, WIDE - 4, 1)
        fifteen = (
            pltpu.roll(eight, WIDE - 1, 1)
            + pltpu.roll(four, WIDE - 9, 1)
            + pltpu.roll(two, WIDE - 13, 1)
            + pltpu.roll(whole, WIDE - 15, 1)
        )
        power = (up + fifteen + pltpu.roll(down, WIDE - REACH, 1)) / (3.0 * L)
        inv = 1.0 / (3.0 * L * jnp.sqrt(power + EPS))
        for i in range(3):
            term = inv.astype(jnp.bfloat16)
            xs_ref[s, INV + i * PHASES : INV + (i + 1) * PHASES, :] = term
            inv = inv - term.astype(jnp.float32)
        xs_ref[s, INV + 3 * PHASES :, :] = jnp.zeros((DEPTH - INV - 3 * PHASES, WIDE), jnp.bfloat16)

    @pl.loop(0, wave_ref.shape[1] // 2)
    def _(i):
        one_station(2 * i)
        one_station(2 * i + 1)
        pair = pl.ds(2 * i, 2)
        pltpu.make_async_copy(xs_ref.at[pair], xs_hbm.at[pair], sems.at[i]).start()

    @pl.loop(0, wave_ref.shape[1] // 2)
    def _(i):
        pair = pl.ds(2 * i, 2)
        pltpu.make_async_copy(xs_ref.at[pair], xs_hbm.at[pair], sems.at[i]).wait()


def correlate_kernel(
    got_ref, xs_hbm, out_ref, more_ref, flag_ref, xs_ref, sorted_ref, order_ref, held_ref, table_ref, sem, xs_sems
):
    width = got_ref.shape[0]
    stations = xs_ref.shape[0]
    total = width * ROWS
    room = sorted_ref.shape[0]
    loads = [pltpu.make_async_copy(xs_hbm.at[s], xs_ref.at[s], xs_sems.at[s]) for s in range(stations)]
    for load in loads:
        load.start()
    got = got_ref[...].reshape(total, DEPTH)
    pieces = got[:, : 3 * L]
    eye = (iota((8, BLOCK), 0) == iota((8, BLOCK), 1)).astype(jnp.bfloat16)
    fields = dot(eye, got[:, 3 * L :], NT)
    live = fields[2:3, :] > 0.5
    at_station = jnp.where(
        (iota((stations, total), 0) == fields[0:1, :].astype(jnp.int32)) & live, 1.0, 0.0
    )
    before = (iota((total, total), 0) < iota((total, total), 1)).astype(jnp.bfloat16)
    rank = dot(at_station.astype(jnp.bfloat16), before)
    chunks = jnp.floor((jnp.sum(at_station, axis=1, keepdims=True) + (CHUNK - 1)) / CHUNK)
    earlier = (iota((stations, stations), 1) < iota((stations, stations), 0)).astype(jnp.bfloat16)
    start = dot(earlier, jnp.broadcast_to(chunks, (stations, BLOCK)).astype(jnp.bfloat16))[:, 0:1]
    place = jnp.sum(at_station * (start * CHUNK + rank), axis=0, keepdims=True).astype(jnp.int32)
    place = jnp.where(live, place, -1)
    pick = (iota((room, total), 0) == place).astype(jnp.bfloat16)
    kind = iota((8, total), 0)
    late = fields[3:4, :] > HALF - 0.5
    source = iota((1, total), 1) // ROWS
    turn = jnp.where(late, fields[3:4, :] - HALF, fields[3:4, :]).astype(jnp.int32)
    target = ((jnp.where(late, width, 0) + source) * 4 + turn).astype(jnp.float32)
    rows = jnp.where(kind == 3, target, jnp.where(kind < 3, fields, 0.0)).astype(jnp.bfloat16)
    table = dot(rows, pick, NT)
    over = jnp.max(fields[4:5, :])
    kind = iota((8, room), 0)
    table = jnp.where((kind == 3) & (table[2:3, :] < 0.5), float(held_ref.shape[0] - 1), table)
    table = jnp.where(kind == 4, jnp.sum(chunks), jnp.where(kind == 5, over, table))
    order_ref[...] = table.astype(jnp.int32)
    copy = pltpu.make_async_copy(order_ref, table_ref, sem)
    copy.start()
    flag_ref[...] = jnp.full(flag_ref.shape, over, jnp.float32).astype(jnp.int32)
    sorted_ref[...] = dot(pick, pieces)
    blank = jnp.zeros((PHASES, WIDE), jnp.float32)

    @pl.loop(0, jnp.where(over > 0.5, width, width // 2))
    def _(i):
        for r in (0, 1, 2, 4, 5, 6):
            held_ref[8 * i + r] = blank

    copy.wait()

    def arrive(s, carry):
        pltpu.make_async_copy(xs_hbm.at[s], xs_ref.at[s], xs_sems.at[s]).wait()
        return carry

    sub = iota((PHASES, BLOCK), 0)
    lane = iota((PHASES, BLOCK), 1)
    own = [lane >= PHASES * c + sub for c in range(3)]

    def toeplitz(slot):
        bands = []
        for k in range(CHUNK):
            band = []
            before = None
            for c in range(3):
                turned = []
                for h in range(2):
                    at = c * L + h * BLOCK
                    row = jnp.broadcast_to(slot[k : k + 1, at : at + BLOCK], (PHASES, BLOCK))
                    turned.append(pltpu.roll(row, c * PHASES, 1, stride=1, stride_axis=0))
                rest = 0.0 if c == 0 else jnp.where(own[c - 1], 0.0, before)
                band.append(jnp.where(own[c], turned[0], rest).astype(jnp.bfloat16))
                band.append(jnp.where(own[c], turned[1], turned[0]).astype(jnp.bfloat16))
                before = turned[1]
            band.append(jnp.where(own[2], 0.0, before).astype(jnp.bfloat16))
            bands.append(jnp.concatenate(band, axis=1))
        return jnp.concatenate(bands, axis=0)

    def chunk(i):
        first = pl.multiple_of(i * CHUNK, CHUNK)
        s = table_ref[0, first]
        slot = sorted_ref[pl.ds(first, CHUNK), :]
        mean = jnp.sum(slot * slot, axis=1, keepdims=True) / (3.0 * L)
        unit = 1.0 / jnp.sqrt(mean + EPS)
        corr = dot(toeplitz(slot), xs_ref[s])
        parts = [xs_ref[s, INV + i * PHASES : INV + (i + 1) * PHASES, :].astype(jnp.float32) for i in range(3)]
        inv = (parts[2] + parts[1]) + parts[0]
        for k in range(CHUNK):
            y = corr[k * PHASES : (k + 1) * PHASES] * (inv * unit[k : k + 1, :])
            move = table_ref[1, first + k] * (BLOCK // PHASES)
            turned = [
                pltpu.roll(y[:, b * BLOCK : (b + 1) * BLOCK], (BLOCK - move) % BLOCK, 1) for b in range(3)
            ]
            stay = lane < BLOCK - move
            target = table_ref[3, first + k]
            held_ref[target, :, :BLOCK] += jnp.where(stay, turned[0], turned[1])
            held_ref[target, :, BLOCK : 2 * BLOCK] += jnp.where(stay, turned[1], turned[2])
            held_ref[target, :, 2 * BLOCK :] += turned[2]

    def three_chunks(i, ready):
        last = table_ref[0, 3 * CHUNK * i]
        for k in range(1, 3):
            last = jnp.maximum(last, table_ref[0, (3 * i + k) * CHUNK])
        lax.fori_loop(ready, last + 1, arrive, 0)
        for k in range(3):
            chunk(3 * i + k)
        return jnp.maximum(ready, last + 1)

    ready = lax.fori_loop(0, (table_ref[4, 0] + 2) // 3, three_chunks, 0)
    lax.fori_loop(ready, stations, arrive, 0)
    end = KEPT - 2 * BLOCK

    def finish(ref, o, at):
        last = jnp.zeros((PHASES, BLOCK), jnp.float32)
        for r in range(HALF):
            y = held_ref[at * 4 + r]
            a, b = y[:, :BLOCK], y[:, BLOCK : 2 * BLOCK]
            c = jnp.where(lane < end, y[:, 2 * BLOCK :], 0.0)
            top = jnp.maximum(jnp.maximum(jnp.abs(a), jnp.abs(b)), jnp.abs(c))
            top = jnp.maximum(jnp.max(top, axis=1, keepdims=True), 2.0**-110)
            power = jnp.ceil(FINE * jnp.log2(jnp.broadcast_to(top, (PHASES, BLOCK))))
            scale = FULL * jnp.exp2(power * (-1.0 / FINE))
            ref[o, 2 * r] = jnp.round(a * scale).astype(jnp.int32).astype(jnp.int16)
            ref[o, 2 * r + 1] = jnp.round(b * scale).astype(jnp.int32).astype(jnp.int16)
            c = jnp.round(c * scale)
            last = last + (c if r == 0 else pltpu.roll(c, end * r, 1))
            last = jnp.where(lane == HALF * end + r, power, last)
        ref[o, 2 * HALF] = last.astype(jnp.int32).astype(jnp.int16)

    @pl.loop(0, width // 4)
    def _(i):
        for r in range(4):
            finish(out_ref, 4 * i + r, 4 * i + r)

    @pl.when(table_ref[5, 0] > 0)
    def _():
        @pl.loop(0, width)
        def _(o):
            finish(more_ref, o, width + o)


def add_kernel(list_ref, count_ref, back_ref, stack_ref, best_ref, scale_ref, tail_ref):
    end = KEPT - 2 * BLOCK

    def wide(x):
        return x.astype(jnp.int32).astype(jnp.float32)

    @pl.loop(0, back_ref.shape[0] // 4)
    def _(i):
        for part in range(4):
            o = 4 * i + part
            last = wide(back_ref[o, 2 * HALF])
            scales = jnp.exp2(last * (1.0 / FINE)) * (1.0 / FULL)
            for r in range(HALF):
                at = HALF * end + r
                scale_ref[o * 4 + r] = jnp.broadcast_to(scales[:, at : at + 1], (PHASES, BLOCK))
                tail_ref[o * 4 + r] = last if r == 0 else pltpu.roll(last, BLOCK - end * r, 1)

    def one_template(t, best):
        count = count_ref[t]
        number = list_ref[t, BLOCK - 1]

        def four_traces(g, total):
            for i in range(4):
                entry = list_ref[t, 4 * g + i]
                o = entry // 4
                r = entry % 4
                scale = jnp.where(4 * g + i < number, scale_ref[entry], 0.0)
                parts = (wide(back_ref[o, 2 * r]), wide(back_ref[o, 2 * r + 1]), tail_ref[entry])
                total = tuple(a + p * scale for a, p in zip(total, parts))
            return total

        zero = jnp.zeros((PHASES, BLOCK), jnp.float32)
        total = lax.fori_loop(0, (number + 3) // 4, four_traces, (zero, zero, zero))
        factor = jnp.sqrt(3.0 * L / jnp.full((1, 1), count, jnp.int32).astype(jnp.float32))
        whole = jnp.concatenate(total, axis=1) * factor
        stack_ref[t] = whole[:, :KEPT]
        return jnp.maximum(best, whole)

    start = jnp.full((PHASES, WIDE), -jnp.inf, jnp.float32)
    best = lax.fori_loop(0, stack_ref.shape[0], one_template, start)
    best_ref[...] = best[:, :KEPT]


VMEM = pl.BlockSpec(memory_space=pltpu.VMEM)
ANY = pl.BlockSpec(memory_space=pl.ANY)
SMEM = pl.BlockSpec(memory_space=pltpu.SMEM)


def params(mib):
    return pltpu.CompilerParams(vmem_limit_bytes=mib * 2**20)


def prep_call(waveforms):
    stations, _, samples = waveforms.shape
    return pl.pallas_call(
        prep_kernel,
        out_shape=jax.ShapeDtypeStruct((2 * stations + 4, DEPTH, WIDE), jnp.bfloat16),
        in_specs=[VMEM],
        out_specs=ANY,
        scratch_shapes=[
            pltpu.VMEM((stations, DEPTH, WIDE), jnp.bfloat16),
            pltpu.VMEM((3, stations, samples), jnp.float32),
            pltpu.SemaphoreType.DMA((stations // 2,)),
        ],
        compiler_params=params(40),
        cost_estimate=pl.CostEstimate(flops=2 * 10**9, bytes_accessed=12 * 2**20, transcendentals=0),
    )(waveforms.transpose(1, 0, 2))


def correlate_call(got, xs, stations):
    width = got.shape[0]
    room = 8 * (width * CAP // CHUNK + stations)
    return pl.pallas_call(
        correlate_kernel,
        out_shape=(
            jax.ShapeDtypeStruct((width, BLOCKS, PHASES, BLOCK), jnp.int16),
            jax.ShapeDtypeStruct((width, BLOCKS, PHASES, BLOCK), jnp.int16),
            jax.ShapeDtypeStruct((1, BLOCK), jnp.int32),
        ),
        in_specs=[VMEM, ANY],
        out_specs=(VMEM, VMEM, VMEM),
        scratch_shapes=[
            pltpu.VMEM((stations, DEPTH, WIDE), jnp.bfloat16),
            pltpu.VMEM((room, 3 * L), jnp.float32),
            pltpu.VMEM((8, room), jnp.int32),
            pltpu.VMEM((8 * width + 8, PHASES, WIDE), jnp.float32),
            pltpu.SMEM((8, room), jnp.int32),
            pltpu.SemaphoreType.DMA,
            pltpu.SemaphoreType.DMA((stations,)),
        ],
        compiler_params=params(40),
    )(got, xs)


def add_call(listed, counts, back):
    tpl_dev = counts.shape[0]
    return pl.pallas_call(
        add_kernel,
        out_shape=(
            jax.ShapeDtypeStruct((tpl_dev, PHASES, KEPT), jnp.float32),
            jax.ShapeDtypeStruct((PHASES, KEPT), jnp.float32),
        ),
        in_specs=[SMEM, SMEM, VMEM],
        out_specs=(VMEM, VMEM),
        scratch_shapes=[
            pltpu.VMEM((back.shape[0] * 4, PHASES, BLOCK), jnp.float32),
            pltpu.VMEM((back.shape[0] * 4, PHASES, BLOCK), jnp.float32),
        ],
        compiler_params=params(40),
    )(listed, counts, back)


def body(waveforms, station_home, templates, template_stations, station_counts, moveouts):
    stations, _, samples = waveforms.shape
    tpl_dev = templates.shape[0]
    width = lax.axis_size("sta")
    parts = station_home.shape[0] // BLOCK
    send, listed = pl.pallas_call(
        pack_kernel,
        out_shape=(
            jax.ShapeDtypeStruct((width, ROWS, DEPTH), jnp.bfloat16),
            jax.ShapeDtypeStruct((tpl_dev, BLOCK), jnp.int32),
        ),
        in_specs=[ANY] * 5,
        out_specs=(VMEM, VMEM),
        scratch_shapes=[
            pltpu.VMEM((tpl_dev, SLOTS), jnp.int32),
            pltpu.VMEM((tpl_dev, SLOTS), jnp.int32),
            pltpu.SMEM((tpl_dev,), jnp.int32),
            pltpu.VMEM((parts, BLOCK), jnp.int32),
            pltpu.VMEM((SLOTS, tpl_dev, 3 * L), jnp.bfloat16),
            pltpu.SemaphoreType.DMA((5,)),
        ],
        compiler_params=params(60),
    )(
        template_stations,
        moveouts,
        station_counts,
        station_home.reshape(parts, BLOCK),
        templates.transpose(1, 0, 2),
    )
    got = lax.all_to_all(send, "sta", split_axis=0, concat_axis=0, tiled=True)
    xs = prep_call(waveforms)
    traces, more, flag = correlate_call(got, xs, stations)

    def home(x):
        return lax.all_to_all(x, "sta", split_axis=0, concat_axis=0, tiled=True)

    def one_exchange(traces, more):
        return add_call(listed, station_counts, home(traces))

    def two_exchanges(traces, more):
        return add_call(listed, station_counts, jnp.concatenate([home(traces), home(more)]))

    stack, best = lax.cond(flag[0, 0] > 0, two_exchanges, one_exchange, traces, more)
    best = best.T.reshape(-1, BLOCK)
    for n, (axis, steps) in enumerate(ROUNDS):
        size = lax.axis_size(axis)
        others = [lax.ppermute(best, axis, [(i, i ^ step) for i in range(size)]) for step in steps]
        for other in others:
            best = jnp.maximum(best, other)
        if n == 0:
            best, stack = lax.optimization_barrier((best, stack))
            stack = stack.transpose(0, 2, 1).reshape(tpl_dev, PHASES * KEPT)
        if n == 1:
            best, stack = lax.optimization_barrier((best, stack))
    return (stack, best.reshape(PHASES * KEPT))


ROUNDS = (("tpl", (1, 2, 3)), ("tpl", (6,)), ("sta", (1,)), ("sta", (2, 6, 4)), ("sta", (8, 24, 16)))


def solution(mesh):
    in_specs = (
        P("sta", None, None),
        P(),
        P(("sta", "tpl"), None, None),
        P(("sta", "tpl"), None),
        P(("sta", "tpl")),
        P(("sta", "tpl"), None),
    )
    out_specs = (P(("sta", "tpl"), None), P())
    return jax.shard_map(body, mesh=mesh, in_specs=in_specs, out_specs=out_specs, check_vma=False)
```

```python
import functools

import jax
import jax.numpy as jnp
from jax import lax
from jax.experimental import pallas as pl
from jax.experimental.pallas import tpu as pltpu
from jax.sharding import PartitionSpec as P

SLOTS = 20
L = 256
BLOCK = 128
LAG_BLOCKS = 40
MOVE_BLOCKS = 4
EPS = 1e-06

PHASES = 16
COLS = LAG_BLOCKS * BLOCK // PHASES
KEPT = (LAG_BLOCKS - MOVE_BLOCKS) * BLOCK // PHASES
WIDE = 384
REACH = L // PHASES
DEPTH = 3 * L + BLOCK
INV = 3 * L + 3 * PHASES
CHUNK = 8
CAP = 6
ROWS = 8
HALF = 3
BLOCKS = 7

FINE = 8.0
FULL = 32700.0
NT = (((1,), (1,)), ((), ()))


def iota(shape, dim):
    return lax.broadcasted_iota(jnp.int32, shape, dim)


def dot(a, b, dims=None):
    if dims is None:
        dims = (((1,), (0,)), ((), ()))
    return lax.dot_general(a, b, dims, preferred_element_type=jnp.float32)


def pack_kernel(
    stations_hbm, moves_hbm, counts_hbm, home_hbm, templates_hbm, send_ref, list_ref,
    stations_ref, moves_ref, counts_ref, home_ref, templates_ref, sems,
):
    copies = [
        pltpu.make_async_copy(src, dst, sems.at[i])
        for i, (src, dst) in enumerate(
            (
                (stations_hbm, stations_ref),
                (moves_hbm, moves_ref),
                (counts_hbm, counts_ref),
                (home_hbm, home_ref),
                (templates_hbm, templates_ref),
            )
        )
    ]
    for copy in copies:
        copy.start()
    tpl_dev, slots = stations_ref.shape
    total = tpl_dev * slots
    width = send_ref.shape[0]
    parts = home_ref.shape[0]
    sta_dev = parts * BLOCK // width
    place = iota((1, total), 1)
    of_template = place % tpl_dev
    for copy in copies[:4]:
        copy.wait()
    stations = stations_ref[...]
    high = stations // 16
    fields = jnp.concatenate([high, stations - 16 * high, moves_ref[...]], axis=0)
    expand = (iota((slots, total), 1) // tpl_dev == iota((slots, total), 0)).astype(jnp.bfloat16)
    spread = dot(fields.astype(jnp.float32).astype(jnp.bfloat16), expand)
    mine = iota((tpl_dev, total), 0) == of_template
    rows = [
        jnp.sum(jnp.where(mine, spread[i * tpl_dev : (i + 1) * tpl_dev], 0.0), axis=0, keepdims=True)
        for i in range(3)
    ]
    station = (rows[0] * 16.0 + rows[1]).astype(jnp.int32)
    moves = rows[2]
    counts = jnp.zeros((1, total), jnp.int32)
    for t in range(tpl_dev):
        counts = jnp.where(of_template == t, counts_ref[t], counts)
    home = home_ref[...]
    owners = home // sta_dev
    table = jnp.concatenate([owners, home - owners * sta_dev], axis=0)
    hit = (iota((BLOCK, total), 0) == station % BLOCK).astype(jnp.bfloat16)
    found = dot(table.astype(jnp.float32).astype(jnp.bfloat16), hit)
    part = iota((parts, total), 0) == station // BLOCK
    owner = jnp.sum(jnp.where(part, found[:parts], 0.0), axis=0, keepdims=True).astype(jnp.int32)
    local = jnp.sum(jnp.where(part, found[parts:], 0.0), axis=0, keepdims=True)
    live = place // tpl_dev < counts
    before = (iota((total, total), 0) < iota((total, total), 1)).astype(jnp.bfloat16)
    pairs = width * tpl_dev
    of_pair = jnp.where((iota((pairs, total), 0) == owner * tpl_dev + of_template) & live, 1.0, 0.0)
    earlier = jnp.sum(of_pair * dot(of_pair.astype(jnp.bfloat16), before), axis=0, keepdims=True)
    first = live & (earlier < 0.5)
    present = jnp.minimum(jnp.sum(of_pair, axis=1, keepdims=True), 1.0)
    row, col = iota((pairs, pairs), 0), iota((pairs, pairs), 1)
    lower = ((row // tpl_dev == col // tpl_dev) & (col < row)).astype(jnp.bfloat16)
    order = dot(lower, jnp.broadcast_to(present, (pairs, BLOCK)).astype(jnp.bfloat16))[:, 0:1]
    turn = jnp.sum(of_pair * order, axis=0, keepdims=True)
    over = jnp.max(jnp.where(live & (turn > HALF - 0.5), 1.0, 0.0))
    late = turn > HALF - 0.5
    home_of = (jnp.where(late, width, 0) + owner) * 4 + jnp.where(late, turn - HALF, turn).astype(jnp.int32)
    own_first = jnp.where((iota((tpl_dev, total), 0) == of_template) & first, 1.0, 0.0)
    nth = dot(own_first.astype(jnp.bfloat16), before)
    nth = jnp.sum(own_first * nth, axis=0, keepdims=True).astype(jnp.int32)
    entry = (iota((BLOCK, total), 0) == nth).astype(jnp.bfloat16)
    listed = dot((own_first * home_of.astype(jnp.float32)).astype(jnp.bfloat16), entry, NT)
    number = jnp.sum(own_first, axis=1, keepdims=True)
    list_ref[...] = jnp.where(iota((tpl_dev, BLOCK), 1) == BLOCK - 1, number, listed).astype(jnp.int32)
    at_owner = jnp.where((iota((width, total), 0) == owner) & live, 1.0, 0.0)
    rank = jnp.sum(at_owner * dot(at_owner.astype(jnp.bfloat16), before), axis=0, keepdims=True)
    dest = jnp.where(live, owner * ROWS + rank.astype(jnp.int32), -1)
    pick = (iota((width * ROWS, total), 0) == dest).astype(jnp.bfloat16)
    kind = iota((BLOCK, total), 0)
    fields = jnp.where(kind == 0, local, jnp.where(kind == 1, moves, jnp.where(kind == 2, 1.0, 0.0)))
    fields = jnp.where(kind == 3, turn, fields).astype(jnp.bfloat16)
    tail = dot(pick, fields, NT)
    tail = jnp.where(iota(tail.shape, 1) == 4, over, tail).astype(jnp.bfloat16)
    copies[4].wait()
    send = dot(pick, templates_ref[...].reshape(total, 3 * L)).astype(jnp.bfloat16)
    send_ref[:, :, : 3 * L] = send.reshape(width, ROWS, 3 * L)
    send_ref[:, :, 3 * L :] = tail.reshape(width, ROWS, BLOCK)


def prep_kernel(wave_ref, xs_hbm, xs_ref, wide_ref, sems):
    tiles = wave_ref.shape[2] // BLOCK
    wide_ref[...] = wave_ref[...].astype(jnp.float32)
    lane = iota((8, BLOCK), 1)
    own = (lane // PHASES == iota((8, BLOCK), 0)).astype(jnp.float32)
    spread = (
        (iota((3 * PHASES, 3 * BLOCK), 1) // BLOCK == iota((3 * PHASES, 3 * BLOCK), 0) // PHASES)
        & (iota((3 * PHASES, 3 * BLOCK), 1) % PHASES == iota((3 * PHASES, 3 * BLOCK), 0) % PHASES)
    ).astype(jnp.bfloat16)
    sub = iota((PHASES, WIDE), 0)

    def one_station(s):
        comps = []
        for c in range(3):
            parts = []
            group = wide_ref[c, pl.ds(pl.multiple_of(s // 8 * 8, 8), 8), :]
            line = pltpu.roll(group, (8 - s % 8) % 8, 0)[0:1, :]
            for r in range(tiles):
                row = line[:, r * BLOCK : (r + 1) * BLOCK]
                parts.append(jnp.broadcast_to(row, (8, BLOCK)) * own)
            parts.append(jnp.zeros((WIDE - 8 * tiles, BLOCK), jnp.float32))
            comps.append(jnp.concatenate(parts, axis=0).astype(jnp.bfloat16))
        grid = jnp.concatenate(comps, axis=1)
        phases = dot(spread, grid, NT)
        squares = jnp.zeros((PHASES, WIDE), jnp.float32)
        for c in range(3):
            x = phases[c * PHASES : (c + 1) * PHASES]
            squares = squares + x * x
            short = x.astype(jnp.bfloat16)
            for r in range(REACH + 1):
                at = (c * (REACH + 1) + r) * PHASES
                xs_ref[s, at : at + PHASES, :] = short if r == 0 else pltpu.roll(short, WIDE - r, 1)
        up = squares
        down = jnp.where(sub >= 1, pltpu.roll(squares, 1, 0), 0.0)
        for step in (1, 2, 4, 8):
            up = up + jnp.where(sub < PHASES - step, pltpu.roll(up, PHASES - step, 0), 0.0)
            down = down + jnp.where(sub >= step, pltpu.roll(down, step, 0), 0.0)
        whole = jnp.broadcast_to(up[0:1, :], (PHASES, WIDE))
        two = whole + pltpu.roll(whole, WIDE - 1, 1)
        four = two + pltpu.roll(two, WIDE - 2, 1)
        eight = four + pltpu.roll(four, WIDE - 4, 1)
        fifteen = (
            pltpu.roll(eight, WIDE - 1, 1)
            + pltpu.roll(four, WIDE - 9, 1)
            + pltpu.roll(two, WIDE - 13, 1)
            + pltpu.roll(whole, WIDE - 15, 1)
        )
        power = (up + fifteen + pltpu.roll(down, WIDE - REACH, 1)) / (3.0 * L)
        inv = 1.0 / (3.0 * L * jnp.sqrt(power + EPS))
        for i in range(3):
            term = inv.astype(jnp.bfloat16)
            xs_ref[s, INV + i * PHASES : INV + (i + 1) * PHASES, :] = term
            inv = inv - term.astype(jnp.float32)
        xs_ref[s, INV + 3 * PHASES :, :] = jnp.zeros((DEPTH - INV - 3 * PHASES, WIDE), jnp.bfloat16)

    @pl.loop(0, wave_ref.shape[1] // 2)
    def _(i):
        one_station(2 * i)
        one_station(2 * i + 1)
        pair = pl.ds(2 * i, 2)
        pltpu.make_async_copy(xs_ref.at[pair], xs_hbm.at[pair], sems.at[i]).start()

    @pl.loop(0, wave_ref.shape[1] // 2)
    def _(i):
        pair = pl.ds(2 * i, 2)
        pltpu.make_async_copy(xs_ref.at[pair], xs_hbm.at[pair], sems.at[i]).wait()


def correlate_kernel(
    got_ref, xs_hbm, out_ref, more_ref, flag_ref, xs_ref, sorted_ref, order_ref, held_ref, table_ref, sem, xs_sems
):
    width = got_ref.shape[0]
    stations = xs_ref.shape[0]
    total = width * ROWS
    room = sorted_ref.shape[0]
    loads = [pltpu.make_async_copy(xs_hbm.at[s], xs_ref.at[s], xs_sems.at[s]) for s in range(stations)]
    for load in loads:
        load.start()
    got = got_ref[...].reshape(total, DEPTH)
    pieces = got[:, : 3 * L]
    eye = (iota((8, BLOCK), 0) == iota((8, BLOCK), 1)).astype(jnp.bfloat16)
    fields = dot(eye, got[:, 3 * L :], NT)
    live = fields[2:3, :] > 0.5
    at_station = jnp.where(
        (iota((stations, total), 0) == fields[0:1, :].astype(jnp.int32)) & live, 1.0, 0.0
    )
    before = (iota((total, total), 0) < iota((total, total), 1)).astype(jnp.bfloat16)
    rank = dot(at_station.astype(jnp.bfloat16), before)
    chunks = jnp.floor((jnp.sum(at_station, axis=1, keepdims=True) + (CHUNK - 1)) / CHUNK)
    earlier = (iota((stations, stations), 1) < iota((stations, stations), 0)).astype(jnp.bfloat16)
    start = dot(earlier, jnp.broadcast_to(chunks, (stations, BLOCK)).astype(jnp.bfloat16))[:, 0:1]
    place = jnp.sum(at_station * (start * CHUNK + rank), axis=0, keepdims=True).astype(jnp.int32)
    place = jnp.where(live, place, -1)
    pick = (iota((room, total), 0) == place).astype(jnp.bfloat16)
    kind = iota((8, total), 0)
    late = fields[3:4, :] > HALF - 0.5
    source = iota((1, total), 1) // ROWS
    turn = jnp.where(late, fields[3:4, :] - HALF, fields[3:4, :]).astype(jnp.int32)
    target = ((jnp.where(late, width, 0) + source) * 4 + turn).astype(jnp.float32)
    rows = jnp.where(kind == 3, target, jnp.where(kind < 3, fields, 0.0)).astype(jnp.bfloat16)
    table = dot(rows, pick, NT)
    over = jnp.max(fields[4:5, :])
    kind = iota((8, room), 0)
    table = jnp.where((kind == 3) & (table[2:3, :] < 0.5), float(held_ref.shape[0] - 1), table)
    table = jnp.where(kind == 4, jnp.sum(chunks), jnp.where(kind == 5, over, table))
    order_ref[...] = table.astype(jnp.int32)
    copy = pltpu.make_async_copy(order_ref, table_ref, sem)
    copy.start()
    flag_ref[...] = jnp.full(flag_ref.shape, over, jnp.float32).astype(jnp.int32)
    sorted_ref[...] = dot(pick, pieces)
    blank = jnp.zeros((PHASES, WIDE), jnp.float32)

    @pl.loop(0, jnp.where(over > 0.5, width, width // 2))
    def _(i):
        for r in (0, 1, 2, 4, 5, 6):
            held_ref[8 * i + r] = blank

    copy.wait()

    def arrive(s, carry):
        pltpu.make_async_copy(xs_hbm.at[s], xs_ref.at[s], xs_sems.at[s]).wait()
        return carry

    sub = iota((PHASES, BLOCK), 0)
    lane = iota((PHASES, BLOCK), 1)
    own = [lane >= PHASES * c + sub for c in range(3)]

    def toeplitz(slot):
        bands = []
        for k in range(CHUNK):
            band = []
            before = None
            for c in range(3):
                turned = []
                for h in range(2):
                    at = c * L + h * BLOCK
                    row = jnp.broadcast_to(slot[k : k + 1, at : at + BLOCK], (PHASES, BLOCK))
                    turned.append(pltpu.roll(row, c * PHASES, 1, stride=1, stride_axis=0))
                rest = 0.0 if c == 0 else jnp.where(own[c - 1], 0.0, before)
                band.append(jnp.where(own[c], turned[0], rest).astype(jnp.bfloat16))
                band.append(jnp.where(own[c], turned[1], turned[0]).astype(jnp.bfloat16))
                before = turned[1]
            band.append(jnp.where(own[2], 0.0, before).astype(jnp.bfloat16))
            bands.append(jnp.concatenate(band, axis=1))
        return jnp.concatenate(bands, axis=0)

    def chunk(i):
        first = pl.multiple_of(i * CHUNK, CHUNK)
        s = table_ref[0, first]
        slot = sorted_ref[pl.ds(first, CHUNK), :]
        mean = jnp.sum(slot * slot, axis=1, keepdims=True) / (3.0 * L)
        unit = 1.0 / jnp.sqrt(mean + EPS)
        corr = dot(toeplitz(slot), xs_ref[s])
        parts = [xs_ref[s, INV + i * PHASES : INV + (i + 1) * PHASES, :].astype(jnp.float32) for i in range(3)]
        inv = (parts[2] + parts[1]) + parts[0]
        for k in range(CHUNK):
            y = corr[k * PHASES : (k + 1) * PHASES] * (inv * unit[k : k + 1, :])
            move = table_ref[1, first + k] * (BLOCK // PHASES)
            turned = [
                pltpu.roll(y[:, b * BLOCK : (b + 1) * BLOCK], (BLOCK - move) % BLOCK, 1) for b in range(3)
            ]
            stay = lane < BLOCK - move
            target = table_ref[3, first + k]
            held_ref[target, :, :BLOCK] += jnp.where(stay, turned[0], turned[1])
            held_ref[target, :, BLOCK : 2 * BLOCK] += jnp.where(stay, turned[1], turned[2])
            held_ref[target, :, 2 * BLOCK :] += turned[2]

    def three_chunks(i, ready):
        last = table_ref[0, 3 * CHUNK * i]
        for k in range(1, 3):
            last = jnp.maximum(last, table_ref[0, (3 * i + k) * CHUNK])
        lax.fori_loop(ready, last + 1, arrive, 0)
        for k in range(3):
            chunk(3 * i + k)
        return jnp.maximum(ready, last + 1)

    ready = lax.fori_loop(0, (table_ref[4, 0] + 2) // 3, three_chunks, 0)
    lax.fori_loop(ready, stations, arrive, 0)
    end = KEPT - 2 * BLOCK

    def finish(ref, o, at):
        last = jnp.zeros((PHASES, BLOCK), jnp.float32)
        for r in range(HALF):
            y = held_ref[at * 4 + r]
            a, b = y[:, :BLOCK], y[:, BLOCK : 2 * BLOCK]
            c = jnp.where(lane < end, y[:, 2 * BLOCK :], 0.0)
            top = jnp.maximum(jnp.maximum(jnp.abs(a), jnp.abs(b)), jnp.abs(c))
            top = jnp.maximum(jnp.max(top, axis=1, keepdims=True), 2.0**-110)
            power = jnp.ceil(FINE * jnp.log2(jnp.broadcast_to(top, (PHASES, BLOCK))))
            scale = FULL * jnp.exp2(power * (-1.0 / FINE))
            ref[o, 2 * r] = jnp.round(a * scale).astype(jnp.int32).astype(jnp.int16)
            ref[o, 2 * r + 1] = jnp.round(b * scale).astype(jnp.int32).astype(jnp.int16)
            c = jnp.round(c * scale)
            last = last + (c if r == 0 else pltpu.roll(c, end * r, 1))
            last = jnp.where(lane == HALF * end + r, power, last)
        ref[o, 2 * HALF] = last.astype(jnp.int32).astype(jnp.int16)

    @pl.loop(0, width // 4)
    def _(i):
        for r in range(4):
            finish(out_ref, 4 * i + r, 4 * i + r)

    @pl.when(table_ref[5, 0] > 0)
    def _():
        @pl.loop(0, width)
        def _(o):
            finish(more_ref, o, width + o)


def add_kernel(list_ref, count_ref, back_ref, stack_ref, best_ref, scale_ref, tail_ref):
    end = KEPT - 2 * BLOCK

    def wide(x):
        return x.astype(jnp.int32).astype(jnp.float32)

    @pl.loop(0, back_ref.shape[0] // 8)
    def _(i):
        for part in range(8):
            o = 8 * i + part
            last = wide(back_ref[o, 2 * HALF])
            scales = jnp.exp2(last * (1.0 / FINE)) * (1.0 / FULL)
            for r in range(HALF):
                at = HALF * end + r
                scale_ref[o * 4 + r] = jnp.broadcast_to(scales[:, at : at + 1], (PHASES, BLOCK))
                tail_ref[o * 4 + r] = last if r == 0 else pltpu.roll(last, BLOCK - end * r, 1)

    def one_template(t, best):
        count = count_ref[t]
        number = list_ref[t, BLOCK - 1]

        def four_traces(g, total):
            for i in range(4):
                entry = list_ref[t, 4 * g + i]
                o = entry // 4
                r = entry % 4
                scale = jnp.where(4 * g + i < number, scale_ref[entry], 0.0)
                parts = (wide(back_ref[o, 2 * r]), wide(back_ref[o, 2 * r + 1]), tail_ref[entry])
                total = tuple(a + p * scale for a, p in zip(total, parts))
            return total

        zero = jnp.zeros((PHASES, BLOCK), jnp.float32)
        total = lax.fori_loop(0, (number + 3) // 4, four_traces, (zero, zero, zero))
        factor = jnp.sqrt(3.0 * L / jnp.full((1, 1), count, jnp.int32).astype(jnp.float32))
        whole = jnp.concatenate(total, axis=1) * factor
        stack_ref[t] = whole[:, :KEPT]
        return jnp.maximum(best, whole)

    start = jnp.full((PHASES, WIDE), -jnp.inf, jnp.float32)
    best = lax.fori_loop(0, stack_ref.shape[0], one_template, start)
    best_ref[...] = best[:, :KEPT]


VMEM = pl.BlockSpec(memory_space=pltpu.VMEM)
ANY = pl.BlockSpec(memory_space=pl.ANY)
SMEM = pl.BlockSpec(memory_space=pltpu.SMEM)


def params(mib):
    return pltpu.CompilerParams(vmem_limit_bytes=mib * 2**20)


def prep_call(waveforms):
    stations, _, samples = waveforms.shape
    return pl.pallas_call(
        prep_kernel,
        out_shape=jax.ShapeDtypeStruct((2 * stations + 4, DEPTH, WIDE), jnp.bfloat16),
        in_specs=[VMEM],
        out_specs=ANY,
        scratch_shapes=[
            pltpu.VMEM((stations, DEPTH, WIDE), jnp.bfloat16),
            pltpu.VMEM((3, stations, samples), jnp.float32),
            pltpu.SemaphoreType.DMA((stations // 2,)),
        ],
        compiler_params=params(40),
        cost_estimate=pl.CostEstimate(flops=2 * 10**9, bytes_accessed=12 * 2**20, transcendentals=0),
    )(waveforms.transpose(1, 0, 2))


def correlate_call(got, xs, stations):
    width = got.shape[0]
    room = 8 * (width * CAP // CHUNK + stations)
    return pl.pallas_call(
        correlate_kernel,
        out_shape=(
            jax.ShapeDtypeStruct((width, BLOCKS, PHASES, BLOCK), jnp.int16),
            jax.ShapeDtypeStruct((width, BLOCKS, PHASES, BLOCK), jnp.int16),
            jax.ShapeDtypeStruct((1, BLOCK), jnp.int32),
        ),
        in_specs=[VMEM, ANY],
        out_specs=(VMEM, VMEM, VMEM),
        scratch_shapes=[
            pltpu.VMEM((stations, DEPTH, WIDE), jnp.bfloat16),
            pltpu.VMEM((room, 3 * L), jnp.float32),
            pltpu.VMEM((8, room), jnp.int32),
            pltpu.VMEM((8 * width + 8, PHASES, WIDE), jnp.float32),
            pltpu.SMEM((8, room), jnp.int32),
            pltpu.SemaphoreType.DMA,
            pltpu.SemaphoreType.DMA((stations,)),
        ],
        compiler_params=params(40),
    )(got, xs)


def add_call(listed, counts, back):
    tpl_dev = counts.shape[0]
    return pl.pallas_call(
        add_kernel,
        out_shape=(
            jax.ShapeDtypeStruct((tpl_dev, PHASES, KEPT), jnp.float32),
            jax.ShapeDtypeStruct((PHASES, KEPT), jnp.float32),
        ),
        in_specs=[SMEM, SMEM, VMEM],
        out_specs=(VMEM, VMEM),
        scratch_shapes=[
            pltpu.VMEM((back.shape[0] * 4, PHASES, BLOCK), jnp.float32),
            pltpu.VMEM((back.shape[0] * 4, PHASES, BLOCK), jnp.float32),
        ],
        compiler_params=params(40),
    )(listed, counts, back)


def body(waveforms, station_home, templates, template_stations, station_counts, moveouts):
    stations, _, samples = waveforms.shape
    tpl_dev = templates.shape[0]
    width = lax.axis_size("sta")
    parts = station_home.shape[0] // BLOCK
    send, listed = pl.pallas_call(
        pack_kernel,
        out_shape=(
            jax.ShapeDtypeStruct((width, ROWS, DEPTH), jnp.bfloat16),
            jax.ShapeDtypeStruct((tpl_dev, BLOCK), jnp.int32),
        ),
        in_specs=[ANY] * 5,
        out_specs=(VMEM, VMEM),
        scratch_shapes=[
            pltpu.VMEM((tpl_dev, SLOTS), jnp.int32),
            pltpu.VMEM((tpl_dev, SLOTS), jnp.int32),
            pltpu.SMEM((tpl_dev,), jnp.int32),
            pltpu.VMEM((parts, BLOCK), jnp.int32),
            pltpu.VMEM((SLOTS, tpl_dev, 3 * L), jnp.bfloat16),
            pltpu.SemaphoreType.DMA((5,)),
        ],
        compiler_params=params(60),
    )(
        template_stations,
        moveouts,
        station_counts,
        station_home.reshape(parts, BLOCK),
        templates.transpose(1, 0, 2),
    )
    got = lax.all_to_all(send, "sta", split_axis=0, concat_axis=0, tiled=True)
    xs = prep_call(waveforms)
    traces, more, flag = correlate_call(got, xs, stations)

    def home(x):
        return lax.all_to_all(x, "sta", split_axis=0, concat_axis=0, tiled=True)

    def one_exchange(traces, more):
        return add_call(listed, station_counts, home(traces))

    def two_exchanges(traces, more):
        return add_call(listed, station_counts, jnp.concatenate([home(traces), home(more)]))

    stack, best = lax.cond(flag[0, 0] > 0, two_exchanges, one_exchange, traces, more)
    best = best.T.reshape(-1, BLOCK)
    for n, (axis, steps) in enumerate(ROUNDS):
        size = lax.axis_size(axis)
        others = [lax.ppermute(best, axis, [(i, i ^ step) for i in range(size)]) for step in steps]
        for other in others:
            best = jnp.maximum(best, other)
        if n == 0:
            best, stack = lax.optimization_barrier((best, stack))
            stack = stack.transpose(0, 2, 1).reshape(tpl_dev, PHASES * KEPT)
        if n == 1:
            best, stack = lax.optimization_barrier((best, stack))
    return (stack, best.reshape(PHASES * KEPT))


ROUNDS = (("tpl", (1, 2, 3)), ("tpl", (6,)), ("sta", (1,)), ("sta", (2, 6, 4)), ("sta", (8, 24, 16)))


def solution(mesh):
    in_specs = (
        P("sta", None, None),
        P(),
        P(("sta", "tpl"), None, None),
        P(("sta", "tpl"), None),
        P(("sta", "tpl")),
        P(("sta", "tpl"), None),
    )
    out_specs = (P(("sta", "tpl"), None), P())
    return jax.shard_map(body, mesh=mesh, in_specs=in_specs, out_specs=out_specs, check_vma=False)
```

```python
import functools

import jax
import jax.numpy as jnp
from jax import lax
from jax.experimental import pallas as pl
from jax.experimental.pallas import tpu as pltpu
from jax.sharding import PartitionSpec as P

SLOTS = 20
L = 256
BLOCK = 128
LAG_BLOCKS = 40
MOVE_BLOCKS = 4
EPS = 1e-06

PHASES = 16
COLS = LAG_BLOCKS * BLOCK // PHASES
KEPT = (LAG_BLOCKS - MOVE_BLOCKS) * BLOCK // PHASES
WIDE = 384
REACH = L // PHASES
DEPTH = 3 * L + BLOCK
INV = 3 * L + 3 * PHASES
CHUNK = 8
CAP = 6
ROWS = 8
HALF = 3
BLOCKS = 7

FINE = 8.0
FULL = 32700.0
NT = (((1,), (1,)), ((), ()))


def iota(shape, dim):
    return lax.broadcasted_iota(jnp.int32, shape, dim)


def dot(a, b, dims=None):
    if dims is None:
        dims = (((1,), (0,)), ((), ()))
    return lax.dot_general(a, b, dims, preferred_element_type=jnp.float32)


def pack_kernel(
    stations_hbm, moves_hbm, counts_hbm, home_hbm, templates_hbm, send_ref, list_ref,
    stations_ref, moves_ref, counts_ref, home_ref, templates_ref, sems,
):
    copies = [
        pltpu.make_async_copy(src, dst, sems.at[i])
        for i, (src, dst) in enumerate(
            (
                (stations_hbm, stations_ref),
                (moves_hbm, moves_ref),
                (counts_hbm, counts_ref),
                (home_hbm, home_ref),
                (templates_hbm, templates_ref),
            )
        )
    ]
    for copy in copies:
        copy.start()
    tpl_dev, slots = stations_ref.shape
    total = tpl_dev * slots
    width = send_ref.shape[0]
    parts = home_ref.shape[0]
    sta_dev = parts * BLOCK // width
    place = iota((1, total), 1)
    of_template = place % tpl_dev
    for copy in copies[:4]:
        copy.wait()
    stations = stations_ref[...]
    high = stations // 16
    fields = jnp.concatenate([high, stations - 16 * high, moves_ref[...]], axis=0)
    expand = (iota((slots, total), 1) // tpl_dev == iota((slots, total), 0)).astype(jnp.bfloat16)
    spread = dot(fields.astype(jnp.float32).astype(jnp.bfloat16), expand)
    mine = iota((tpl_dev, total), 0) == of_template
    rows = [
        jnp.sum(jnp.where(mine, spread[i * tpl_dev : (i + 1) * tpl_dev], 0.0), axis=0, keepdims=True)
        for i in range(3)
    ]
    station = (rows[0] * 16.0 + rows[1]).astype(jnp.int32)
    moves = rows[2]
    counts = jnp.zeros((1, total), jnp.int32)
    for t in range(tpl_dev):
        counts = jnp.where(of_template == t, counts_ref[t], counts)
    home = home_ref[...]
    owners = home // sta_dev
    table = jnp.concatenate([owners, home - owners * sta_dev], axis=0)
    hit = (iota((BLOCK, total), 0) == station % BLOCK).astype(jnp.bfloat16)
    found = dot(table.astype(jnp.float32).astype(jnp.bfloat16), hit)
    part = iota((parts, total), 0) == station // BLOCK
    owner = jnp.sum(jnp.where(part, found[:parts], 0.0), axis=0, keepdims=True).astype(jnp.int32)
    local = jnp.sum(jnp.where(part, found[parts:], 0.0), axis=0, keepdims=True)
    live = place // tpl_dev < counts
    before = (iota((total, total), 0) < iota((total, total), 1)).astype(jnp.bfloat16)
    pairs = width * tpl_dev
    of_pair = jnp.where((iota((pairs, total), 0) == owner * tpl_dev + of_template) & live, 1.0, 0.0)
    earlier = jnp.sum(of_pair * dot(of_pair.astype(jnp.bfloat16), before), axis=0, keepdims=True)
    first = live & (earlier < 0.5)
    present = jnp.minimum(jnp.sum(of_pair, axis=1, keepdims=True), 1.0)
    row, col = iota((pairs, pairs), 0), iota((pairs, pairs), 1)
    lower = ((row // tpl_dev == col // tpl_dev) & (col < row)).astype(jnp.bfloat16)
    order = dot(lower, jnp.broadcast_to(present, (pairs, BLOCK)).astype(jnp.bfloat16))[:, 0:1]
    turn = jnp.sum(of_pair * order, axis=0, keepdims=True)
    over = jnp.max(jnp.where(live & (turn > HALF - 0.5), 1.0, 0.0))
    late = turn > HALF - 0.5
    home_of = (jnp.where(late, width, 0) + owner) * 4 + jnp.where(late, turn - HALF, turn).astype(jnp.int32)
    own_first = jnp.where((iota((tpl_dev, total), 0) == of_template) & first, 1.0, 0.0)
    nth = dot(own_first.astype(jnp.bfloat16), before)
    nth = jnp.sum(own_first * nth, axis=0, keepdims=True).astype(jnp.int32)
    entry = (iota((BLOCK, total), 0) == nth).astype(jnp.bfloat16)
    listed = dot((own_first * home_of.astype(jnp.float32)).astype(jnp.bfloat16), entry, NT)
    number = jnp.sum(own_first, axis=1, keepdims=True)
    list_ref[...] = jnp.where(iota((tpl_dev, BLOCK), 1) == BLOCK - 1, number, listed).astype(jnp.int32)
    at_owner = jnp.where((iota((width, total), 0) == owner) & live, 1.0, 0.0)
    rank = jnp.sum(at_owner * dot(at_owner.astype(jnp.bfloat16), before), axis=0, keepdims=True)
    dest = jnp.where(live, owner * ROWS + rank.astype(jnp.int32), -1)
    pick = (iota((width * ROWS, total), 0) == dest).astype(jnp.bfloat16)
    kind = iota((BLOCK, total), 0)
    fields = jnp.where(kind == 0, local, jnp.where(kind == 1, moves, jnp.where(kind == 2, 1.0, 0.0)))
    fields = jnp.where(kind == 3, turn, fields).astype(jnp.bfloat16)
    tail = dot(pick, fields, NT)
    tail = jnp.where(iota(tail.shape, 1) == 4, over, tail).astype(jnp.bfloat16)
    copies[4].wait()
    send = dot(pick, templates_ref[...]).astype(jnp.bfloat16)
    send_ref[:, :, : 3 * L] = send.reshape(width, ROWS, 3 * L)
    send_ref[:, :, 3 * L :] = tail.reshape(width, ROWS, BLOCK)


def prep_kernel(wave_ref, xs_hbm, xs_ref, wide_ref, sems):
    tiles = wave_ref.shape[2] // BLOCK
    wide_ref[...] = wave_ref[...].astype(jnp.float32)
    lane = iota((8, BLOCK), 1)
    own = (lane // PHASES == iota((8, BLOCK), 0)).astype(jnp.float32)
    spread = (
        (iota((3 * PHASES, 3 * BLOCK), 1) // BLOCK == iota((3 * PHASES, 3 * BLOCK), 0) // PHASES)
        & (iota((3 * PHASES, 3 * BLOCK), 1) % PHASES == iota((3 * PHASES, 3 * BLOCK), 0) % PHASES)
    ).astype(jnp.bfloat16)
    sub = iota((PHASES, WIDE), 0)

    def one_station(s):
        comps = []
        for c in range(3):
            parts = []
            group = wide_ref[c, pl.ds(pl.multiple_of(s // 8 * 8, 8), 8), :]
            line = pltpu.roll(group, (8 - s % 8) % 8, 0)[0:1, :]
            for r in range(tiles):
                row = line[:, r * BLOCK : (r + 1) * BLOCK]
                parts.append(jnp.broadcast_to(row, (8, BLOCK)) * own)
            parts.append(jnp.zeros((WIDE - 8 * tiles, BLOCK), jnp.float32))
            comps.append(jnp.concatenate(parts, axis=0).astype(jnp.bfloat16))
        grid = jnp.concatenate(comps, axis=1)
        phases = dot(spread, grid, NT)
        squares = jnp.zeros((PHASES, WIDE), jnp.float32)
        for c in range(3):
            x = phases[c * PHASES : (c + 1) * PHASES]
            squares = squares + x * x
            short = x.astype(jnp.bfloat16)
            for r in range(REACH + 1):
                at = (c * (REACH + 1) + r) * PHASES
                xs_ref[s, at : at + PHASES, :] = short if r == 0 else pltpu.roll(short, WIDE - r, 1)
        up = squares
        down = jnp.where(sub >= 1, pltpu.roll(squares, 1, 0), 0.0)
        for step in (1, 2, 4, 8):
            up = up + jnp.where(sub < PHASES - step, pltpu.roll(up, PHASES - step, 0), 0.0)
            down = down + jnp.where(sub >= step, pltpu.roll(down, step, 0), 0.0)
        whole = jnp.broadcast_to(up[0:1, :], (PHASES, WIDE))
        two = whole + pltpu.roll(whole, WIDE - 1, 1)
        four = two + pltpu.roll(two, WIDE - 2, 1)
        eight = four + pltpu.roll(four, WIDE - 4, 1)
        fifteen = (
            pltpu.roll(eight, WIDE - 1, 1)
            + pltpu.roll(four, WIDE - 9, 1)
            + pltpu.roll(two, WIDE - 13, 1)
            + pltpu.roll(whole, WIDE - 15, 1)
        )
        power = (up + fifteen + pltpu.roll(down, WIDE - REACH, 1)) / (3.0 * L)
        inv = 1.0 / (3.0 * L * jnp.sqrt(power + EPS))
        for i in range(3):
            term = inv.astype(jnp.bfloat16)
            xs_ref[s, INV + i * PHASES : INV + (i + 1) * PHASES, :] = term
            inv = inv - term.astype(jnp.float32)
        xs_ref[s, INV + 3 * PHASES :, :] = jnp.zeros((DEPTH - INV - 3 * PHASES, WIDE), jnp.bfloat16)

    @pl.loop(0, wave_ref.shape[1] // 2)
    def _(i):
        one_station(2 * i)
        one_station(2 * i + 1)
        pair = pl.ds(2 * i, 2)
        pltpu.make_async_copy(xs_ref.at[pair], xs_hbm.at[pair], sems.at[i]).start()

    @pl.loop(0, wave_ref.shape[1] // 2)
    def _(i):
        pair = pl.ds(2 * i, 2)
        pltpu.make_async_copy(xs_ref.at[pair], xs_hbm.at[pair], sems.at[i]).wait()


def correlate_kernel(
    got_ref, xs_hbm, out_ref, more_ref, flag_ref, xs_ref, sorted_ref, order_ref, held_ref, table_ref, sem, xs_sems
):
    width = got_ref.shape[0]
    stations = xs_ref.shape[0]
    total = width * ROWS
    room = sorted_ref.shape[0]
    loads = [pltpu.make_async_copy(xs_hbm.at[s], xs_ref.at[s], xs_sems.at[s]) for s in range(stations)]
    for load in loads:
        load.start()
    got = got_ref[...].reshape(total, DEPTH)
    pieces = got[:, : 3 * L]
    eye = (iota((8, BLOCK), 0) == iota((8, BLOCK), 1)).astype(jnp.bfloat16)
    fields = dot(eye, got[:, 3 * L :], NT)
    live = fields[2:3, :] > 0.5
    at_station = jnp.where(
        (iota((stations, total), 0) == fields[0:1, :].astype(jnp.int32)) & live, 1.0, 0.0
    )
    before = (iota((total, total), 0) < iota((total, total), 1)).astype(jnp.bfloat16)
    rank = dot(at_station.astype(jnp.bfloat16), before)
    chunks = jnp.floor((jnp.sum(at_station, axis=1, keepdims=True) + (CHUNK - 1)) / CHUNK)
    earlier = (iota((stations, stations), 1) < iota((stations, stations), 0)).astype(jnp.bfloat16)
    start = dot(earlier, jnp.broadcast_to(chunks, (stations, BLOCK)).astype(jnp.bfloat16))[:, 0:1]
    place = jnp.sum(at_station * (start * CHUNK + rank), axis=0, keepdims=True).astype(jnp.int32)
    place = jnp.where(live, place, -1)
    pick = (iota((room, total), 0) == place).astype(jnp.bfloat16)
    kind = iota((8, total), 0)
    late = fields[3:4, :] > HALF - 0.5
    source = iota((1, total), 1) // ROWS
    turn = jnp.where(late, fields[3:4, :] - HALF, fields[3:4, :]).astype(jnp.int32)
    target = ((jnp.where(late, width, 0) + source) * 4 + turn).astype(jnp.float32)
    rows = jnp.where(kind == 3, target, jnp.where(kind < 3, fields, 0.0)).astype(jnp.bfloat16)
    table = dot(rows, pick, NT)
    over = jnp.max(fields[4:5, :])
    kind = iota((8, room), 0)
    table = jnp.where((kind == 3) & (table[2:3, :] < 0.5), float(held_ref.shape[0] - 1), table)
    table = jnp.where(kind == 4, jnp.sum(chunks), jnp.where(kind == 5, over, table))
    order_ref[...] = table.astype(jnp.int32)
    copy = pltpu.make_async_copy(order_ref, table_ref, sem)
    copy.start()
    flag_ref[...] = jnp.full(flag_ref.shape, over, jnp.float32).astype(jnp.int32)
    sorted_ref[...] = dot(pick, pieces)
    blank = jnp.zeros((PHASES, WIDE), jnp.float32)

    @pl.loop(0, jnp.where(over > 0.5, width, width // 2))
    def _(i):
        for r in (0, 1, 2, 4, 5, 6):
            held_ref[8 * i + r] = blank

    copy.wait()

    def arrive(s, carry):
        pltpu.make_async_copy(xs_hbm.at[s], xs_ref.at[s], xs_sems.at[s]).wait()
        return carry

    sub = iota((PHASES, BLOCK), 0)
    lane = iota((PHASES, BLOCK), 1)
    own = [lane >= PHASES * c + sub for c in range(3)]

    def toeplitz(slot):
        bands = []
        for k in range(CHUNK):
            band = []
            before = None
            for c in range(3):
                turned = []
                for h in range(2):
                    at = c * L + h * BLOCK
                    row = jnp.broadcast_to(slot[k : k + 1, at : at + BLOCK], (PHASES, BLOCK))
                    turned.append(pltpu.roll(row, c * PHASES, 1, stride=1, stride_axis=0))
                rest = 0.0 if c == 0 else jnp.where(own[c - 1], 0.0, before)
                band.append(jnp.where(own[c], turned[0], rest).astype(jnp.bfloat16))
                band.append(jnp.where(own[c], turned[1], turned[0]).astype(jnp.bfloat16))
                before = turned[1]
            band.append(jnp.where(own[2], 0.0, before).astype(jnp.bfloat16))
            bands.append(jnp.concatenate(band, axis=1))
        return jnp.concatenate(bands, axis=0)

    def chunk(i):
        first = pl.multiple_of(i * CHUNK, CHUNK)
        s = table_ref[0, first]
        slot = sorted_ref[pl.ds(first, CHUNK), :]
        mean = jnp.sum(slot * slot, axis=1, keepdims=True) / (3.0 * L)
        unit = 1.0 / jnp.sqrt(mean + EPS)
        corr = dot(toeplitz(slot), xs_ref[s])
        parts = [xs_ref[s, INV + i * PHASES : INV + (i + 1) * PHASES, :].astype(jnp.float32) for i in range(3)]
        inv = (parts[2] + parts[1]) + parts[0]
        for k in range(CHUNK):
            y = corr[k * PHASES : (k + 1) * PHASES] * (inv * unit[k : k + 1, :])
            move = table_ref[1, first + k] * (BLOCK // PHASES)
            turned = [
                pltpu.roll(y[:, b * BLOCK : (b + 1) * BLOCK], (BLOCK - move) % BLOCK, 1) for b in range(3)
            ]
            stay = lane < BLOCK - move
            target = table_ref[3, first + k]
            held_ref[target, :, :BLOCK] += jnp.where(stay, turned[0], turned[1])
            held_ref[target, :, BLOCK : 2 * BLOCK] += jnp.where(stay, turned[1], turned[2])
            held_ref[target, :, 2 * BLOCK :] += turned[2]

    def three_chunks(i, ready):
        last = table_ref[0, 3 * CHUNK * i]
        for k in range(1, 3):
            last = jnp.maximum(last, table_ref[0, (3 * i + k) * CHUNK])
        lax.fori_loop(ready, last + 1, arrive, 0)
        for k in range(3):
            chunk(3 * i + k)
        return jnp.maximum(ready, last + 1)

    ready = lax.fori_loop(0, (table_ref[4, 0] + 2) // 3, three_chunks, 0)
    lax.fori_loop(ready, stations, arrive, 0)
    end = KEPT - 2 * BLOCK

    def finish(ref, o, at):
        last = jnp.zeros((PHASES, BLOCK), jnp.float32)
        for r in range(HALF):
            y = held_ref[at * 4 + r]
            a, b = y[:, :BLOCK], y[:, BLOCK : 2 * BLOCK]
            c = jnp.where(lane < end, y[:, 2 * BLOCK :], 0.0)
            top = jnp.maximum(jnp.maximum(jnp.abs(a), jnp.abs(b)), jnp.abs(c))
            top = jnp.maximum(jnp.max(top, axis=1, keepdims=True), 2.0**-110)
            power = jnp.ceil(FINE * jnp.log2(jnp.broadcast_to(top, (PHASES, BLOCK))))
            scale = FULL * jnp.exp2(power * (-1.0 / FINE))
            ref[o, 2 * r] = jnp.round(a * scale).astype(jnp.int32).astype(jnp.int16)
            ref[o, 2 * r + 1] = jnp.round(b * scale).astype(jnp.int32).astype(jnp.int16)
            c = jnp.round(c * scale)
            last = last + (c if r == 0 else pltpu.roll(c, end * r, 1))
            last = jnp.where(lane == HALF * end + r, power, last)
        ref[o, 2 * HALF] = last.astype(jnp.int32).astype(jnp.int16)

    @pl.loop(0, width // 4)
    def _(i):
        for r in range(4):
            finish(out_ref, 4 * i + r, 4 * i + r)

    @pl.when(table_ref[5, 0] > 0)
    def _():
        @pl.loop(0, width)
        def _(o):
            finish(more_ref, o, width + o)


def add_kernel(list_ref, count_ref, back_ref, stack_ref, best_ref, scale_ref, tail_ref):
    end = KEPT - 2 * BLOCK

    def wide(x):
        return x.astype(jnp.int32).astype(jnp.float32)

    @pl.loop(0, back_ref.shape[0] // 8)
    def _(i):
        for part in range(8):
            o = 8 * i + part
            last = wide(back_ref[o, 2 * HALF])
            scales = jnp.exp2(last * (1.0 / FINE)) * (1.0 / FULL)
            for r in range(HALF):
                at = HALF * end + r
                scale_ref[o * 4 + r] = jnp.broadcast_to(scales[:, at : at + 1], (PHASES, BLOCK))
                tail_ref[o * 4 + r] = last if r == 0 else pltpu.roll(last, BLOCK - end * r, 1)

    def one_template(t, best):
        count = count_ref[t]
        number = list_ref[t, BLOCK - 1]

        def four_traces(g, total):
            for i in range(4):
                entry = list_ref[t, 4 * g + i]
                o = entry // 4
                r = entry % 4
                scale = jnp.where(4 * g + i < number, scale_ref[entry], 0.0)
                parts = (wide(back_ref[o, 2 * r]), wide(back_ref[o, 2 * r + 1]), tail_ref[entry])
                total = tuple(a + p * scale for a, p in zip(total, parts))
            return total

        zero = jnp.zeros((PHASES, BLOCK), jnp.float32)
        total = lax.fori_loop(0, (number + 3) // 4, four_traces, (zero, zero, zero))
        factor = jnp.sqrt(3.0 * L / jnp.full((1, 1), count, jnp.int32).astype(jnp.float32))
        whole = jnp.concatenate(total, axis=1) * factor
        stack_ref[t] = whole[:, :KEPT]
        return jnp.maximum(best, whole)

    start = jnp.full((PHASES, WIDE), -jnp.inf, jnp.float32)
    best = lax.fori_loop(0, stack_ref.shape[0], one_template, start)
    best_ref[...] = best[:, :KEPT]


VMEM = pl.BlockSpec(memory_space=pltpu.VMEM)
ANY = pl.BlockSpec(memory_space=pl.ANY)
SMEM = pl.BlockSpec(memory_space=pltpu.SMEM)


def params(mib):
    return pltpu.CompilerParams(vmem_limit_bytes=mib * 2**20)


def prep_call(waveforms):
    stations, _, samples = waveforms.shape
    return pl.pallas_call(
        prep_kernel,
        out_shape=jax.ShapeDtypeStruct((2 * stations + 4, DEPTH, WIDE), jnp.bfloat16),
        in_specs=[VMEM],
        out_specs=ANY,
        scratch_shapes=[
            pltpu.VMEM((stations, DEPTH, WIDE), jnp.bfloat16),
            pltpu.VMEM((3, stations, samples), jnp.float32),
            pltpu.SemaphoreType.DMA((stations // 2,)),
        ],
        compiler_params=params(40),
        cost_estimate=pl.CostEstimate(flops=2 * 10**9, bytes_accessed=12 * 2**20, transcendentals=0),
    )(waveforms.transpose(1, 0, 2))


def correlate_call(got, xs, stations):
    width = got.shape[0]
    room = 8 * (width * CAP // CHUNK + stations)
    return pl.pallas_call(
        correlate_kernel,
        out_shape=(
            jax.ShapeDtypeStruct((width, BLOCKS, PHASES, BLOCK), jnp.int16),
            jax.ShapeDtypeStruct((width, BLOCKS, PHASES, BLOCK), jnp.int16),
            jax.ShapeDtypeStruct((1, BLOCK), jnp.int32),
        ),
        in_specs=[VMEM, ANY],
        out_specs=(VMEM, VMEM, VMEM),
        scratch_shapes=[
            pltpu.VMEM((stations, DEPTH, WIDE), jnp.bfloat16),
            pltpu.VMEM((room, 3 * L), jnp.float32),
            pltpu.VMEM((8, room), jnp.int32),
            pltpu.VMEM((8 * width + 8, PHASES, WIDE), jnp.float32),
            pltpu.SMEM((8, room), jnp.int32),
            pltpu.SemaphoreType.DMA,
            pltpu.SemaphoreType.DMA((stations,)),
        ],
        compiler_params=params(40),
    )(got, xs)


def add_call(listed, counts, back):
    tpl_dev = counts.shape[0]
    return pl.pallas_call(
        add_kernel,
        out_shape=(
            jax.ShapeDtypeStruct((tpl_dev, PHASES, KEPT), jnp.float32),
            jax.ShapeDtypeStruct((PHASES, KEPT), jnp.float32),
        ),
        in_specs=[SMEM, SMEM, VMEM],
        out_specs=(VMEM, VMEM),
        scratch_shapes=[
            pltpu.VMEM((back.shape[0] * 4, PHASES, BLOCK), jnp.float32),
            pltpu.VMEM((back.shape[0] * 4, PHASES, BLOCK), jnp.float32),
        ],
        compiler_params=params(40),
    )(listed, counts, back)


def body(waveforms, station_home, templates, template_stations, station_counts, moveouts):
    stations, _, samples = waveforms.shape
    tpl_dev = templates.shape[0]
    width = lax.axis_size("sta")
    parts = station_home.shape[0] // BLOCK
    send, listed = pl.pallas_call(
        pack_kernel,
        out_shape=(
            jax.ShapeDtypeStruct((width, ROWS, DEPTH), jnp.bfloat16),
            jax.ShapeDtypeStruct((tpl_dev, BLOCK), jnp.int32),
        ),
        in_specs=[ANY] * 5,
        out_specs=(VMEM, VMEM),
        scratch_shapes=[
            pltpu.VMEM((tpl_dev, SLOTS), jnp.int32),
            pltpu.VMEM((tpl_dev, SLOTS), jnp.int32),
            pltpu.SMEM((tpl_dev,), jnp.int32),
            pltpu.VMEM((parts, BLOCK), jnp.int32),
            pltpu.VMEM((tpl_dev * SLOTS, 3 * L), jnp.bfloat16),
            pltpu.SemaphoreType.DMA((5,)),
        ],
        compiler_params=params(60),
    )(
        template_stations,
        moveouts,
        station_counts,
        station_home.reshape(parts, BLOCK),
        templates.transpose(1, 0, 2).reshape(tpl_dev * SLOTS, 3 * L),
    )
    got = lax.all_to_all(send, "sta", split_axis=0, concat_axis=0, tiled=True)
    xs = prep_call(waveforms)
    traces, more, flag = correlate_call(got, xs, stations)

    def home(x):
        return lax.all_to_all(x, "sta", split_axis=0, concat_axis=0, tiled=True)

    def one_exchange(traces, more):
        return add_call(listed, station_counts, home(traces))

    def two_exchanges(traces, more):
        return add_call(listed, station_counts, jnp.concatenate([home(traces), home(more)]))

    stack, best = lax.cond(flag[0, 0] > 0, two_exchanges, one_exchange, traces, more)
    best = best.T.reshape(-1, BLOCK)
    for n, (axis, steps) in enumerate(ROUNDS):
        size = lax.axis_size(axis)
        others = [lax.ppermute(best, axis, [(i, i ^ step) for i in range(size)]) for step in steps]
        for other in others:
            best = jnp.maximum(best, other)
        if n == 0:
            best, stack = lax.optimization_barrier((best, stack))
            stack = stack.transpose(0, 2, 1).reshape(tpl_dev, PHASES * KEPT)
        if n == 1:
            best, stack = lax.optimization_barrier((best, stack))
    return (stack, best.reshape(PHASES * KEPT))


ROUNDS = (("sta", (1,)), ("tpl", (6,)), ("tpl", (1, 2, 3)), ("sta", (2, 6, 4)), ("sta", (8, 24, 16)))


def solution(mesh):
    in_specs = (
        P("sta", None, None),
        P(),
        P(("sta", "tpl"), None, None),
        P(("sta", "tpl"), None),
        P(("sta", "tpl")),
        P(("sta", "tpl"), None),
    )
    out_specs = (P(("sta", "tpl"), None), P())
    return jax.shard_map(body, mesh=mesh, in_specs=in_specs, out_specs=out_specs, check_vma=False)
```

```python
import functools

import jax
import jax.numpy as jnp
from jax import lax
from jax.experimental import pallas as pl
from jax.experimental.pallas import tpu as pltpu
from jax.sharding import PartitionSpec as P

SLOTS = 20
L = 256
BLOCK = 128
LAG_BLOCKS = 40
MOVE_BLOCKS = 4
EPS = 1e-06

PHASES = 16
COLS = LAG_BLOCKS * BLOCK // PHASES
KEPT = (LAG_BLOCKS - MOVE_BLOCKS) * BLOCK // PHASES
WIDE = 384
REACH = L // PHASES
DEPTH = 3 * L + BLOCK
INV = 3 * L + 3 * PHASES
USED = INV + 3 * PHASES
CHUNK = 8
CAP = 6
ROWS = 8
HALF = 3
BLOCKS = 7

FINE = 8.0
FULL = 32700.0
NT = (((1,), (1,)), ((), ()))


def iota(shape, dim):
    return lax.broadcasted_iota(jnp.int32, shape, dim)


def dot(a, b, dims=None):
    if dims is None:
        dims = (((1,), (0,)), ((), ()))
    return lax.dot_general(a, b, dims, preferred_element_type=jnp.float32)


def pack_kernel(
    stations_hbm, moves_hbm, counts_hbm, home_hbm, templates_hbm, send_ref, list_ref,
    stations_ref, moves_ref, counts_ref, home_ref, templates_ref, sems,
):
    copies = [
        pltpu.make_async_copy(src, dst, sems.at[i])
        for i, (src, dst) in enumerate(
            (
                (stations_hbm, stations_ref),
                (moves_hbm, moves_ref),
                (counts_hbm, counts_ref),
                (home_hbm, home_ref),
                (templates_hbm, templates_ref),
            )
        )
    ]
    for copy in copies:
        copy.start()
    tpl_dev, slots = stations_ref.shape
    total = tpl_dev * slots
    width = send_ref.shape[0]
    parts = home_ref.shape[0]
    sta_dev = parts * BLOCK // width
    place = iota((1, total), 1)
    of_template = place % tpl_dev
    for copy in copies[:4]:
        copy.wait()
    stations = stations_ref[...]
    high = stations // 16
    fields = jnp.concatenate([high, stations - 16 * high, moves_ref[...]], axis=0)
    expand = (iota((slots, total), 1) // tpl_dev == iota((slots, total), 0)).astype(jnp.bfloat16)
    spread = dot(fields.astype(jnp.float32).astype(jnp.bfloat16), expand)
    mine = iota((tpl_dev, total), 0) == of_template
    rows = [
        jnp.sum(jnp.where(mine, spread[i * tpl_dev : (i + 1) * tpl_dev], 0.0), axis=0, keepdims=True)
        for i in range(3)
    ]
    station = (rows[0] * 16.0 + rows[1]).astype(jnp.int32)
    moves = rows[2]
    counts = jnp.zeros((1, total), jnp.int32)
    for t in range(tpl_dev):
        counts = jnp.where(of_template == t, counts_ref[t], counts)
    home = home_ref[...]
    owners = home // sta_dev
    table = jnp.concatenate([owners, home - owners * sta_dev], axis=0)
    hit = (iota((BLOCK, total), 0) == station % BLOCK).astype(jnp.bfloat16)
    found = dot(table.astype(jnp.float32).astype(jnp.bfloat16), hit)
    part = iota((parts, total), 0) == station // BLOCK
    owner = jnp.sum(jnp.where(part, found[:parts], 0.0), axis=0, keepdims=True).astype(jnp.int32)
    local = jnp.sum(jnp.where(part, found[parts:], 0.0), axis=0, keepdims=True)
    live = place // tpl_dev < counts
    before = (iota((total, total), 0) < iota((total, total), 1)).astype(jnp.bfloat16)
    pairs = width * tpl_dev
    of_pair = jnp.where((iota((pairs, total), 0) == owner * tpl_dev + of_template) & live, 1.0, 0.0)
    earlier = jnp.sum(of_pair * dot(of_pair.astype(jnp.bfloat16), before), axis=0, keepdims=True)
    first = live & (earlier < 0.5)
    present = jnp.minimum(jnp.sum(of_pair, axis=1, keepdims=True), 1.0)
    row, col = iota((pairs, pairs), 0), iota((pairs, pairs), 1)
    lower = ((row // tpl_dev == col // tpl_dev) & (col < row)).astype(jnp.bfloat16)
    order = dot(lower, jnp.broadcast_to(present, (pairs, BLOCK)).astype(jnp.bfloat16))[:, 0:1]
    turn = jnp.sum(of_pair * order, axis=0, keepdims=True)
    over = jnp.max(jnp.where(live & (turn > HALF - 0.5), 1.0, 0.0))
    late = turn > HALF - 0.5
    home_of = (jnp.where(late, width, 0) + owner) * 4 + jnp.where(late, turn - HALF, turn).astype(jnp.int32)
    own_first = jnp.where((iota((tpl_dev, total), 0) == of_template) & first, 1.0, 0.0)
    nth = dot(own_first.astype(jnp.bfloat16), before)
    nth = jnp.sum(own_first * nth, axis=0, keepdims=True).astype(jnp.int32)
    entry = (iota((BLOCK, total), 0) == nth).astype(jnp.bfloat16)
    listed = dot((own_first * home_of.astype(jnp.float32)).astype(jnp.bfloat16), entry, NT)
    number = jnp.sum(own_first, axis=1, keepdims=True)
    list_ref[...] = jnp.where(iota((tpl_dev, BLOCK), 1) == BLOCK - 1, number, listed).astype(jnp.int32)
    at_owner = jnp.where((iota((width, total), 0) == owner) & live, 1.0, 0.0)
    rank = jnp.sum(at_owner * dot(at_owner.astype(jnp.bfloat16), before), axis=0, keepdims=True)
    dest = jnp.where(live, owner * ROWS + rank.astype(jnp.int32), -1)
    pick = (iota((width * ROWS, total), 0) == dest).astype(jnp.bfloat16)
    kind = iota((BLOCK, total), 0)
    fields = jnp.where(kind == 0, local, jnp.where(kind == 1, moves, jnp.where(kind == 2, 1.0, 0.0)))
    fields = jnp.where(kind == 3, turn, fields).astype(jnp.bfloat16)
    tail = dot(pick, fields, NT)
    tail = jnp.where(iota(tail.shape, 1) == 4, over, tail).astype(jnp.bfloat16)
    copies[4].wait()
    send = dot(pick, templates_ref[...]).astype(jnp.bfloat16)
    send_ref[:, :, : 3 * L] = send.reshape(width, ROWS, 3 * L)
    send_ref[:, :, 3 * L :] = tail.reshape(width, ROWS, BLOCK)


def prep_kernel(wave_ref, xs_hbm, xs_ref, wide_ref, sems):
    tiles = wave_ref.shape[2] // BLOCK
    wide_ref[...] = wave_ref[...].astype(jnp.float32)
    lane = iota((8, BLOCK), 1)
    own = (lane // PHASES == iota((8, BLOCK), 0)).astype(jnp.float32)
    spread = (
        (iota((3 * PHASES, 3 * BLOCK), 1) // BLOCK == iota((3 * PHASES, 3 * BLOCK), 0) // PHASES)
        & (iota((3 * PHASES, 3 * BLOCK), 1) % PHASES == iota((3 * PHASES, 3 * BLOCK), 0) % PHASES)
    ).astype(jnp.bfloat16)
    sub = iota((PHASES, WIDE), 0)

    def one_station(s):
        comps = []
        for c in range(3):
            parts = []
            group = wide_ref[c, pl.ds(pl.multiple_of(s // 8 * 8, 8), 8), :]
            line = pltpu.roll(group, (8 - s % 8) % 8, 0)[0:1, :]
            for r in range(tiles):
                row = line[:, r * BLOCK : (r + 1) * BLOCK]
                parts.append(jnp.broadcast_to(row, (8, BLOCK)) * own)
            parts.append(jnp.zeros((WIDE - 8 * tiles, BLOCK), jnp.float32))
            comps.append(jnp.concatenate(parts, axis=0).astype(jnp.bfloat16))
        grid = jnp.concatenate(comps, axis=1)
        phases = dot(spread, grid, NT)
        squares = jnp.zeros((PHASES, WIDE), jnp.float32)
        for c in range(3):
            x = phases[c * PHASES : (c + 1) * PHASES]
            squares = squares + x * x
            short = x.astype(jnp.bfloat16)
            for r in range(REACH + 1):
                at = (c * (REACH + 1) + r) * PHASES
                xs_ref[s, at : at + PHASES, :] = short if r == 0 else pltpu.roll(short, WIDE - r, 1)
        up = squares
        down = jnp.where(sub >= 1, pltpu.roll(squares, 1, 0), 0.0)
        for step in (1, 2, 4, 8):
            up = up + jnp.where(sub < PHASES - step, pltpu.roll(up, PHASES - step, 0), 0.0)
            down = down + jnp.where(sub >= step, pltpu.roll(down, step, 0), 0.0)
        whole = jnp.broadcast_to(up[0:1, :], (PHASES, WIDE))
        two = whole + pltpu.roll(whole, WIDE - 1, 1)
        four = two + pltpu.roll(two, WIDE - 2, 1)
        eight = four + pltpu.roll(four, WIDE - 4, 1)
        fifteen = (
            pltpu.roll(eight, WIDE - 1, 1)
            + pltpu.roll(four, WIDE - 9, 1)
            + pltpu.roll(two, WIDE - 13, 1)
            + pltpu.roll(whole, WIDE - 15, 1)
        )
        power = (up + fifteen + pltpu.roll(down, WIDE - REACH, 1)) / (3.0 * L)
        inv = 1.0 / (3.0 * L * jnp.sqrt(power + EPS))
        for i in range(3):
            term = inv.astype(jnp.bfloat16)
            xs_ref[s, INV + i * PHASES : INV + (i + 1) * PHASES, :] = term
            inv = inv - term.astype(jnp.float32)

    @pl.loop(0, wave_ref.shape[1] // 2)
    def _(i):
        one_station(2 * i)
        one_station(2 * i + 1)
        pair = pl.ds(2 * i, 2)
        pltpu.make_async_copy(xs_ref.at[pair, pl.ds(0, USED)], xs_hbm.at[pair, pl.ds(0, USED)], sems.at[i]).start()

    @pl.loop(0, wave_ref.shape[1] // 2)
    def _(i):
        pair = pl.ds(2 * i, 2)
        pltpu.make_async_copy(xs_ref.at[pair, pl.ds(0, USED)], xs_hbm.at[pair, pl.ds(0, USED)], sems.at[i]).wait()


def correlate_kernel(
    got_ref, xs_hbm, out_ref, more_ref, flag_ref, xs_ref, sorted_ref, order_ref, held_ref, table_ref, sem, xs_sems
):
    width = got_ref.shape[0]
    stations = xs_ref.shape[0]
    total = width * ROWS
    room = sorted_ref.shape[0]
    loads = [pltpu.make_async_copy(xs_hbm.at[s, pl.ds(0, USED)], xs_ref.at[s, pl.ds(0, USED)], xs_sems.at[s]) for s in range(stations)]
    for load in loads:
        load.start()
    for s in range(stations):
        xs_ref[s, USED:, :] = jnp.zeros((DEPTH - USED, WIDE), jnp.bfloat16)
    got = got_ref[...].reshape(total, DEPTH)
    pieces = got[:, : 3 * L]
    eye = (iota((8, BLOCK), 0) == iota((8, BLOCK), 1)).astype(jnp.bfloat16)
    fields = dot(eye, got[:, 3 * L :], NT)
    live = fields[2:3, :] > 0.5
    at_station = jnp.where(
        (iota((stations, total), 0) == fields[0:1, :].astype(jnp.int32)) & live, 1.0, 0.0
    )
    before = (iota((total, total), 0) < iota((total, total), 1)).astype(jnp.bfloat16)
    rank = dot(at_station.astype(jnp.bfloat16), before)
    chunks = jnp.floor((jnp.sum(at_station, axis=1, keepdims=True) + (CHUNK - 1)) / CHUNK)
    earlier = (iota((stations, stations), 1) < iota((stations, stations), 0)).astype(jnp.bfloat16)
    start = dot(earlier, jnp.broadcast_to(chunks, (stations, BLOCK)).astype(jnp.bfloat16))[:, 0:1]
    place = jnp.sum(at_station * (start * CHUNK + rank), axis=0, keepdims=True).astype(jnp.int32)
    place = jnp.where(live, place, -1)
    pick = (iota((room, total), 0) == place).astype(jnp.bfloat16)
    kind = iota((8, total), 0)
    late = fields[3:4, :] > HALF - 0.5
    source = iota((1, total), 1) // ROWS
    turn = jnp.where(late, fields[3:4, :] - HALF, fields[3:4, :]).astype(jnp.int32)
    target = ((jnp.where(late, width, 0) + source) * 4 + turn).astype(jnp.float32)
    rows = jnp.where(kind == 3, target, jnp.where(kind < 3, fields, 0.0)).astype(jnp.bfloat16)
    table = dot(rows, pick, NT)
    over = jnp.max(fields[4:5, :])
    kind = iota((8, room), 0)
    table = jnp.where((kind == 3) & (table[2:3, :] < 0.5), float(held_ref.shape[0] - 1), table)
    table = jnp.where(kind == 4, jnp.sum(chunks), jnp.where(kind == 5, over, table))
    order_ref[...] = table.astype(jnp.int32)
    copy = pltpu.make_async_copy(order_ref, table_ref, sem)
    copy.start()
    flag_ref[...] = jnp.full(flag_ref.shape, over, jnp.float32).astype(jnp.int32)
    sorted_ref[...] = dot(pick, pieces)
    blank = jnp.zeros((PHASES, WIDE), jnp.float32)

    @pl.loop(0, jnp.where(over > 0.5, width, width // 2))
    def _(i):
        for r in (0, 1, 2, 4, 5, 6):
            held_ref[8 * i + r] = blank

    copy.wait()

    def arrive(s, carry):
        pltpu.make_async_copy(xs_hbm.at[s, pl.ds(0, USED)], xs_ref.at[s, pl.ds(0, USED)], xs_sems.at[s]).wait()
        return carry

    sub = iota((PHASES, BLOCK), 0)
    lane = iota((PHASES, BLOCK), 1)
    own = [lane >= PHASES * c + sub for c in range(3)]

    def toeplitz(slot):
        bands = []
        for k in range(CHUNK):
            band = []
            before = None
            for c in range(3):
                turned = []
                for h in range(2):
                    at = c * L + h * BLOCK
                    row = jnp.broadcast_to(slot[k : k + 1, at : at + BLOCK], (PHASES, BLOCK))
                    turned.append(pltpu.roll(row, c * PHASES, 1, stride=1, stride_axis=0))
                rest = 0.0 if c == 0 else jnp.where(own[c - 1], 0.0, before)
                band.append(jnp.where(own[c], turned[0], rest).astype(jnp.bfloat16))
                band.append(jnp.where(own[c], turned[1], turned[0]).astype(jnp.bfloat16))
                before = turned[1]
            band.append(jnp.where(own[2], 0.0, before).astype(jnp.bfloat16))
            bands.append(jnp.concatenate(band, axis=1))
        return jnp.concatenate(bands, axis=0)

    def chunk(i):
        first = pl.multiple_of(i * CHUNK, CHUNK)
        s = table_ref[0, first]
        slot = sorted_ref[pl.ds(first, CHUNK), :]
        mean = jnp.sum(slot * slot, axis=1, keepdims=True) / (3.0 * L)
        unit = 1.0 / jnp.sqrt(mean + EPS)
        corr = dot(toeplitz(slot), xs_ref[s])
        parts = [xs_ref[s, INV + i * PHASES : INV + (i + 1) * PHASES, :].astype(jnp.float32) for i in range(3)]
        inv = (parts[2] + parts[1]) + parts[0]
        for k in range(CHUNK):
            y = corr[k * PHASES : (k + 1) * PHASES] * (inv * unit[k : k + 1, :])
            move = table_ref[1, first + k] * (BLOCK // PHASES)
            turned = [
                pltpu.roll(y[:, b * BLOCK : (b + 1) * BLOCK], (BLOCK - move) % BLOCK, 1) for b in range(3)
            ]
            stay = lane < BLOCK - move
            target = table_ref[3, first + k]
            held_ref[target, :, :BLOCK] += jnp.where(stay, turned[0], turned[1])
            held_ref[target, :, BLOCK : 2 * BLOCK] += jnp.where(stay, turned[1], turned[2])
            held_ref[target, :, 2 * BLOCK :] += turned[2]

    def three_chunks(i, ready):
        last = table_ref[0, 3 * CHUNK * i]
        for k in range(1, 3):
            last = jnp.maximum(last, table_ref[0, (3 * i + k) * CHUNK])
        lax.fori_loop(ready, last + 1, arrive, 0)
        for k in range(3):
            chunk(3 * i + k)
        return jnp.maximum(ready, last + 1)

    ready = lax.fori_loop(0, (table_ref[4, 0] + 2) // 3, three_chunks, 0)
    lax.fori_loop(ready, stations, arrive, 0)
    end = KEPT - 2 * BLOCK

    def finish(ref, o, at):
        last = jnp.zeros((PHASES, BLOCK), jnp.float32)
        for r in range(HALF):
            y = held_ref[at * 4 + r]
            a, b = y[:, :BLOCK], y[:, BLOCK : 2 * BLOCK]
            c = jnp.where(lane < end, y[:, 2 * BLOCK :], 0.0)
            top = jnp.maximum(jnp.maximum(jnp.abs(a), jnp.abs(b)), jnp.abs(c))
            top = jnp.maximum(jnp.max(top, axis=1, keepdims=True), 2.0**-110)
            power = jnp.ceil(FINE * jnp.log2(jnp.broadcast_to(top, (PHASES, BLOCK))))
            scale = FULL * jnp.exp2(power * (-1.0 / FINE))
            ref[o, 2 * r] = jnp.round(a * scale).astype(jnp.int32).astype(jnp.int16)
            ref[o, 2 * r + 1] = jnp.round(b * scale).astype(jnp.int32).astype(jnp.int16)
            c = jnp.round(c * scale)
            last = last + (c if r == 0 else pltpu.roll(c, end * r, 1))
            last = jnp.where(lane == HALF * end + r, power, last)
        ref[o, 2 * HALF] = last.astype(jnp.int32).astype(jnp.int16)

    @pl.loop(0, width // 4)
    def _(i):
        for r in range(4):
            finish(out_ref, 4 * i + r, 4 * i + r)

    @pl.when(table_ref[5, 0] > 0)
    def _():
        @pl.loop(0, width)
        def _(o):
            finish(more_ref, o, width + o)


def add_kernel(list_ref, count_ref, back_ref, stack_ref, best_ref, scale_ref, tail_ref):
    end = KEPT - 2 * BLOCK

    def wide(x):
        return x.astype(jnp.int32).astype(jnp.float32)

    @pl.loop(0, back_ref.shape[0] // 8)
    def _(i):
        for part in range(8):
            o = 8 * i + part
            last = wide(back_ref[o, 2 * HALF])
            scales = jnp.exp2(last * (1.0 / FINE)) * (1.0 / FULL)
            for r in range(HALF):
                at = HALF * end + r
                scale_ref[o * 4 + r] = jnp.broadcast_to(scales[:, at : at + 1], (PHASES, BLOCK))
                tail_ref[o * 4 + r] = last if r == 0 else pltpu.roll(last, BLOCK - end * r, 1)

    def one_template(t, best):
        count = count_ref[t]
        number = list_ref[t, BLOCK - 1]

        def four_traces(g, total):
            for i in range(4):
                entry = list_ref[t, 4 * g + i]
                o = entry // 4
                r = entry % 4
                scale = jnp.where(4 * g + i < number, scale_ref[entry], 0.0)
                parts = (wide(back_ref[o, 2 * r]), wide(back_ref[o, 2 * r + 1]), tail_ref[entry])
                total = tuple(a + p * scale for a, p in zip(total, parts))
            return total

        zero = jnp.zeros((PHASES, BLOCK), jnp.float32)
        total = lax.fori_loop(0, (number + 3) // 4, four_traces, (zero, zero, zero))
        factor = jnp.sqrt(3.0 * L / jnp.full((1, 1), count, jnp.int32).astype(jnp.float32))
        whole = jnp.concatenate(total, axis=1) * factor
        stack_ref[t] = whole[:, :KEPT]
        return jnp.maximum(best, whole)

    start = jnp.full((PHASES, WIDE), -jnp.inf, jnp.float32)
    best = lax.fori_loop(0, stack_ref.shape[0], one_template, start)
    best_ref[...] = best[:, :KEPT]


VMEM = pl.BlockSpec(memory_space=pltpu.VMEM)
ANY = pl.BlockSpec(memory_space=pl.ANY)
SMEM = pl.BlockSpec(memory_space=pltpu.SMEM)


def params(mib):
    return pltpu.CompilerParams(vmem_limit_bytes=mib * 2**20)


def prep_call(waveforms):
    stations, _, samples = waveforms.shape
    return pl.pallas_call(
        prep_kernel,
        out_shape=jax.ShapeDtypeStruct((2 * stations + 4, DEPTH, WIDE), jnp.bfloat16),
        in_specs=[VMEM],
        out_specs=ANY,
        scratch_shapes=[
            pltpu.VMEM((stations, DEPTH, WIDE), jnp.bfloat16),
            pltpu.VMEM((3, stations, samples), jnp.float32),
            pltpu.SemaphoreType.DMA((stations // 2,)),
        ],
        compiler_params=params(40),
        cost_estimate=pl.CostEstimate(flops=2 * 10**9, bytes_accessed=12 * 2**20, transcendentals=0),
    )(waveforms.transpose(1, 0, 2))


def correlate_call(got, xs, stations):
    width = got.shape[0]
    room = 8 * (width * CAP // CHUNK + stations)
    return pl.pallas_call(
        correlate_kernel,
        out_shape=(
            jax.ShapeDtypeStruct((width, BLOCKS, PHASES, BLOCK), jnp.int16),
            jax.ShapeDtypeStruct((width, BLOCKS, PHASES, BLOCK), jnp.int16),
            jax.ShapeDtypeStruct((1, BLOCK), jnp.int32),
        ),
        in_specs=[VMEM, ANY],
        out_specs=(VMEM, VMEM, VMEM),
        scratch_shapes=[
            pltpu.VMEM((stations, DEPTH, WIDE), jnp.bfloat16),
            pltpu.VMEM((room, 3 * L), jnp.float32),
            pltpu.VMEM((8, room), jnp.int32),
            pltpu.VMEM((8 * width + 8, PHASES, WIDE), jnp.float32),
            pltpu.SMEM((8, room), jnp.int32),
            pltpu.SemaphoreType.DMA,
            pltpu.SemaphoreType.DMA((stations,)),
        ],
        compiler_params=params(40),
    )(got, xs)


def add_call(listed, counts, back):
    tpl_dev = counts.shape[0]
    return pl.pallas_call(
        add_kernel,
        out_shape=(
            jax.ShapeDtypeStruct((tpl_dev, PHASES, KEPT), jnp.float32),
            jax.ShapeDtypeStruct((PHASES, KEPT), jnp.float32),
        ),
        in_specs=[SMEM, SMEM, VMEM],
        out_specs=(VMEM, VMEM),
        scratch_shapes=[
            pltpu.VMEM((back.shape[0] * 4, PHASES, BLOCK), jnp.float32),
            pltpu.VMEM((back.shape[0] * 4, PHASES, BLOCK), jnp.float32),
        ],
        compiler_params=params(40),
    )(listed, counts, back)


def body(waveforms, station_home, templates, template_stations, station_counts, moveouts):
    stations, _, samples = waveforms.shape
    tpl_dev = templates.shape[0]
    width = lax.axis_size("sta")
    parts = station_home.shape[0] // BLOCK
    send, listed = pl.pallas_call(
        pack_kernel,
        out_shape=(
            jax.ShapeDtypeStruct((width, ROWS, DEPTH), jnp.bfloat16),
            jax.ShapeDtypeStruct((tpl_dev, BLOCK), jnp.int32),
        ),
        in_specs=[ANY] * 5,
        out_specs=(VMEM, VMEM),
        scratch_shapes=[
            pltpu.VMEM((tpl_dev, SLOTS), jnp.int32),
            pltpu.VMEM((tpl_dev, SLOTS), jnp.int32),
            pltpu.SMEM((tpl_dev,), jnp.int32),
            pltpu.VMEM((parts, BLOCK), jnp.int32),
            pltpu.VMEM((tpl_dev * SLOTS, 3 * L), jnp.bfloat16),
            pltpu.SemaphoreType.DMA((5,)),
        ],
        compiler_params=params(60),
    )(
        template_stations,
        moveouts,
        station_counts,
        station_home.reshape(parts, BLOCK),
        templates.transpose(1, 0, 2).reshape(tpl_dev * SLOTS, 3 * L),
    )
    got = lax.all_to_all(send, "sta", split_axis=0, concat_axis=0, tiled=True)
    xs = prep_call(waveforms)
    traces, more, flag = correlate_call(got, xs, stations)

    def home(x):
        return lax.all_to_all(x, "sta", split_axis=0, concat_axis=0, tiled=True)

    def one_exchange(traces, more):
        return add_call(listed, station_counts, home(traces))

    def two_exchanges(traces, more):
        return add_call(listed, station_counts, jnp.concatenate([home(traces), home(more)]))

    stack, best = lax.cond(flag[0, 0] > 0, two_exchanges, one_exchange, traces, more)
    best = best.T.reshape(-1, BLOCK)
    for n, (axis, steps) in enumerate(ROUNDS):
        size = lax.axis_size(axis)
        others = [lax.ppermute(best, axis, [(i, i ^ step) for i in range(size)]) for step in steps]
        for other in others:
            best = jnp.maximum(best, other)
        if n == 0:
            best, stack = lax.optimization_barrier((best, stack))
            stack = stack.transpose(0, 2, 1).reshape(tpl_dev, PHASES * KEPT)
        if n == 1:
            best, stack = lax.optimization_barrier((best, stack))
    return (stack, best.reshape(PHASES * KEPT))


ROUNDS = (("sta", (1,)), ("tpl", (6,)), ("tpl", (1, 2, 3)), ("sta", (2, 6, 4)), ("sta", (8, 24, 16)))


def solution(mesh):
    in_specs = (
        P("sta", None, None),
        P(),
        P(("sta", "tpl"), None, None),
        P(("sta", "tpl"), None),
        P(("sta", "tpl")),
        P(("sta", "tpl"), None),
    )
    out_specs = (P(("sta", "tpl"), None), P())
    return jax.shard_map(body, mesh=mesh, in_specs=in_specs, out_specs=out_specs, check_vma=False)
```
